32 devices in a mesh: dp: 4 (over y, x), seq: 2 (over core), tensor: 4 (over z).
Axes of the slice: x: 2, y: 2, z: 4, core: 2. Of those that a mesh axis runs over, the one named last changes fastest.
Arguments:
- tokens: bfloat16 [4, 2048, 1024], P('dp', 'seq'), may hold values from -6 to 6
- cotangent: bfloat16 [4, 2048, 1024], P('dp', 'seq'), may hold values from -6 to 6
- segments: int32 [4, 2048], P('dp', 'seq'), may hold values from 0 to 3, as said below
- positions: int32 [4, 2048], P('dp', 'seq'), may hold values from 0 to 4095, as said below
- attn_gain: bfloat16 [2, 1024], replicated, may hold values from 0.25 to 1.75
- w_query: bfloat16 [2, 1024, 2048], P(None, None, 'tensor'), may hold values from -0.1875 to 0.1875
- key_projection: bfloat16 [2, 1024, 1024], P(None, None, 'tensor'), may hold values from -0.1875 to 0.1875
- value_projection: bfloat16 [2, 1024, 1024], P(None, None, 'tensor'), may hold values from -0.1875 to 0.1875
- query_gain: bfloat16 [2, 128], replicated, may hold values from 0.25 to 1.75
- key_gain: bfloat16 [2, 128], replicated, may hold values from 0.25 to 1.75
- w_output: bfloat16 [2, 2048, 1024], P(None, 'tensor'), may hold values from -0.5 to 0.5
- mlp_gain: bfloat16 [2, 1024], replicated, may hold values from 0.25 to 1.75
- w_gate: bfloat16 [2, 1024, 3072], P(None, None, 'tensor'), may hold values from -0.1875 to 0.1875
- w_up: bfloat16 [2, 1024, 3072], P(None, None, 'tensor'), may hold values from -0.1875 to 0.1875
- w_down: bfloat16 [2, 3072, 1024], P(None, 'tensor'), may hold values from -0.109375 to 0.109375
Outputs:
- output: bfloat16 [4, 2048, 1024], P('dp', 'seq')
- input_grad: float32 [4, 2048, 1024], P('dp', 'seq')
- grad_attn_gain: float32 [2, 1024], replicated
- grad_query: float32 [2, 1024, 2048], P(None, ('dp', 'seq'), 'tensor')
- grad_key: float32 [2, 1024, 1024], P(None, ('dp', 'seq'), 'tensor')
- grad_value: float32 [2, 1024, 1024], P(None, ('dp', 'seq'), 'tensor')
- grad_query_gain: float32 [2, 128], replicated
- grad_key_gain: float32 [2, 128], replicated
- grad_output: float32 [2, 2048, 1024], P(None, 'tensor', ('dp', 'seq'))
- grad_mlp_gain: float32 [2, 1024], replicated
- grad_gate: float32 [2, 1024, 3072], P(None, ('dp', 'seq'), 'tensor')
- grad_up: float32 [2, 1024, 3072], P(None, ('dp', 'seq'), 'tensor')
- grad_down: float32 [2, 3072, 1024], P(None, 'tensor', ('dp', 'seq'))
The draws below stay inside these ranges and needn't reach their ends.
Inputs may be any that keep to these rules, and one draw needn't show every extreme that they name: `segments`: along each sequence the numbers start at 0 and never fall; each sequence holds 4 documents. Within a document the positions rise by one from token to token.
All inputs are finite; a program needn't handle non-finite values.
Results may differ from the reference program's by a relative error of at most 0.033.
Values may be sent and summed in bfloat16 or wider, within the bound.
A program may use at most 320 MiB of HBM per device.

```python
import jax
import jax.numpy as jnp
from jax import lax

MODEL_WIDTH = 1024
QUERY_HEADS = 16
KEY_VALUE_HEADS = 8
HEAD_SIZE = 128
FF = 3072
LAYER_COUNT = 2
WINDOW = 1024
SEQ_LEN = 2048
DOCS = 4
STRETCH = 1024
SEQS_DEV = 1
SEQS = 4


def document_layout(key):
    pick_key, long_key, short_key = jax.random.split(key, 3)
    query_groups = SEQS // SEQS_DEV
    picked = jax.random.randint(pick_key, (query_groups,), 0, SEQS_DEV)
    member = jnp.arange(SEQS) % SEQS_DEV
    chosen = member == jnp.repeat(picked, SEQS_DEV)

    def long_cuts(one_key):
        return jax.random.permutation(one_key, SEQ_LEN - 1)[:DOCS - 1] + 1

    def short_cuts(one_key):
        return jax.random.permutation(one_key, STRETCH - 1)[:DOCS - 1] + 1
    spread_cuts = jax.vmap(long_cuts)(jax.random.split(long_key, SEQS))
    early_cuts = jax.vmap(short_cuts)(jax.random.split(short_key, SEQS))
    cuts = jnp.where(chosen[:, None], early_cuts, spread_cuts)
    places = jnp.arange(SEQ_LEN)
    segment = jnp.sum(places[None, :, None] >= cuts[:, None, :], axis=2).astype(jnp.int32)
    return (segment, chosen)


def draw_segments(key, part):
    segment, chosen = document_layout(key)
    return segment


def draw_positions(key, part):
    segment, chosen = document_layout(key)
    key = jax.random.fold_in(key, 7)
    offsets = jax.random.randint(key, (SEQS, DOCS), 0, SEQ_LEN + 1)
    docs = jnp.arange(DOCS)
    starts = jnp.sum(segment[:, None, :] < docs[None, :, None], axis=2)
    last_offset = SEQ_LEN + starts[:, DOCS - 1]
    offsets = jnp.where(docs[None, :] == 0, 0, offsets)
    offsets = jnp.where(chosen[:, None] & (docs[None, :] == DOCS - 1), last_offset[:, None], offsets)
    matches = segment[:, :, None] == docs[None, None, :]
    moved = jnp.sum(jnp.where(matches, (offsets - starts)[:, None, :], 0), axis=2)
    places = jnp.arange(SEQ_LEN)
    return (places[None, :] + moved).astype(jnp.int32)


def raised(values, rng, source, target, shards_of, factor):
    def block_of(axis_at):
        return (jnp.arange(values.shape[axis_at]) // (values.shape[axis_at] // shards_of)).reshape((-1,) + (1,) * (values.ndim - 1 - axis_at))

    one_side = jax.random.permutation(rng, shards_of)[block_of(target)]
    second = (block_of(target) + shards_of // 2) % shards_of
    return jnp.where((block_of(source) == one_side) | (block_of(source) == second), factor * values, values)


def steps_of(rng, extent, cuts, low, largest):
    loudness = 1.0
    for position, blocks in cuts:
        steps = jax.random.uniform(jax.random.fold_in(jax.random.fold_in(rng, 6), position), (blocks,), jnp.float32, low / len(cuts), largest / len(cuts))
        loudness = loudness * jnp.repeat(jnp.exp(steps), extent[position] // blocks).reshape((-1,) + (1,) * (len(extent) - 1 - position))
    return loudness


def bell_draw(stream_key, dims, scale, most, cuts=(), held_as=jnp.bfloat16):
    drawn = jax.random.normal(stream_key, dims, jnp.float32) * scale
    if len(cuts) > 0:
        drawn = steps_of(stream_key, dims, cuts, -0.22, 0.18) * drawn
    return jnp.clip(drawn, min=-most, max=most).astype(held_as)


def gaussian_with(rng, shape, scale, most, cuts, heavy, kind=jnp.bfloat16):
    entries = scale * jax.random.normal(rng, shape, jnp.float32)
    if cuts:
        entries = entries * steps_of(rng, shape, cuts, -0.22, 0.18)
    return jnp.clip(raised(entries, jax.random.fold_in(rng, 3), *heavy), -most, most).astype(kind)


def setup_inputs(seed: int = 0) -> dict:
    arg_keys = jax.random.split(jax.random.key(seed), 16)
    tokens = gaussian_with(arg_keys[0], (SEQS, SEQ_LEN, MODEL_WIDTH), 1.0, 6.0, ((0, 4), (1, 2)), (1, 2, 2, 2.0))
    cotangent = bell_draw(arg_keys[1], (SEQS, SEQ_LEN, MODEL_WIDTH), 1.0, 6.0, ((0, 4), (1, 2)))
    segments = draw_segments(jax.random.fold_in(arg_keys[15], 71), 0)
    positions = draw_positions(jax.random.fold_in(arg_keys[15], 71), 0)
    attn_gain = jnp.clip(1.0 + 0.15 * jax.random.normal(arg_keys[4], (LAYER_COUNT, MODEL_WIDTH), jnp.float32), 0.25, 1.75).astype(jnp.bfloat16)
    w_query = bell_draw(arg_keys[5], (LAYER_COUNT, MODEL_WIDTH, QUERY_HEADS * HEAD_SIZE), MODEL_WIDTH ** -0.5, 0.1875, ((2, 4),))
    key_projection = bell_draw(arg_keys[6], (LAYER_COUNT, MODEL_WIDTH, KEY_VALUE_HEADS * HEAD_SIZE), MODEL_WIDTH ** -0.5, 0.1875, ((2, 4),))
    value_projection = bell_draw(arg_keys[7], (LAYER_COUNT, MODEL_WIDTH, KEY_VALUE_HEADS * HEAD_SIZE), MODEL_WIDTH ** -0.5, 0.1875, ((2, 4),))
    query_gain = jnp.clip(1.0 + 0.15 * jax.random.normal(arg_keys[8], (LAYER_COUNT, HEAD_SIZE), jnp.float32), 0.25, 1.75).astype(jnp.bfloat16)
    key_gain = jnp.clip(1.0 + 0.15 * jax.random.normal(arg_keys[9], (LAYER_COUNT, HEAD_SIZE), jnp.float32), 0.25, 1.75).astype(jnp.bfloat16)
    w_output = bell_draw(arg_keys[10], (LAYER_COUNT, QUERY_HEADS * HEAD_SIZE, MODEL_WIDTH), (QUERY_HEADS * HEAD_SIZE // 16) ** -0.5, 0.5, ((1, 4),))
    mlp_gain = jnp.clip(1.0 + 0.15 * jax.random.normal(arg_keys[11], (LAYER_COUNT, MODEL_WIDTH), jnp.float32), 0.25, 1.75).astype(jnp.bfloat16)
    w_gate = bell_draw(arg_keys[12], (LAYER_COUNT, MODEL_WIDTH, FF), MODEL_WIDTH ** -0.5, 0.1875, ((2, 4),))
    w_up = bell_draw(arg_keys[13], (LAYER_COUNT, MODEL_WIDTH, FF), MODEL_WIDTH ** -0.5, 0.1875, ((2, 4),))
    w_down = bell_draw(arg_keys[14], (LAYER_COUNT, FF, MODEL_WIDTH), FF ** -0.5, 0.109375, ((1, 4),))
    return {"tokens": tokens, "cotangent": cotangent, "segments": segments, "positions": positions, "attn_gain": attn_gain, "w_query": w_query, "key_projection": key_projection, "value_projection": value_projection, "query_gain": query_gain, "key_gain": key_gain, "w_output": w_output, "mlp_gain": mlp_gain, "w_gate": w_gate, "w_up": w_up, "w_down": w_down}


EPS = 1e-06
THETA = 1000000.0
NEG_FILL = -1e+30
HIGHEST = lax.Precision.HIGHEST

@jax.custom_vjp
def reduced_precision(v):
    return lax.optimization_barrier(v.astype(jnp.bfloat16)).astype(jnp.float32)

@jax.custom_vjp
def reduced_precision_back(v):
    return v

def low_keep(v):
    return (reduced_precision(v), None)

def low_pass(kept, grad):
    return (grad,)

def back_keep(v):
    return (v, None)

def back_low(kept, grad):
    return (reduced_precision(grad),)
reduced_precision.defvjp(low_keep, low_pass)
reduced_precision_back.defvjp(back_keep, back_low)

def matrix_product(left, right):
    return jnp.dot(left, right, precision=HIGHEST, preferred_element_type=jnp.float32)

def root_mean_norm(value_block, gain):
    return value_block * lax.rsqrt(lax.optimization_barrier(jnp.mean(value_block * value_block, -1, keepdims=True)) + EPS) * gain

def rope_tables(places):
    halves = HEAD_SIZE // 2
    frequency = THETA ** (-(jnp.arange(halves, dtype=jnp.float32) * 2.0) / HEAD_SIZE)
    angle = places.astype(jnp.float32)[..., None] * frequency
    cosine = jnp.cos(angle)
    sine_part = jnp.sin(angle)
    return (jnp.concatenate([cosine, cosine], -1)[..., None, :], jnp.concatenate([sine_part, sine_part], -1)[..., None, :])

def apply_rotary(value_block, rotary_tables):
    cosine, sine_part = rotary_tables
    halves = value_block.shape[-1] // 2
    turned = jnp.concatenate([-value_block[..., halves:], value_block[..., :halves]], -1)
    return value_block * cosine + turned * sine_part

def attention(query_block, keys, value_block, doc_row):
    token_length = query_block.shape[0]
    block = min(512, token_length)
    scale = HEAD_SIZE ** (-0.5)
    key_index = jnp.arange(token_length, dtype=jnp.int32)

    def one_block(start):
        query_rows = lax.dynamic_slice_in_dim(query_block, start, block, 0)
        query_index = start + jnp.arange(block, dtype=jnp.int32)
        query_docs = lax.dynamic_slice_in_dim(doc_row, start, block, 0)
        scores = reduced_precision_back(jnp.einsum('qhgd,khd->hgqk', query_rows, keys, precision=HIGHEST) * scale)
        distance = query_index[:, None] - key_index[None, :]
        visible = (distance >= 0) & (distance < WINDOW) & (query_docs[:, None] == doc_row[None, :])
        scores = jnp.where(visible[None, None], scores, NEG_FILL)
        probs = reduced_precision(jax.nn.softmax(scores, axis=-1))
        return jnp.einsum('hgqk,khd->qhgd', probs, value_block, precision=HIGHEST)
    starts = jnp.arange(token_length // block, dtype=jnp.int32) * block
    blocks = lax.map(jax.checkpoint(one_block), starts)
    return blocks.reshape(token_length, -1)

def layer(hidden, weights, rotary_tables, doc_row):
    gain_a, w_q, key_weight, value_weight, query_norm_scale, gain_k, w_o, gain_m, w_g, w_u, w_d = weights
    token_length = hidden.shape[0]
    query_groups = QUERY_HEADS // KEY_VALUE_HEADS
    attention_input = reduced_precision(root_mean_norm(hidden, gain_a))
    query_unnormed = reduced_precision_back(matrix_product(attention_input, w_q)).reshape(token_length, QUERY_HEADS, HEAD_SIZE)
    key_unnormed = reduced_precision_back(matrix_product(attention_input, key_weight)).reshape(token_length, KEY_VALUE_HEADS, HEAD_SIZE)
    value_block = reduced_precision(reduced_precision_back(matrix_product(attention_input, value_weight))).reshape(token_length, KEY_VALUE_HEADS, HEAD_SIZE)
    query_block = reduced_precision(apply_rotary(root_mean_norm(query_unnormed, query_norm_scale), rotary_tables)).reshape(token_length, KEY_VALUE_HEADS, query_groups, HEAD_SIZE)
    keys = reduced_precision(apply_rotary(root_mean_norm(key_unnormed, gain_k), rotary_tables))
    context = reduced_precision(reduced_precision_back(attention(query_block, keys, value_block, doc_row)))
    hidden = hidden + reduced_precision_back(matrix_product(context, w_o))
    mlp_in = reduced_precision(root_mean_norm(hidden, gain_m))
    gate = reduced_precision_back(matrix_product(mlp_in, w_g))
    up_branch = reduced_precision_back(matrix_product(mlp_in, w_u))
    act = reduced_precision(jax.nn.silu(gate) * up_branch)
    return hidden + reduced_precision_back(matrix_product(act, w_d))

def reference(tokens, cotangent, segments, positions, attn_gain, w_query, key_projection, value_projection, query_gain, key_gain, w_output, mlp_gain, w_gate, w_up, w_down):
    params = tuple((p.astype(jnp.float32) for p in (attn_gain, w_query, key_projection, value_projection, query_gain, key_gain, w_output, mlp_gain, w_gate, w_up, w_down)))

    def one_sequence(totals, items):
        row_tokens, row_cot, row_docs, row_places = items
        rotary_tables = rope_tables(row_places)

        def apply(hidden, weights):
            for layer_index in range(LAYER_COUNT):
                hidden = layer(hidden, tuple((w[layer_index] for w in weights)), rotary_tables, row_docs)
            return hidden
        result, pullback = jax.vjp(apply, row_tokens.astype(jnp.float32), params)
        grad_in, grad_weights = pullback(row_cot.astype(jnp.float32))
        totals = tuple((a + b for a, b in zip(totals, grad_weights)))
        return (totals, (result.astype(jnp.bfloat16), grad_in))
    zeros = tuple((jnp.zeros_like(p) for p in params))
    totals, (output, input_grad) = lax.scan(one_sequence, zeros, (tokens, cotangent, segments, positions))
    return (output, input_grad, totals[0], totals[1], totals[2], totals[3], totals[4], totals[5], totals[6], totals[7], totals[8], totals[9], totals[10])
```

```python
import functools

import jax
import jax.numpy as jnp
from jax import lax
from jax.experimental import pallas as pl
from jax.experimental.pallas import tpu as pltpu
from jax.sharding import PartitionSpec as P

HEAD_SIZE = 128
LAYER_COUNT = 2
WINDOW = 1024
LOG2E = 1.4426950408889634
SCALE = HEAD_SIZE ** (-0.5)
MESH = pl.DeviceIdType.MESH

NT = (((1,), (1,)), ((), ()))
NN = (((1,), (0,)), ((), ()))
TN = (((0,), (0,)), ((), ()))


def dot(a, b, dims=NN):
    return lax.dot_general(a, b, dims, preferred_element_type=jnp.float32)


def attn_fwd_kernel(qb, kb, offset, first_ref, low_ref, q_ref, k_ref, v_ref, o_ref, of_ref, lse_ref):
    step = pl.program_id(1)
    heads = q_ref.shape[1] // HEAD_SIZE
    q_start = step * qb + offset
    queries = [q_ref[:, h * HEAD_SIZE:(h + 1) * HEAD_SIZE] for h in range(heads)]
    q_index = q_start + lax.broadcasted_iota(jnp.int32, (qb, 1), 0)
    low = low_ref[...]

    def block(kk, carry):
        start = pl.multiple_of(kk * kb, kb)
        keys = k_ref[pl.ds(start, kb), :]
        values = v_ref[pl.ds(start, kb), :]
        key_index = start + lax.broadcasted_iota(jnp.int32, (qb, kb), 1)
        mask = (key_index >= low) & (key_index <= q_index)
        out = []
        for h in range(heads):
            acc, total = carry[h]
            s = dot(queries[h], keys, NT) * (SCALE * LOG2E)
            p = jnp.where(mask, jnp.exp2(s), 0.0)
            part = p[:, :128]
            for c in range(1, kb // 128):
                part = part + p[:, c * 128:(c + 1) * 128]
            out.append((acc + dot(p.astype(jnp.bfloat16), values), total + part))
        return tuple(out)

    zero = jnp.zeros((qb, HEAD_SIZE), jnp.float32)
    first = first_ref[step] // kb
    last = (q_start + qb - 1) // kb + 1
    result = lax.fori_loop(first, last, block, tuple((zero, zero) for _ in range(heads)))
    for h in range(heads):
        acc, total = result[h]
        total = jnp.sum(total, 1, keepdims=True)
        o = acc / total
        of_ref[:, h * HEAD_SIZE:(h + 1) * HEAD_SIZE] = o
        o_ref[:, h * HEAD_SIZE:(h + 1) * HEAD_SIZE] = o.astype(jnp.bfloat16)
        lse_ref[:, h:h + 1] = jnp.log2(total)


def attn_fwd(q, k, v, first, low, offset, qb=256, kb=256):
    rows, span = q.shape[0], k.shape[0]
    kv_heads = k.shape[1] // HEAD_SIZE
    group = q.shape[1] // k.shape[1]
    qb = min(qb, rows)
    width = group * HEAD_SIZE
    return pl.pallas_call(
        functools.partial(attn_fwd_kernel, qb, kb, offset),
        grid_spec=pltpu.PrefetchScalarGridSpec(
            num_scalar_prefetch=1,
            grid=(kv_heads, rows // qb),
            in_specs=[
                pl.BlockSpec((qb, 1), lambda g, i, f: (i, 0)),
                pl.BlockSpec((qb, width), lambda g, i, f: (i, g)),
                pl.BlockSpec((span, HEAD_SIZE), lambda g, i, f: (0, g)),
                pl.BlockSpec((span, HEAD_SIZE), lambda g, i, f: (0, g)),
            ],
            out_specs=[
                pl.BlockSpec((qb, width), lambda g, i, f: (i, g)),
                pl.BlockSpec((qb, width), lambda g, i, f: (i, g)),
                pl.BlockSpec((None, qb, group), lambda g, i, f: (g, i, 0)),
            ],
        ),
        out_shape=[
            jax.ShapeDtypeStruct(q.shape, jnp.bfloat16),
            jax.ShapeDtypeStruct(q.shape, jnp.float32),
            jax.ShapeDtypeStruct((kv_heads, rows, group), jnp.float32),
        ],
        name="attn_fwd",
        compiler_params=pltpu.CompilerParams(vmem_limit_bytes=32 << 20),
    )(first, low, q, k, v)


def attn_bwd_kernel(qb, kb, offset, first_ref, low_ref, lse_ref, delta_ref, q_ref, do_ref, k_ref, v_ref,
                    dq_ref, dk_ref, dv_ref):
    step = pl.program_id(1)
    heads = q_ref.shape[1] // HEAD_SIZE
    q_start = step * qb + offset

    @pl.when(step == 0)
    def _():
        dk_ref[...] = jnp.zeros_like(dk_ref)
        dv_ref[...] = jnp.zeros_like(dv_ref)

    def stack(ref):
        return jnp.concatenate([ref[:, h * HEAD_SIZE:(h + 1) * HEAD_SIZE] for h in range(heads)], 0)

    queries = stack(q_ref)
    d_out = stack(do_ref)
    q_index = q_start + lax.broadcasted_iota(jnp.int32, (1, qb), 1)
    low = low_ref[...]
    lse = jnp.concatenate([lse_ref[h:h + 1, :] for h in range(heads)], 1)
    delta = jnp.concatenate([delta_ref[h:h + 1, :] for h in range(heads)], 1)

    def block(kk, dq):
        start = pl.multiple_of(kk * kb, kb)
        keys = k_ref[pl.ds(start, kb), :]
        values = v_ref[pl.ds(start, kb), :]
        key_index = start + lax.broadcasted_iota(jnp.int32, (kb, qb), 0)
        mask = (key_index >= low) & (key_index <= q_index)
        mask = jnp.concatenate([mask] * heads, 1)
        s = dot(keys, queries, NT) * (SCALE * LOG2E) - lse
        p = jnp.where(mask, jnp.exp2(s), 0.0)
        dp = dot(values, d_out, NT)
        ds = (p * (dp - delta)).astype(jnp.bfloat16)
        dv_ref[pl.ds(start, kb), :] += dot(p.astype(jnp.bfloat16), d_out)
        dk_ref[pl.ds(start, kb), :] += dot(ds, queries)
        return dq + dot(ds, keys, TN)

    first = first_ref[step] // kb
    last = (q_start + qb - 1) // kb + 1
    dq = lax.fori_loop(first, last, block, jnp.zeros((heads * qb, HEAD_SIZE), jnp.float32))
    for h in range(heads):
        dq_ref[:, h * HEAD_SIZE:(h + 1) * HEAD_SIZE] = dq[h * qb:(h + 1) * qb] * SCALE

    @pl.when(step == pl.num_programs(1) - 1)
    def _():
        dk_ref[...] = dk_ref[...] * SCALE


def attn_bwd(q, d_out, k, v, first, low_row, lse, delta, offset, qb=256, kb=256):
    rows, span = q.shape[0], k.shape[0]
    kv_heads = k.shape[1] // HEAD_SIZE
    group = q.shape[1] // k.shape[1]
    qb = min(qb, rows)
    width = group * HEAD_SIZE
    return pl.pallas_call(
        functools.partial(attn_bwd_kernel, qb, kb, offset),
        grid_spec=pltpu.PrefetchScalarGridSpec(
            num_scalar_prefetch=1,
            grid=(kv_heads, rows // qb),
            in_specs=[
                pl.BlockSpec((1, qb), lambda g, i, f: (0, i)),
                pl.BlockSpec((None, group, qb), lambda g, i, f: (g, 0, i)),
                pl.BlockSpec((None, group, qb), lambda g, i, f: (g, 0, i)),
                pl.BlockSpec((qb, width), lambda g, i, f: (i, g)),
                pl.BlockSpec((qb, width), lambda g, i, f: (i, g)),
                pl.BlockSpec((span, HEAD_SIZE), lambda g, i, f: (0, g)),
                pl.BlockSpec((span, HEAD_SIZE), lambda g, i, f: (0, g)),
            ],
            out_specs=[
                pl.BlockSpec((qb, width), lambda g, i, f: (i, g)),
                pl.BlockSpec((span, HEAD_SIZE), lambda g, i, f: (0, g)),
                pl.BlockSpec((span, HEAD_SIZE), lambda g, i, f: (0, g)),
            ],
        ),
        out_shape=[
            jax.ShapeDtypeStruct(q.shape, jnp.float32),
            jax.ShapeDtypeStruct(k.shape, jnp.float32),
            jax.ShapeDtypeStruct(k.shape, jnp.float32),
        ],
        name="attn_bwd",
        compiler_params=pltpu.CompilerParams(vmem_limit_bytes=32 << 20),
    )(first, low_row, lse, delta, q, d_out, k, v)


def attention_forward(queries, keys, values, low, offset):
    seqs_here, stretch = low.shape
    outs = []
    for s in range(seqs_here):
        here = queries[s * stretch : (s + 1) * stretch]
        block = min(512, stretch)
        outs.append(
            attn_fwd(here, keys[s], values[s], low[s, ::block], low[s][:, None], offset, block, min(512, stretch))
        )
    low_out, full, lse = (jnp.concatenate(parts, 0) for parts in zip(*outs))
    return low_out, full, lse.reshape((seqs_here,) + outs[0][2].shape)


def attention_backward(queries, d_context, context, lse, keys, values, low, offset):
    seqs_here, stretch = low.shape
    product = d_context.astype(jnp.float32) * context
    kv_heads, group = lse.shape[1], lse.shape[3]
    delta = jnp.sum(product.reshape(seqs_here, stretch, kv_heads, group, HEAD_SIZE), -1)
    outs = []
    for s in range(seqs_here):
        here = slice(s * stretch, (s + 1) * stretch)
        block = min(512, stretch)
        outs.append(
            attn_bwd(
                queries[here], d_context[here], keys[s], values[s], low[s, ::block], low[s][None],
                lse[s].transpose(0, 2, 1), delta[s].transpose(1, 2, 0), offset, block, min(512, stretch),
            )
        )
    d_queries, d_keys, d_values = zip(*outs)
    return jnp.concatenate(d_queries, 0), jnp.stack(d_keys), jnp.stack(d_values)


def line_sum_kernel(chunks, x_ref, o_ref, p_ref, land_ref, send_sem, land_sem, out_sem, total_sem):
    n = lax.axis_size("tensor")
    half = n // 2
    z = lax.axis_index("tensor")
    left = z < half
    middle = (z == half - 1) | (z == half)
    has_outer = (z > 0) & (z < n - 1)
    inner = jnp.where(left, z + 1, z - 1)
    outer = jnp.clip(jnp.where(left, z - 1, z + 1), 0, n - 1)
    rows = x_ref.shape[0] // chunks
    barrier = pltpu.get_barrier_semaphore()
    pl.semaphore_signal(barrier, inc=1, device_id={"tensor": inner}, device_id_type=MESH)

    @pl.when(has_outer)
    def _():
        pl.semaphore_signal(barrier, inc=1, device_id={"tensor": outer}, device_id_type=MESH)

    pl.semaphore_wait(barrier, jnp.where(has_outer, 2, 1))
    slot = jnp.where(middle, 1, 0)

    def part(ref, c):
        return ref.at[pl.ds(pl.multiple_of(c * rows, rows), rows)]

    def inward(source, c):
        return pltpu.make_async_remote_copy(
            part(source, c), part(land_ref.at[slot], c), send_sem.at[c], land_sem.at[slot, c],
            device_id={"tensor": inner}, device_id_type=MESH)

    def landed(which, c):
        return pltpu.make_async_remote_copy(
            part(x_ref, c), part(land_ref.at[which], c), send_sem.at[c], land_sem.at[which, c],
            device_id={"tensor": inner}, device_id_type=MESH)

    def outward(c):
        return pltpu.make_async_remote_copy(
            part(o_ref, c), part(o_ref, c), out_sem.at[c], total_sem.at[c],
            device_id={"tensor": outer}, device_id_type=MESH)

    @pl.when(jnp.logical_not(has_outer))
    def _():
        @pl.loop(0, chunks)
        def _(c):
            inward(x_ref, c).start()

    @pl.loop(0, chunks + 1)
    def _(step):
        @pl.when((step < chunks) & has_outer)
        def _():
            c = step
            landed(0, c).wait_recv()
            p_ref[pl.ds(pl.multiple_of(c * rows, rows), rows), :] = (
                part(x_ref, c)[...].astype(jnp.float32) + part(land_ref.at[0], c)[...].astype(jnp.float32)
            ).astype(jnp.bfloat16)
            inward(p_ref, c).start()

        @pl.when((step > 0) & middle)
        def _():
            c = step - 1
            landed(1, c).wait_recv()

            def finish(own):
                o_ref[pl.ds(pl.multiple_of(c * rows, rows), rows), :] = (
                    part(own, c)[...].astype(jnp.float32) + part(land_ref.at[1], c)[...].astype(jnp.float32)
                ).astype(jnp.bfloat16)

            @pl.when(has_outer)
            def _():
                finish(p_ref)
                outward(c).start()

            @pl.when(jnp.logical_not(has_outer))
            def _():
                finish(x_ref)

    @pl.loop(0, chunks)
    def _(c):
        @pl.when(jnp.logical_not(middle))
        def _():
            outward(c).wait_recv()

            @pl.when(has_outer)
            def _():
                outward(c).start()

        inward(x_ref, c).wait_send()

        @pl.when(has_outer)
        def _():
            outward(c).wait_send()


def line_sum(x, collective_id, chunks=8):
    n = lax.axis_size("tensor")
    if n == 1:
        return x
    if n % 2:
        return lax.psum(x, "tensor")
    while x.shape[0] % (16 * chunks):
        chunks //= 2
    return pl.pallas_call(
        functools.partial(line_sum_kernel, chunks),
        out_shape=jax.ShapeDtypeStruct(x.shape, x.dtype),
        in_specs=[pl.BlockSpec(memory_space=pltpu.VMEM)],
        out_specs=pl.BlockSpec(memory_space=pltpu.VMEM),
        scratch_shapes=[
            pltpu.VMEM(x.shape, x.dtype),
            pltpu.VMEM((2,) + x.shape, x.dtype),
            pltpu.SemaphoreType.DMA((chunks,)),
            pltpu.SemaphoreType.DMA((2, chunks)),
            pltpu.SemaphoreType.DMA((chunks,)),
            pltpu.SemaphoreType.DMA((chunks,)),
        ],
        name="line_sum",
        compiler_params=pltpu.CompilerParams(
            collective_id=collective_id, has_side_effects=True, vmem_limit_bytes=40 << 20),
    )(x)


def exchange_axes():
    dp_bits = lax.axis_size("dp").bit_length() - 1
    seq_bits = lax.axis_size("seq").bit_length() - 1
    return [("dp", b) for b in reversed(range(dp_bits))] + [("seq", b) for b in reversed(range(seq_bits))]


def scatter_kernel(orders, axes, *refs):
    count = len(orders)
    phases = len(axes)
    in_refs = refs[:count]
    out_refs = refs[count : 2 * count]
    scratch = refs[2 * count :]
    lands = [scratch[k * count : (k + 1) * count] for k in range(phases)]
    sums = [scratch[(phases + k) * count : (phases + k + 1) * count] for k in range(phases - 1)]
    send_sem, land_sem = scratch[-2:]
    here = {"dp": lax.axis_index("dp"), "seq": lax.axis_index("seq")}

    def bit(axis):
        name, b = axis
        return lax.rem(here[name] // (1 << b), 2)

    def partner(axis):
        name, b = axis
        return {name: here[name] + (1 - 2 * bit(axis)) * (1 << b)}

    barrier = pltpu.get_barrier_semaphore()
    for axis in axes:
        pl.semaphore_signal(barrier, inc=1, device_id=partner(axis), device_id_type=MESH)
    pl.semaphore_wait(barrier, phases)

    def view(ref, place, index):
        return ref.at[(slice(None),) * place + (index,)]

    def place_of(i, k):
        left = [a for a in range(phases) if a not in orders[i][:k]]
        return left.index(orders[i][k])

    def source(i, k):
        return in_refs[i] if k == 0 else sums[k - 1][i]

    def copy(i, k):
        axis = axes[orders[i][k]]
        return pltpu.make_async_remote_copy(
            view(source(i, k), place_of(i, k), 1 - bit(axis)), lands[k][i], send_sem.at[k, i],
            land_sem.at[k, i], device_id=partner(axis), device_id_type=MESH)

    for i in range(count):
        copy(i, 0).start()
    for k in range(phases):
        for i in range(count):
            copy(i, k).wait_recv()
            axis = axes[orders[i][k]]
            kept = view(source(i, k), place_of(i, k), bit(axis))
            total = kept[...].astype(jnp.float32) + lands[k][i][...].astype(jnp.float32)
            if k == phases - 1:
                out_refs[i][...] = total
            else:
                sums[k][i][...] = total.astype(jnp.bfloat16)
                copy(i, k + 1).start()
    for k in range(phases):
        for i in range(count):
            copy(i, k).wait_send()


def scatter_sums(arrays, collective_id):
    dp, seq = lax.axis_size("dp"), lax.axis_size("seq")
    if dp & (dp - 1) or seq & (seq - 1) or dp * seq == 1:
        return [
            lax.psum_scatter(a, ("dp", "seq"), scatter_dimension=0, tiled=True).astype(jnp.float32)
            for a in arrays
        ]
    axes = exchange_axes()
    phases = len(axes)
    near = [k for k in range(phases) if axes[k][0] == "seq"][::-1]
    far = [k for k in range(phases) if axes[k][0] == "dp"]
    loads = [0, 0]
    orders = []
    for a in arrays:
        side = 0 if loads[0] <= loads[1] else 1
        loads[side] += a.shape[1]
        orders.append(tuple(near + (far if side else far[::-1])))
    blocks = [a.reshape((2,) * phases + (a.shape[0] // (dp * seq), a.shape[1])) for a in arrays]
    tails = [b.shape[phases:] for b in blocks]
    scratch = []
    for k in range(phases):
        scratch += [pltpu.VMEM((2,) * (phases - k - 1) + t, jnp.bfloat16) for t in tails]
    for k in range(phases - 1):
        scratch += [pltpu.VMEM((2,) * (phases - k - 1) + t, jnp.bfloat16) for t in tails]
    scratch += [pltpu.SemaphoreType.DMA((phases, len(arrays)))] * 2
    return pl.pallas_call(
        functools.partial(scatter_kernel, orders, axes),
        out_shape=[jax.ShapeDtypeStruct(t, jnp.float32) for t in tails],
        in_specs=[pl.BlockSpec(memory_space=pltpu.VMEM)] * len(arrays),
        out_specs=[pl.BlockSpec(memory_space=pltpu.VMEM)] * len(arrays),
        scratch_shapes=scratch,
        name="scatter_sums",
        compiler_params=pltpu.CompilerParams(
            collective_id=collective_id, has_side_effects=True, vmem_limit_bytes=50 << 20),
    )(*blocks)


EPS = 1e-06
THETA = 1000000.0
NEG_FILL = -1e30


def shifted(array, axis, by):
    devices = lax.axis_size(axis)
    pairs = [(i, i + by) for i in range(devices) if 0 <= i + by < devices]
    return lax.ppermute(array, axis, pairs)


def rope_tables(places):
    halves = HEAD_SIZE // 2
    frequency = THETA ** (-(jnp.arange(halves, dtype=jnp.float32) * 2.0) / HEAD_SIZE)
    angle = places.astype(jnp.float32)[..., None] * frequency
    cosine = jnp.cos(angle)
    sine_part = jnp.sin(angle)
    return (
        jnp.concatenate([cosine, cosine], -1)[..., None, :],
        jnp.concatenate([sine_part, sine_part], -1)[..., None, :],
    )


def apply_rotary(value_block, rotary_tables):
    cosine, sine_part = rotary_tables
    halves = value_block.shape[-1] // 2
    turned = jnp.concatenate([-value_block[..., halves:], value_block[..., :halves]], -1)
    return value_block * cosine + turned * sine_part


def rotate_back(grad, rotary_tables):
    cosine, sine_part = rotary_tables
    halves = grad.shape[-1] // 2
    scaled = grad * sine_part
    return grad * cosine + jnp.concatenate([scaled[..., halves:], -scaled[..., :halves]], -1)


def norm_forward(value_block, gain):
    inverse = lax.rsqrt(jnp.mean(value_block * value_block, -1, keepdims=True) + EPS)
    normed = value_block * inverse
    return (normed * gain, normed, inverse)


def norm_backward(grad, gain, normed, inverse):
    scaled = grad * gain
    inner = jnp.mean(scaled * normed, -1, keepdims=True)
    gain_grad = jnp.sum((grad * normed).reshape(-1, grad.shape[-1]), 0)
    return (inverse * (scaled - normed * inner), gain_grad)


def forward_layer(hidden, weights, rotary_tables, visible, reach, stretch, ids):
    gain_a, w_q, key_weight, value_weight, query_norm_scale, gain_k, w_o, gain_m, w_g, w_u, w_d = (
        weights
    )
    seqs_here = visible.shape[0]
    rows = hidden.shape[0]
    scale = HEAD_SIZE ** (-0.5)
    attention_input, attn_hat, attn_inverse = norm_forward(hidden, gain_a.astype(jnp.float32))
    attn_low = attention_input.astype(jnp.bfloat16)
    query_unnormed = jnp.dot(attn_low, w_q, preferred_element_type=jnp.float32).reshape(
        seqs_here, stretch, -1, HEAD_SIZE
    )
    key_unnormed = jnp.dot(attn_low, key_weight, preferred_element_type=jnp.float32).reshape(
        seqs_here, stretch, -1, HEAD_SIZE
    )
    values_low = jnp.dot(attn_low, value_weight, preferred_element_type=jnp.float32).astype(
        jnp.bfloat16
    )
    key_heads = key_unnormed.shape[2]
    q_normed, q_hat, q_inverse = norm_forward(query_unnormed, query_norm_scale.astype(jnp.float32))
    k_normed, k_hat, k_inverse = norm_forward(key_unnormed, gain_k.astype(jnp.float32))
    queries_low = apply_rotary(q_normed, rotary_tables).astype(jnp.bfloat16)
    keys_low = (
        apply_rotary(k_normed, rotary_tables)
        .astype(jnp.bfloat16)
        .reshape(seqs_here, stretch, key_heads * HEAD_SIZE)
    )
    local_pair = jnp.stack(
        [keys_low, values_low.reshape(seqs_here, stretch, key_heads * HEAD_SIZE)]
    )
    earlier = [shifted(local_pair, "seq", back) for back in range(reach, 0, -1)]
    window_pair = jnp.concatenate(earlier + [local_pair], 2)
    queries_flat = queries_low.reshape(rows, -1)
    context_low, context, lse = attention_forward(
        queries_flat, window_pair[0], window_pair[1], visible, reach * stretch
    )
    attn_part = jnp.dot(context_low, w_o, preferred_element_type=jnp.float32)
    hidden_mid = hidden + line_sum(attn_part.astype(jnp.bfloat16), ids + 0).astype(jnp.float32)
    mlp_in, mlp_hat, mlp_inverse = norm_forward(hidden_mid, gain_m.astype(jnp.float32))
    mlp_low = mlp_in.astype(jnp.bfloat16)
    gate = jnp.dot(mlp_low, w_g, preferred_element_type=jnp.float32)
    up_branch = jnp.dot(mlp_low, w_u, preferred_element_type=jnp.float32)
    act_low = (jax.nn.silu(gate) * up_branch).astype(jnp.bfloat16)
    mlp_part = jnp.dot(act_low, w_d, preferred_element_type=jnp.float32)
    hidden_next = hidden_mid + line_sum(mlp_part.astype(jnp.bfloat16), ids + 1).astype(jnp.float32)
    saved = dict(
        attn_hat=attn_hat,
        attn_inverse=attn_inverse,
        attn_low=attn_low,
        q_hat=q_hat,
        q_inverse=q_inverse,
        k_hat=k_hat,
        k_inverse=k_inverse,
        queries=queries_flat,
        window_pair=window_pair,
        lse=lse,
        context=context,
        context_low=context_low,
        mlp_hat=mlp_hat,
        mlp_inverse=mlp_inverse,
        mlp_low=mlp_low,
        gate=gate,
        up_branch=up_branch,
        act_low=act_low,
    )
    return (hidden_next, saved)


def backward_layer(grad, weights, saved, rotary_tables, visible, reach, stretch, ids):
    gain_a, w_q, key_weight, value_weight, query_norm_scale, gain_k, w_o, gain_m, w_g, w_u, w_d = (
        weights
    )
    seqs_here = visible.shape[0]
    rows = grad.shape[0]
    scale = HEAD_SIZE ** (-0.5)
    grad_low = grad.astype(jnp.bfloat16)
    grad_down_turned = jnp.einsum(
        "rf,rd->df", saved["act_low"], grad_low, preferred_element_type=jnp.float32
    )
    d_act = jnp.einsum("rd,fd->rf", grad_low, w_d, preferred_element_type=jnp.float32)
    gate = saved["gate"]
    sigma = jax.nn.sigmoid(gate)
    d_gate = (d_act * saved["up_branch"] * sigma * (1.0 + gate * (1.0 - sigma))).astype(
        jnp.bfloat16
    )
    d_up = (d_act * gate * sigma).astype(jnp.bfloat16)
    grad_gate = jnp.einsum(
        "rd,rf->df", saved["mlp_low"], d_gate, preferred_element_type=jnp.float32
    )
    grad_up = jnp.einsum("rd,rf->df", saved["mlp_low"], d_up, preferred_element_type=jnp.float32)
    d_mlp_part = jnp.einsum(
        "rf,df->rd", d_gate, w_g, preferred_element_type=jnp.float32
    ) + jnp.einsum("rf,df->rd", d_up, w_u, preferred_element_type=jnp.float32)
    d_mlp_in = line_sum(d_mlp_part.astype(jnp.bfloat16), ids + 2).astype(jnp.float32)
    d_mid, grad_gain_m = norm_backward(
        d_mlp_in, gain_m.astype(jnp.float32), saved["mlp_hat"], saved["mlp_inverse"]
    )
    grad_mid = grad + d_mid
    mid_low = grad_mid.astype(jnp.bfloat16)
    grad_o_turned = jnp.einsum(
        "rc,rd->dc", saved["context_low"], mid_low, preferred_element_type=jnp.float32
    )
    d_context = jnp.einsum("rd,cd->rc", mid_low, w_o, preferred_element_type=jnp.float32)
    d_context = d_context.astype(jnp.bfloat16)
    key_window, value_window = saved["window_pair"]
    key_heads = key_window.shape[2] // HEAD_SIZE
    d_queries, d_key_window, d_value_window = attention_backward(
        saved["queries"], d_context, saved["context"], saved["lse"], key_window, value_window,
        visible, reach * stretch,
    )
    d_pair = jnp.stack([d_key_window, d_value_window])
    own_pair = d_pair[:, :, reach * stretch :]
    for back in range(1, reach + 1):
        piece = d_pair[:, :, (reach - back) * stretch : (reach - back + 1) * stretch]
        own_pair = own_pair + shifted(piece.astype(jnp.bfloat16), "seq", -back).astype(piece.dtype)
    d_keys = own_pair[0].reshape(seqs_here, stretch, key_heads, HEAD_SIZE)
    d_values_low = own_pair[1].astype(jnp.bfloat16).reshape(rows, -1)
    d_q_normed = rotate_back(d_queries.reshape(seqs_here, stretch, -1, HEAD_SIZE), rotary_tables)
    d_k_normed = rotate_back(d_keys, rotary_tables)
    d_q_raw, grad_gain_q = norm_backward(
        d_q_normed, query_norm_scale.astype(jnp.float32), saved["q_hat"], saved["q_inverse"]
    )
    d_k_raw, grad_gain_k = norm_backward(
        d_k_normed, gain_k.astype(jnp.float32), saved["k_hat"], saved["k_inverse"]
    )
    d_q_low = d_q_raw.astype(jnp.bfloat16).reshape(rows, -1)
    d_k_low = d_k_raw.astype(jnp.bfloat16).reshape(rows, -1)
    attn_low = saved["attn_low"]
    grad_q = jnp.einsum("rd,rc->dc", attn_low, d_q_low, preferred_element_type=jnp.float32)
    grad_k = jnp.einsum("rd,rc->dc", attn_low, d_k_low, preferred_element_type=jnp.float32)
    grad_v = jnp.einsum("rd,rc->dc", attn_low, d_values_low, preferred_element_type=jnp.float32)
    d_attn_part = (
        jnp.einsum("rc,dc->rd", d_q_low, w_q, preferred_element_type=jnp.float32)
        + jnp.einsum("rc,dc->rd", d_k_low, key_weight, preferred_element_type=jnp.float32)
        + jnp.einsum("rc,dc->rd", d_values_low, value_weight, preferred_element_type=jnp.float32)
    )
    d_attn_in, grad_gain_q, grad_gain_k = (
        line_sum(d_attn_part.astype(jnp.bfloat16), ids + 3).astype(jnp.float32),
        lax.psum(grad_gain_q.astype(jnp.bfloat16), "tensor").astype(jnp.float32),
        lax.psum(grad_gain_k.astype(jnp.bfloat16), "tensor").astype(jnp.float32),
    )
    d_hidden, grad_gain_a = norm_backward(
        d_attn_in, gain_a.astype(jnp.float32), saved["attn_hat"], saved["attn_inverse"]
    )
    gain_grads = (grad_gain_a, grad_gain_q, grad_gain_k, grad_gain_m)
    matrix_grads = (grad_q, grad_k, grad_v, grad_o_turned, grad_gate, grad_up, grad_down_turned)
    return (grad_mid + d_hidden, gain_grads, matrix_grads)


def reduce_grads(gain_grads, matrix_grads, ids):
    gain_a, gain_q, gain_k, gain_m = gain_grads
    gain_a, gain_q, gain_k, gain_m = lax.psum((gain_a, gain_q, gain_k, gain_m), ("dp", "seq"))
    grad_q, grad_k, grad_v, grad_o_turned, grad_gate, grad_up, grad_down_turned = matrix_grads
    grad_q, grad_k, grad_v, grad_o_turned, grad_gate, grad_up, grad_down_turned = scatter_sums(
        [g.astype(jnp.bfloat16) for g in matrix_grads], ids
    )
    return [
        gain_a,
        grad_q,
        grad_k,
        grad_v,
        gain_q,
        gain_k,
        grad_o_turned.T,
        gain_m,
        grad_gate,
        grad_up,
        grad_down_turned.T,
    ]


def per_device(
    tokens,
    cotangent,
    segments,
    positions,
    attn_gain,
    w_query,
    key_projection,
    value_projection,
    query_gain,
    key_gain,
    w_output,
    mlp_gain,
    w_gate,
    w_up,
    w_down,
):
    seqs_here, stretch, width = tokens.shape
    rows = seqs_here * stretch
    seq_count = lax.axis_size("seq")
    place = lax.axis_index("seq")
    reach = min(seq_count - 1, (WINDOW + stretch - 2) // stretch)
    span = (reach + 1) * stretch
    every_doc = lax.all_gather(segments, "seq", axis=1, tiled=True)
    padded_docs = jnp.concatenate(
        [jnp.full((seqs_here, reach * stretch), -1, jnp.int32), every_doc], 1
    )
    key_docs = lax.dynamic_slice_in_dim(padded_docs, place * stretch, span, 1)
    index = jnp.arange(stretch, dtype=jnp.int32)
    doc_start = jnp.sum((key_docs[:, None, :] < segments[:, :, None]).astype(jnp.int32), 2)
    low = jnp.maximum(doc_start, reach * stretch + index - (WINDOW - 1))
    visible = low
    rotary_tables = rope_tables(positions)
    stacked = (
        attn_gain,
        w_query,
        key_projection,
        value_projection,
        query_gain,
        key_gain,
        w_output,
        mlp_gain,
        w_gate,
        w_up,
        w_down,
    )
    hidden = tokens.astype(jnp.float32).reshape(rows, width)
    saved_layers = []
    for layer_index in range(LAYER_COUNT):
        weights = tuple((w[layer_index] for w in stacked))
        hidden, saved = forward_layer(hidden, weights, rotary_tables, visible, reach, stretch, 1 + 8 * layer_index)
        saved_layers.append(saved)
    output = hidden.astype(jnp.bfloat16).reshape(seqs_here, stretch, width)
    grad = cotangent.astype(jnp.float32).reshape(rows, width)
    reduced = [None] * LAYER_COUNT
    for layer_index in range(LAYER_COUNT - 1, -1, -1):
        weights = tuple((w[layer_index] for w in stacked))
        grad, gain_grads, matrix_grads = backward_layer(
            grad, weights, saved_layers[layer_index], rotary_tables, visible, reach, stretch,
            1 + 8 * layer_index,
        )
        reduced[layer_index] = reduce_grads(gain_grads, matrix_grads, 5 + 8 * layer_index)
    input_grad = grad.reshape(seqs_here, stretch, width)
    outs = [
        jnp.stack([reduced[layer_index][slot] for layer_index in range(LAYER_COUNT)])
        for slot in range(11)
    ]
    return (
        output,
        input_grad,
        outs[0],
        outs[1],
        outs[2],
        outs[3],
        outs[4],
        outs[5],
        outs[6],
        outs[7],
        outs[8],
        outs[9],
        outs[10],
    )


def solution(mesh):
    placed = (
        P("dp", "seq", None),
        P("dp", "seq", None),
        P("dp", "seq"),
        P("dp", "seq"),
        P(),
        P(None, None, "tensor"),
        P(None, None, "tensor"),
        P(None, None, "tensor"),
        P(),
        P(),
        P(None, "tensor", None),
        P(),
        P(None, None, "tensor"),
        P(None, None, "tensor"),
        P(None, "tensor", None),
    )
    return jax.shard_map(
        per_device,
        mesh=mesh,
        in_specs=placed,
        out_specs=(
            P("dp", "seq", None),
            P("dp", "seq", None),
            P(),
            P(None, ("dp", "seq"), "tensor"),
            P(None, ("dp", "seq"), "tensor"),
            P(None, ("dp", "seq"), "tensor"),
            P(),
            P(),
            P(None, "tensor", ("dp", "seq")),
            P(),
            P(None, ("dp", "seq"), "tensor"),
            P(None, ("dp", "seq"), "tensor"),
            P(None, "tensor", ("dp", "seq")),
        ),
        check_vma=False,
    )
```

```python
import functools
import types

import jax
import jax.numpy as jnp
from jax import lax
from jax.experimental import pallas as pl
from jax.experimental.pallas import tpu as pltpu
from jax.sharding import PartitionSpec as P

HEAD = 128
LAYER_COUNT = 2
WINDOW = 1024
EPS = 1e-06
THETA = 1000000.0
LOG2E = 1.4426950408889634
SCALE = HEAD ** (-0.5)
CHUNK = 128
PIECES = 2
MESH = pl.DeviceIdType.MESH
BF = jnp.bfloat16
F32 = jnp.float32

NT = (((1,), (1,)), ((), ()))
NN = (((1,), (0,)), ((), ()))
TN = (((0,), (0,)), ((), ()))


def dot(a, b, dims=NN):
    return lax.dot_general(a, b, dims, preferred_element_type=F32)


def attn_fwd_kernel(qb, kb, offset, stretch, first_ref, low_ref, q_ref, k_ref, v_ref, o_ref, lse_ref):
    step = pl.program_id(2)
    heads = q_ref.shape[1] // HEAD
    q_start = step * qb + offset
    queries = [q_ref[:, h * HEAD : (h + 1) * HEAD] for h in range(heads)]
    q_index = q_start + lax.broadcasted_iota(jnp.int32, (qb, 1), 0)
    low = low_ref[...]

    def block(kk, carry):
        start = kk * kb
        place = (start // stretch, pl.ds(pl.multiple_of(lax.rem(start, stretch), kb), kb))
        keys = k_ref[place]
        values = v_ref[place]
        key_index = start + lax.broadcasted_iota(jnp.int32, (qb, kb), 1)
        mask = (key_index >= low) & (key_index <= q_index)
        out = []
        for h in range(heads):
            acc, total = carry[h]
            s = dot(queries[h], keys, NT) * (SCALE * LOG2E)
            p = jnp.where(mask, jnp.exp2(s), 0.0)
            part = p[:, :HEAD]
            for c in range(1, kb // HEAD):
                part = part + p[:, c * HEAD : (c + 1) * HEAD]
            out.append((acc + dot(p.astype(BF), values), total + part))
        return tuple(out)

    zero = jnp.zeros((qb, HEAD), F32)
    first = first_ref[pl.program_id(0) * pl.num_programs(2) + step] // kb
    last = (q_start + qb - 1) // kb + 1
    result = lax.fori_loop(first, last, block, tuple((zero, zero) for _ in range(heads)))
    for h in range(heads):
        acc, total = result[h]
        o_ref[:, h * HEAD : (h + 1) * HEAD] = (acc / jnp.sum(total, 1, keepdims=True)).astype(BF)
        lse_ref[h : h + 1, :] = jnp.log2(jnp.sum(total.T, 0, keepdims=True))


def attn_fwd(q, window, first, low, stretch, qb=512, kb=512):
    rows = q.shape[0]
    reach = window.shape[0] - 1
    kv_heads = window.shape[2] // (2 * HEAD)
    width = q.shape[1] // kv_heads
    group = width // HEAD
    steps = stretch // qb
    return pl.pallas_call(
        functools.partial(attn_fwd_kernel, qb, kb, reach * stretch, stretch),
        grid_spec=pltpu.PrefetchScalarGridSpec(
            num_scalar_prefetch=1,
            grid=(rows // stretch, kv_heads, steps),
            in_specs=[
                pl.BlockSpec((qb, 1), lambda s, g, i, f: (s * steps + i, 0)),
                pl.BlockSpec((qb, width), lambda s, g, i, f: (s * steps + i, g)),
                pl.BlockSpec((reach + 1, stretch, HEAD), lambda s, g, i, f: (0, s, g)),
                pl.BlockSpec((reach + 1, stretch, HEAD), lambda s, g, i, f: (0, s, kv_heads + g)),
            ],
            out_specs=[
                pl.BlockSpec((qb, width), lambda s, g, i, f: (s * steps + i, g)),
                pl.BlockSpec((None, group, qb), lambda s, g, i, f: (g, 0, s * steps + i)),
            ],
        ),
        out_shape=[
            jax.ShapeDtypeStruct(q.shape, BF),
            jax.ShapeDtypeStruct((kv_heads, group, rows), F32),
        ],
        name=attn_fwd.__name__,
        compiler_params=pltpu.CompilerParams(vmem_limit_bytes=62 << 20),
    )(first, low[:, None], q, window, window)


def attn_bwd_kernel(qb, kb, offset, stretch, first_ref, low_ref, lse_ref, q_ref, do_ref, o_ref, k_ref, v_ref,
                    dq_ref, own_ref, prev_ref, dk_ref, dv_ref):
    step = pl.program_id(2)
    heads = q_ref.shape[1] // HEAD
    q_start = step * qb + offset

    @pl.when(step == 0)
    def _():
        dk_ref[...] = jnp.zeros_like(dk_ref)
        dv_ref[...] = jnp.zeros_like(dv_ref)

    def stack(ref):
        return jnp.concatenate([ref[:, h * HEAD : (h + 1) * HEAD] for h in range(heads)], 0)

    queries = stack(q_ref)
    d_out = stack(do_ref)
    q_index = q_start + lax.broadcasted_iota(jnp.int32, (1, qb), 1)
    low = low_ref[...]
    lse = jnp.concatenate([lse_ref[h : h + 1, :] for h in range(heads)], 1)
    product = d_out.astype(F32) * stack(o_ref).astype(F32)
    delta = jnp.sum(product.T, 0, keepdims=True)

    def block(kk, dq):
        start = kk * kb
        place = (start // stretch, pl.ds(pl.multiple_of(lax.rem(start, stretch), kb), kb))
        here = pl.ds(pl.multiple_of(start, kb), kb)
        keys = k_ref[place]
        values = v_ref[place]
        key_index = start + lax.broadcasted_iota(jnp.int32, (kb, qb), 0)
        mask = (key_index >= low) & (key_index <= q_index)
        mask = jnp.concatenate([mask] * heads, 1)
        s = dot(keys, queries, NT) * (SCALE * LOG2E) - lse
        p = jnp.where(mask, jnp.exp2(s), 0.0)
        dp = dot(values, d_out, NT)
        ds = (p * (dp - delta)).astype(BF)
        dv_ref[here, :] += dot(p.astype(BF), d_out)
        dk_ref[here, :] += dot(ds, queries)
        return dq + dot(ds, keys, TN)

    first = first_ref[pl.program_id(0) * pl.num_programs(2) + step] // kb
    last = (q_start + qb - 1) // kb + 1
    dq = lax.fori_loop(first, last, block, jnp.zeros((heads * qb, HEAD), F32))
    for h in range(heads):
        dq_ref[:, h * HEAD : (h + 1) * HEAD] = dq[h * qb : (h + 1) * qb] * SCALE

    @pl.when(step == pl.num_programs(2) - 1)
    def _():
        own_ref[0] = dk_ref[offset:, :] * SCALE
        own_ref[1] = dv_ref[offset:, :]
        for j in range(offset // stretch):
            prev_ref[j, 0] = (dk_ref[j * stretch : (j + 1) * stretch, :] * SCALE).astype(BF)
            prev_ref[j, 1] = dv_ref[j * stretch : (j + 1) * stretch, :].astype(BF)


def attn_bwd(q, d_out, o, window, first, low, lse, stretch, qb=512, kb=512):
    rows = q.shape[0]
    reach = window.shape[0] - 1
    kv_heads = window.shape[2] // (2 * HEAD)
    width = q.shape[1] // kv_heads
    group = width // HEAD
    steps = stretch // qb
    span = (reach + 1) * stretch
    held = max(reach, 1)
    row_spec = pl.BlockSpec((qb, width), lambda s, g, i, f: (s * steps + i, g))
    return pl.pallas_call(
        functools.partial(attn_bwd_kernel, qb, kb, reach * stretch, stretch),
        grid_spec=pltpu.PrefetchScalarGridSpec(
            num_scalar_prefetch=1,
            grid=(rows // stretch, kv_heads, steps),
            in_specs=[
                pl.BlockSpec((1, qb), lambda s, g, i, f: (0, s * steps + i)),
                pl.BlockSpec((None, group, qb), lambda s, g, i, f: (g, 0, s * steps + i)),
                row_spec,
                row_spec,
                row_spec,
                pl.BlockSpec((reach + 1, stretch, HEAD), lambda s, g, i, f: (0, s, g)),
                pl.BlockSpec((reach + 1, stretch, HEAD), lambda s, g, i, f: (0, s, kv_heads + g)),
            ],
            out_specs=[
                row_spec,
                pl.BlockSpec((2, stretch, HEAD), lambda s, g, i, f: (0, s, g)),
                pl.BlockSpec((held, 2, stretch, HEAD), lambda s, g, i, f: (0, 0, s, g)),
            ],
            scratch_shapes=[pltpu.VMEM((span, HEAD), F32), pltpu.VMEM((span, HEAD), F32)],
        ),
        out_shape=[
            jax.ShapeDtypeStruct(q.shape, F32),
            jax.ShapeDtypeStruct((2, rows, kv_heads * HEAD), F32),
            jax.ShapeDtypeStruct((held, 2, rows, kv_heads * HEAD), BF),
        ],
        name=attn_bwd.__name__,
        cost_estimate=pl.CostEstimate(flops=3 * 10**10, bytes_accessed=12 * 2**20, transcendentals=4 * 2**20),
        compiler_params=pltpu.CompilerParams(vmem_limit_bytes=62 << 20),
    )(first, low[None], lse, q, d_out, o, window, window)


def chunk_index(schedule, s):
    rate, lag, count = schedule
    return jnp.clip((s - lag) // rate, 0, count - 1)


def rows_spec(schedule, shape):
    return pl.BlockSpec((shape[0] // schedule[2], shape[1]), lambda s: (chunk_index(schedule, s), 0))


WHOLE, HBM = object(), object()
MLP_WEIGHTS = ("w_gate", "w_up", "w_down")
QKV_WEIGHTS = ("w_q", "w_k", "w_v")
GRAD_OPERANDS = ("d_gate_all", "d_up_all", "context_all", "act_all")


def of_layer(array, layer):
    shape = array.shape[1:]
    zeros = (0,) * len(shape)
    return array, pl.BlockSpec((None,) + shape, lambda s: (layer,) + zeros, pipeline_mode=pl.Buffered(1))


class Late:
    def __init__(self, layer=None):
        self.layer = layer

    def shape(self, array):
        return array.shape if self.layer is None else array.shape[1:]

    def copy(self, source, held, sem):
        return pltpu.make_async_copy(source if self.layer is None else source.at[self.layer], held, sem)


def step_kernel(owner, body, steps, ins, outs, scratch, collective_id, vmem=62):
    def spec(shape, where, is_in):
        if isinstance(where, pl.BlockSpec):
            return where
        if where is HBM or isinstance(where, Late):
            return pl.BlockSpec(memory_space=pl.ANY)
        if where is WHOLE:
            zeros = (0,) * len(shape)
            if is_in:
                return pl.BlockSpec(shape, lambda s: zeros, pipeline_mode=pl.Buffered(1))
            return pl.BlockSpec(memory_space=pltpu.VMEM)
        return rows_spec(where, shape)

    late = {name: where for name, (_, where) in ins.items() if isinstance(where, Late)}
    held = {name: pltpu.VMEM(where.shape(ins[name][0]), ins[name][0].dtype) for name, where in late.items()}
    flat, tree = jax.tree.flatten((scratch, held, {name: pltpu.SemaphoreType.DMA(()) for name in late}))

    def kernel(*refs):
        named = dict(zip(ins, refs))
        named.update(zip(outs, refs[len(ins) :]))
        own, held_refs, sems = jax.tree.unflatten(tree, refs[len(ins) + len(outs) :])
        copies = {name: where.copy(named[name], held_refs[name], sems[name]) for name, where in late.items()}
        for name, ref in own.items():
            named[name] = types.SimpleNamespace(**ref) if isinstance(ref, dict) else ref
        named.update(held_refs)
        s = pl.program_id(0)

        @pl.when(s == 0)
        def _():
            for copy in copies.values():
                copy.start()

        def arrived(step, *names):
            @pl.when(s == step)
            def _():
                for name in names:
                    copies[name].wait()

        body(types.SimpleNamespace(arrived=arrived, **named), s)

    results = pl.pallas_call(
        kernel,
        grid=(steps,),
        in_specs=[spec(a.shape, w, True) for a, w in ins.values()],
        out_specs=[spec(shape, w, False) for shape, _, w in outs.values()],
        out_shape=[jax.ShapeDtypeStruct(shape, dtype) for shape, dtype, _ in outs.values()],
        scratch_shapes=flat,
        name=owner.__name__,
        compiler_params=pltpu.CompilerParams(
            collective_id=collective_id, has_side_effects=True, vmem_limit_bytes=vmem << 20
        ),
    )(*[a for a, _ in ins.values()])
    return types.SimpleNamespace(**dict(zip(outs, results)))


def at_chunk(s, schedule, work):
    rate, lag, count = schedule
    moved = s - lag
    here = (moved >= 0) & (moved < rate * count)
    if rate > 1:
        here = here & (lax.rem(moved, rate) == 0)

    @pl.when(here)
    def _():
        work(moved // rate if rate > 1 else moved)


def enter(devices):
    barrier = pltpu.get_barrier_semaphore()
    count = 0
    for device, exists in devices:
        if exists is True:
            pl.semaphore_signal(barrier, inc=1, device_id=device, device_id_type=MESH)
            count = count + 1
        else:

            @pl.when(exists)
            def _():
                pl.semaphore_signal(barrier, inc=1, device_id=device, device_id_type=MESH)

            count = count + jnp.where(exists, 1, 0)
    pl.semaphore_wait(barrier, count)


class LineSum:
    def __init__(self, refs, x=None):
        self.x, self.land = refs.x if x is None else x, refs.land
        self.send_sem, self.land_sem, self.out_sem = refs.send, refs.arrive, refs.out
        self.pieces = self.send_sem.shape[0]
        self.rows = self.x.shape[0] // self.pieces
        n = lax.axis_size("tensor")
        z = lax.axis_index("tensor")
        half = n // 2
        self.middle = (z == half - 1) | (z == half)
        self.has_outer = (z > 0) & (z < n - 1)
        self.inner = jnp.where(z < half, z + 1, z - 1)
        self.outer = jnp.clip(jnp.where(z < half, z - 1, z + 1), 0, n - 1)
        self.slot = jnp.where(self.middle, 1, 0)

    @staticmethod
    def scratch(rows, width, pieces):
        return dict(
            x=pltpu.VMEM((rows, width), BF),
            land=pltpu.VMEM((2, rows, width), BF),
            send=pltpu.SemaphoreType.DMA((pieces,)),
            arrive=pltpu.SemaphoreType.DMA((2, pieces)),
            out=pltpu.SemaphoreType.DMA((pieces,)),
        )

    def neighbours(self):
        return [({"tensor": self.inner}, True), ({"tensor": self.outer}, self.has_outer)]

    def at(self, j, rows=None):
        rows = rows or self.rows
        return pl.ds(pl.multiple_of(j * rows, rows), rows)

    def inward(self, source, j, slot):
        return pltpu.make_async_remote_copy(
            source.at[self.at(j)], self.land.at[slot, self.at(j)], self.send_sem.at[j], self.land_sem.at[slot, j],
            device_id={"tensor": self.inner}, device_id_type=MESH)

    def outward(self, j):
        return pltpu.make_async_remote_copy(
            self.land.at[1, self.at(j)], self.land.at[1, self.at(j)], self.out_sem.at[j], self.land_sem.at[1, j],
            device_id={"tensor": self.outer}, device_id_type=MESH)

    def put(self, c, value):
        rows = value.shape[0]
        self.x[self.at(c, rows), :] = value.astype(BF)
        self.push(c, rows)

    def push(self, c, rows):
        @pl.when(jnp.logical_not(self.has_outer))
        def _():
            for i in range(rows // self.rows):
                self.inward(self.x, c * (rows // self.rows) + i, self.slot).start()

    def add(self, j, source, slot):
        self.land[slot, self.at(j), :] = (
            source[self.at(j), :].astype(F32) + self.land[slot, self.at(j), :].astype(F32)
        ).astype(BF)

    def relay(self, j):
        @pl.when(self.has_outer)
        def _():
            self.inward(self.x, j, 0).wait_recv()
            self.add(j, self.x, 0)
            self.inward(self.land.at[0], j, self.slot).start()

    def meet(self, j):
        @pl.when(self.middle)
        def _():
            self.inward(self.x, j, 1).wait_recv()

            @pl.when(self.has_outer)
            def _():
                self.add(j, self.land.at[0], 1)
                self.outward(j).start()

            @pl.when(jnp.logical_not(self.has_outer))
            def _():
                self.add(j, self.x, 1)

    def total(self, c, rows):
        @pl.when(jnp.logical_not(self.middle))
        def _():
            for i in range(rows // self.rows):
                j = c * (rows // self.rows) + i
                self.inward(self.x, j, 1).wait_recv()

                @pl.when(self.has_outer)
                def _():
                    self.outward(j).start()

        return self.land[1, self.at(c, rows), :].astype(F32)

    def finish(self):
        @pl.when(self.has_outer)
        def _():
            @pl.loop(0, self.pieces)
            def _(j):
                self.inward(self.land.at[0], j, self.slot).wait_send()
                self.outward(j).wait_send()

        @pl.when(jnp.logical_not(self.has_outer))
        def _():
            @pl.loop(0, self.pieces)
            def _(j):
                self.inward(self.x, j, self.slot).wait_send()


class Spread(LineSum):
    @staticmethod
    def scratch(rows, width, pieces):
        return dict(
            land=pltpu.VMEM((2, rows, width), BF),
            send=pltpu.SemaphoreType.DMA((pieces,)),
            arrive=pltpu.SemaphoreType.DMA((2, pieces)),
            out=pltpu.SemaphoreType.DMA((pieces,)),
        )

    def start(self):
        @pl.when(self.middle)
        def _():
            @pl.loop(0, self.pieces)
            def _(j):
                self.land[1, self.at(j), :] = self.x[self.at(j), :]

                @pl.when(self.has_outer)
                def _():
                    self.outward(j).start()

    def finish(self):
        @pl.when(self.has_outer)
        def _():
            @pl.loop(0, self.pieces)
            def _(j):
                self.outward(j).wait_send()


class KeyValueSend:
    def __init__(self, refs, reach):
        self.held, self.window = refs.kv.held, refs.window
        self.copy_sem, self.send_sem, self.land_sem = refs.kv.copy, refs.kv.send, refs.kv.land
        self.chunks = self.copy_sem.shape[0]
        self.rows = self.held.shape[0] // self.chunks
        self.reach = reach
        self.place = lax.axis_index("seq")
        self.count = lax.axis_size("seq")

    @staticmethod
    def scratch(rows, width, chunks, reach):
        held = max(reach, 1)
        return dict(
            held=pltpu.VMEM((rows, width), BF),
            copy=pltpu.SemaphoreType.DMA((chunks,)),
            send=pltpu.SemaphoreType.DMA((held, chunks)),
            land=pltpu.SemaphoreType.DMA((held, chunks)),
        )

    def neighbours(self):
        found = []
        for back in range(1, self.reach + 1):
            found.append(({"seq": jnp.minimum(self.place + back, self.count - 1)}, self.place + back < self.count))
            found.append(({"seq": jnp.maximum(self.place - back, 0)}, self.place >= back))
        return found

    def at(self, c):
        return pl.ds(pl.multiple_of(c * self.rows, self.rows), self.rows)

    def own(self, c):
        return pltpu.make_async_copy(self.held.at[self.at(c)], self.window.at[self.reach, self.at(c)], self.copy_sem.at[c])

    def remote(self, back, c):
        return pltpu.make_async_remote_copy(
            self.held.at[self.at(c)], self.window.at[self.reach - back, self.at(c)],
            self.send_sem.at[back - 1, c], self.land_sem.at[back - 1, c],
            device_id={"seq": jnp.minimum(self.place + back, self.count - 1)}, device_id_type=MESH)

    def send(self, c):
        self.own(c).start()
        for back in range(1, self.reach + 1):

            @pl.when(self.place + back < self.count)
            def _():
                self.remote(back, c).start()

    def finish(self):
        @pl.loop(0, self.chunks)
        def _(c):
            self.own(c).wait()
            for back in range(1, self.reach + 1):

                @pl.when(self.place + back < self.count)
                def _():
                    self.remote(back, c).wait_send()

                @pl.when(self.place >= back)
                def _():
                    self.remote(back, c).wait_recv()


class KeyValueReturn:
    def __init__(self, refs, reach):
        self.prev, self.land = refs.d_prev, refs.kr.land
        self.send_sem, self.land_sem = refs.kr.send, refs.kr.arrive
        self.chunks = self.send_sem.shape[1]
        self.rows = self.land.shape[2] // self.chunks
        self.reach = reach
        self.place = lax.axis_index("seq")
        self.count = lax.axis_size("seq")

    @staticmethod
    def scratch(rows, width, chunks, reach):
        held = max(reach, 1)
        return dict(
            land=pltpu.VMEM((held, 2, rows, width), BF),
            send=pltpu.SemaphoreType.DMA((held, chunks)),
            arrive=pltpu.SemaphoreType.DMA((held, chunks)),
        )

    neighbours = KeyValueSend.neighbours
    at = KeyValueSend.at

    def copy(self, back, c):
        return pltpu.make_async_remote_copy(
            self.prev.at[self.reach - back, :, self.at(c)], self.land.at[back - 1, :, self.at(c)],
            self.send_sem.at[back - 1, c], self.land_sem.at[back - 1, c],
            device_id={"seq": jnp.maximum(self.place - back, 0)}, device_id_type=MESH)

    def start(self):
        for back in range(1, self.reach + 1):

            @pl.when(self.place >= back)
            def _():
                @pl.loop(0, self.chunks)
                def _(c):
                    self.copy(back, c).start()

    def add(self, own, c):
        for back in range(1, self.reach + 1):
            exists = self.place + back < self.count

            @pl.when(exists)
            def _():
                self.copy(back, c).wait_recv()

            own = own + jnp.where(exists, self.land[back - 1, :, self.at(c), :].astype(F32), 0.0)
        return own

    def finish(self):
        for back in range(1, self.reach + 1):

            @pl.when(self.place >= back)
            def _():
                @pl.loop(0, self.chunks)
                def _(c):
                    self.copy(back, c).wait_send()


def device_bit(axis):
    name, b = axis
    return lax.rem(lax.axis_index(name) // (1 << b), 2)


def device_partner(axis):
    name, b = axis
    return {name: lax.axis_index(name) + (1 - 2 * device_bit(axis)) * (1 << b)}


def bits_of(name):
    return lax.axis_size(name).bit_length() - 1


def block_axes():
    return [(name, b) for name in ("dp", "seq") for b in reversed(range(bits_of(name)))]


class Scatter:
    def __init__(self, refs, swapped):
        self.axes = block_axes()
        phases = len(self.axes)
        near = [k for k in range(phases) if self.axes[k][0] == "seq"][::-1]
        far = [k for k in range(phases) if self.axes[k][0] == "dp"]
        self.order = near + (far if swapped else far[::-1])
        self.buffer, self.lands = refs.held, refs.lands
        self.send_sem, self.land_sem = refs.send, refs.arrive

    @staticmethod
    def scratch(rows, width):
        phases = len(block_axes())
        return dict(
            held=pltpu.VMEM((2,) * phases + (rows, width), BF),
            lands=[pltpu.VMEM((2,) * (phases - k - 1) + (rows, width), BF) for k in range(phases)],
            send=pltpu.SemaphoreType.DMA((phases,)),
            arrive=pltpu.SemaphoreType.DMA((phases,)),
        )

    def neighbours(self):
        return [(device_partner(axis), True) for axis in self.axes]

    def put(self, block, columns, value):
        phases = len(self.axes)
        place = tuple(lax.rem(block // (1 << (phases - 1 - k)), 2) for k in range(phases))
        self.buffer[place + (slice(None), columns)] = value.astype(BF)

    def view(self, k, mine):
        index = [slice(None)] * len(self.axes)
        for earlier in self.order[:k]:
            index[earlier] = device_bit(self.axes[earlier])
        bit = device_bit(self.axes[self.order[k]])
        index[self.order[k]] = bit if mine else 1 - bit
        return tuple(index)

    def copy(self, k):
        return pltpu.make_async_remote_copy(
            self.buffer.at[self.view(k, False)], self.lands[k], self.send_sem.at[k], self.land_sem.at[k],
            device_id=device_partner(self.axes[self.order[k]]), device_id_type=MESH)

    def send(self, k):
        self.copy(k).start()

    def fold(self, k, store=None):
        self.copy(k).wait_recv()
        index = self.view(k, True)
        free = [i for i, v in enumerate(index) if isinstance(v, slice)]
        for j in range(1 << len(free)):
            place = [(j >> (len(free) - 1 - i)) & 1 for i in range(len(free))]
            here = list(index)
            for i, axis in enumerate(free):
                here[axis] = place[i]
            here = tuple(here)
            total = self.buffer[here].astype(F32) + self.lands[k][tuple(place)].astype(F32)
            if store is None:
                self.buffer[here] = total.astype(BF)
            else:
                store(total)

    def finish(self):
        for k in range(len(self.axes)):
            self.copy(k).wait_send()


class Butterfly:
    def __init__(self, refs):
        self.axes = [(name, b) for name in ("seq", "dp", "tensor") for b in range(bits_of(name))]
        self.held, self.land = refs.held, refs.land
        self.send_sem, self.land_sem = refs.send, refs.arrive

    @staticmethod
    def scratch(shape):
        phases = bits_of("seq") + bits_of("dp") + bits_of("tensor")
        return dict(
            held=pltpu.VMEM((phases + 1,) + shape, F32),
            land=pltpu.VMEM((phases,) + shape, F32),
            send=pltpu.SemaphoreType.DMA((phases,)),
            arrive=pltpu.SemaphoreType.DMA((phases,)),
        )

    def neighbours(self):
        return [(device_partner(axis), True) for axis in self.axes]

    def copy(self, k):
        return pltpu.make_async_remote_copy(
            self.held.at[k], self.land.at[k], self.send_sem.at[k], self.land_sem.at[k],
            device_id=device_partner(self.axes[k]), device_id_type=MESH)

    def put(self, value):
        self.held[0] = value
        self.copy(0).start()

    def fold(self, k):
        self.copy(k).wait_recv()
        self.held[k + 1] = self.held[k] + self.land[k]
        if k + 1 < len(self.axes):
            self.copy(k + 1).start()

    def total(self):
        return self.held[len(self.axes)]

    def finish(self):
        for k in range(len(self.axes)):
            self.copy(k).wait_send()


def norm_parts(value):
    inverse = lax.rsqrt(jnp.mean(value * value, -1, keepdims=True) + EPS)
    return value * inverse, inverse


def norm_back(grad, gain, hat, inverse):
    scaled = grad * gain
    inner = jnp.mean(scaled * hat, -1, keepdims=True)
    return inverse * (scaled - hat * inner)


def row_sums(value):
    return jnp.sum(value, 0, keepdims=True)


def heads_of(value):
    return [value[:, h * HEAD : (h + 1) * HEAD] for h in range(value.shape[1] // HEAD)]


def rope(value, cosine, signed_sine):
    return value * cosine + pltpu.roll(value, HEAD // 2, 1) * signed_sine


def rope_back(grad, cosine, signed_sine):
    return grad * cosine - pltpu.roll(grad, HEAD // 2, 1) * signed_sine


def project(r, hidden, kv, c):
    hat, _ = norm_parts(hidden)
    low = (hat * r.attn_gain[...].astype(F32)).astype(BF)
    r.attn_low[...] = low
    q_raw = dot(low, r.w_q[...])
    k_raw = dot(low, r.w_k[...])
    values = dot(low, r.w_v[...])
    r.q_raw[...] = q_raw
    r.k_raw[...] = k_raw
    cosine, sine = r.cosine[...], r.sine[...]

    def turned(raw, gain):
        return jnp.concatenate(
            [rope(norm_parts(u)[0] * gain, cosine, sine).astype(BF) for u in heads_of(raw)], 1)

    r.queries[...] = turned(q_raw, r.q_gain[...].astype(F32))
    kv.held[kv.at(c), :] = jnp.concatenate([turned(k_raw, r.k_gain[...].astype(F32)), values.astype(BF)], 1)
    kv.send(c)


def project_outs(rows, width, w, reach, when):
    q_width, k_width = w.w_q.shape[2], w.w_k.shape[2]
    return dict(
        attn_low=((rows, width), BF, when),
        q_raw=((rows, q_width), F32, when),
        k_raw=((rows, k_width), F32, when),
        queries=((rows, q_width), BF, when),
        window=((reach + 1, rows, k_width + w.w_v.shape[2]), BF, HBM),
    )


def project_ins(w, layer, tables, when, late):
    def weight(array):
        return (array, Late(layer)) if late else of_layer(array, layer)

    return dict(
        attn_gain=of_layer(w.attn_gain, layer),
        w_q=weight(w.w_q),
        w_k=weight(w.w_k),
        w_v=weight(w.w_v),
        q_gain=of_layer(w.q_gain, layer),
        k_gain=of_layer(w.k_gain, layer),
        cosine=(tables[0], when),
        sine=(tables[1], when),
    )


def mlp_gates(r, low):
    gate = dot(low, r.w_gate[...])
    up = dot(low, r.w_up[...])
    sigma = jax.nn.sigmoid(gate)
    return gate, up, sigma


def mlp_back(r, g_low, gate, up, sigma):
    d_act = dot(g_low, r.w_down[...], NT)
    d_gate = (d_act * up * sigma * (1.0 + gate * (1.0 - sigma))).astype(BF)
    d_up = (d_act * gate * sigma).astype(BF)
    return d_gate, d_up, dot(d_gate, r.w_gate[...], NT) + dot(d_up, r.w_up[...], NT)


def first_projection(hidden, w, tables, reach, chunks, collective_id):
    rows, width = hidden.shape
    when = (1, 0, chunks)
    kv_width = w.w_k.shape[2] + w.w_v.shape[2]

    def body(r, s):
        kv = KeyValueSend(r, reach)

        @pl.when(s == 0)
        def _():
            enter(kv.neighbours())

        project(r, r.hidden[...].astype(F32), kv, s)

        @pl.when(s == chunks - 1)
        def _():
            kv.finish()

    return step_kernel(
        first_projection, body, chunks,
        dict(hidden=(hidden, when)) | project_ins(w, 0, tables, when, False),
        project_outs(rows, width, w, reach, when),
        dict(kv=KeyValueSend.scratch(rows, kv_width, chunks, reach)), collective_id)


def between_forward(context, hidden, w, layer, tables, reach, chunks, collective_id):
    rows, width = hidden.shape
    kv_width = w.w_k.shape[2] + w.w_v.shape[2]
    ff = w.w_gate.shape[2]
    pieces = chunks * PIECES
    first, second, third = (PIECES, 0, chunks), (PIECES, 4, chunks), (PIECES, 8, chunks)
    steps = PIECES * (chunks - 1) + third[1] + 1
    chunk = rows // chunks

    def body(r, s):
        kv = KeyValueSend(r, reach)
        attn, mlp = LineSum(r.attn), LineSum(r.mlp)

        @pl.when(s == 0)
        def _():
            enter(attn.neighbours() + kv.neighbours())

        def send_attn(c):
            attn.put(c, dot(r.context[...], r.w_o[...]))

        def feed_forward(c):
            middle = r.hidden[...].astype(F32) + attn.total(c, chunk)
            r.hidden_mid[...] = middle
            r.mid_held[attn.at(c, chunk), :] = middle
            hat, _ = norm_parts(middle)
            low = (hat * r.mlp_gain[...].astype(F32)).astype(BF)
            r.mlp_low[...] = low
            gate, up, sigma = mlp_gates(r, low)
            r.gate[...] = gate
            r.up[...] = up
            act = (gate * sigma * up).astype(BF)
            r.act[...] = act
            mlp.put(c, dot(act, r.w_down[...]))

        def next_layer(c):
            hidden_next = r.mid_held[mlp.at(c, chunk), :] + mlp.total(c, chunk)
            r.hidden_next[...] = hidden_next
            project(r, hidden_next, kv, c)

        at_chunk(s, first, send_attn)
        at_chunk(s, (1, 1, pieces), attn.relay)
        at_chunk(s, (1, 2, pieces), attn.meet)
        r.arrived(second[1], *MLP_WEIGHTS)
        at_chunk(s, second, feed_forward)
        at_chunk(s, (1, 6, pieces), mlp.relay)
        at_chunk(s, (1, 7, pieces), mlp.meet)
        r.arrived(third[1], *QKV_WEIGHTS)
        at_chunk(s, third, next_layer)

        @pl.when(s == steps - 1)
        def _():
            attn.finish()
            mlp.finish()
            kv.finish()

    return step_kernel(
        between_forward, body, steps,
        dict(
            context=(context, first),
            w_o=of_layer(w.w_o, layer),
            hidden=(hidden, second),
            mlp_gain=of_layer(w.mlp_gain, layer),
            w_gate=(w.w_gate, Late(layer)),
            w_up=(w.w_up, Late(layer)),
            w_down=(w.w_down, Late(layer)),
        )
        | project_ins(w, layer + 1, tables, third, True),
        dict(
            hidden_mid=((rows, width), F32, second),
            mlp_low=((rows, width), BF, second),
            gate=((rows, ff), F32, second),
            up=((rows, ff), F32, second),
            act=((rows, ff), BF, second),
            hidden_next=((rows, width), F32, third),
        )
        | project_outs(rows, width, w, reach, third),
        dict(
            attn=LineSum.scratch(rows, width, pieces),
            mlp=LineSum.scratch(rows, width, pieces),
            kv=KeyValueSend.scratch(rows, kv_width, chunks, reach),
            mid_held=pltpu.VMEM((rows, width), F32),
        ),
        collective_id)


def turn_around(context, hidden, cotangent, w, layer, chunks, collective_id):
    rows, width = hidden.shape
    ff = w.w_gate.shape[2]
    pieces = chunks * PIECES
    first, second, third = (PIECES, 0, chunks), (PIECES, 6, chunks), (PIECES, 12, chunks)
    steps = PIECES * (chunks - 1) + third[1] + 1
    chunk = rows // chunks

    def body(r, s):
        attn, back = LineSum(r.attn), LineSum(r.back)

        @pl.when(s == 0)
        def _():
            enter(attn.neighbours())
            r.gain_grad[...] = jnp.zeros_like(r.gain_grad)

        def send_attn(c):
            attn.put(c, dot(r.context[...], r.w_o[...]))

        def feed_forward(c):
            middle = r.hidden[...] + attn.total(c, chunk)
            r.hidden_mid[...] = middle
            r.mid_held[attn.at(c, chunk), :] = middle
            hat, _ = norm_parts(middle)
            low = (hat * r.mlp_gain[...].astype(F32)).astype(BF)
            r.mlp_low[...] = low
            gate, up, sigma = mlp_gates(r, low)
            d_gate, d_up, part = mlp_back(r, r.cotangent[...], gate, up, sigma)
            back.put(c, part)
            r.d_gate[...] = d_gate
            r.d_up[...] = d_up
            act = (gate * sigma * up).astype(BF)
            r.act[...] = act
            r.mlp_part[...] = dot(act, r.w_down[...]).astype(BF)

        def middle_grad(c):
            hat, inverse = norm_parts(r.mid_held[back.at(c, chunk), :])
            d_in = back.total(c, chunk)
            r.gain_grad[0:1, :] += row_sums(d_in * hat)
            g_mid = r.cotangent_late[...].astype(F32) + norm_back(d_in, r.mlp_gain[...].astype(F32), hat, inverse)
            r.g_mid[...] = g_mid
            mid_low = g_mid.astype(BF)
            r.mid_low[...] = mid_low
            r.d_context[...] = dot(mid_low, r.w_o[...], NT).astype(BF)

        at_chunk(s, first, send_attn)
        at_chunk(s, (1, 3, pieces), attn.relay)
        at_chunk(s, (1, 4, pieces), attn.meet)
        r.arrived(second[1], *MLP_WEIGHTS)
        at_chunk(s, second, feed_forward)
        at_chunk(s, (1, 9, pieces), back.relay)
        at_chunk(s, (1, 10, pieces), back.meet)
        at_chunk(s, third, middle_grad)

        @pl.when(s == steps - 1)
        def _():
            attn.finish()
            back.finish()

    return step_kernel(
        turn_around, body, steps,
        dict(
            context=(context, first),
            w_o=of_layer(w.w_o, layer),
            hidden=(hidden, second),
            cotangent=(cotangent, second),
            cotangent_late=(cotangent, third),
            mlp_gain=of_layer(w.mlp_gain, layer),
            w_gate=(w.w_gate, Late(layer)),
            w_up=(w.w_up, Late(layer)),
            w_down=(w.w_down, Late(layer)),
        ),
        dict(
            mlp_low=((rows, width), BF, second),
            act=((rows, ff), BF, second),
            hidden_mid=((rows, width), F32, second),
            mlp_part=((rows, width), BF, second),
            d_gate=((rows, ff), BF, second),
            d_up=((rows, ff), BF, second),
            g_mid=((rows, width), F32, third),
            mid_low=((rows, width), BF, third),
            d_context=(context.shape, BF, third),
            gain_grad=((8, width), F32, WHOLE),
        ),
        dict(
            attn=LineSum.scratch(rows, width, pieces),
            back=LineSum.scratch(rows, width, pieces),
            mid_held=pltpu.VMEM((rows, width), F32),
        ),
        collective_id)


def attention_grads(r, back, line, c):
    cosine, sine = r.cosine[...], r.sine[...]
    both = back.add(r.d_own[...], c)

    def raw_back(grads, raws, gain):
        lows, gains = [], 0.0
        for grad, raw in zip(heads_of(grads), heads_of(raws)):
            grad = rope_back(grad, cosine, sine)
            hat, inverse = norm_parts(raw)
            gains = gains + row_sums(grad * hat)
            lows.append(norm_back(grad, gain, hat, inverse).astype(BF))
        return jnp.concatenate(lows, 1), gains

    d_q, q_gain = raw_back(r.d_q[...], r.q_raw[...], r.q_gain[...].astype(F32))
    d_k, k_gain = raw_back(both[0], r.k_raw[...], r.k_gain[...].astype(F32))
    d_v = both[1].astype(BF)
    r.head_gain[0:1, 0:HEAD] += q_gain
    r.head_gain[0:1, HEAD : 2 * HEAD] += k_gain
    r.d_held[line.at(c, d_q.shape[0]), :] = jnp.concatenate([d_q, d_k, d_v], 1)
    part = dot(d_q, r.w_q[...], NT) + dot(d_k, r.w_k[...], NT) + dot(d_v, r.w_v[...], NT)
    line.put(c, part)
    return part


class WeightGrads:
    def __init__(self, r, plan):
        self.r = r
        self.plan = plan
        self.slabs = plan.slabs[2]
        self.late = Scatter(r.sc_q, False), Scatter(r.sc_kv, True)
        self.early = Scatter(r.sc_a, False), Scatter(r.sc_b, True)
        self.blocks = 1 << len(block_axes())

    @staticmethod
    def scratch(rows, width, q_width, k_width, ff):
        per = width // (1 << len(block_axes()))
        return dict(
            sc_a=Scatter.scratch(per, ff + q_width),
            sc_b=Scatter.scratch(per, 2 * ff),
            sc_q=Scatter.scratch(per, q_width),
            sc_kv=Scatter.scratch(per, 2 * k_width),
            d_held=pltpu.VMEM((rows, q_width + 2 * k_width), BF),
        )

    def neighbours(self):
        return self.late[0].neighbours()

    def put(self, scatter, slab, columns, value):
        per = self.blocks // self.slabs
        rows = value.shape[0] // per
        for j in range(per):
            scatter.put(slab * per + j, columns, value[j * rows : (j + 1) * rows])

    def mlp_slab(self, slab):
        r = self.r
        ff = r.d_gate_all.shape[1]
        q_width = r.context_all.shape[1]
        mlp_low = r.mlp_low_slab[...]
        self.put(self.early[0], slab, slice(0, ff), dot(mlp_low, r.d_gate_all[...], TN))
        self.put(self.early[0], slab, slice(ff, ff + q_width), dot(r.mid_low_slab[...], r.context_all[...], TN))
        self.put(self.early[1], slab, slice(0, ff), dot(mlp_low, r.d_up_all[...], TN))
        self.put(self.early[1], slab, slice(ff, 2 * ff), dot(r.g_low_slab[...], r.act_all[...], TN))

    def qkv_slabs(self, begin, end):
        r = self.r
        slab_width = r.attn_low_all.shape[1] // self.slabs
        q_width = r.d_q.shape[1]

        @pl.loop(begin, end)
        def _(slab):
            columns = pl.ds(pl.multiple_of(slab * slab_width, slab_width), slab_width)
            value = dot(r.attn_low_all[:, columns], r.d_held[...], TN)
            self.put(self.late[0], slab, slice(None), value[:, :q_width])
            self.put(self.late[1], slab, slice(None), value[:, q_width:])

    def each(self, scatters, work):
        for scatter in scatters:
            work(scatter)

    def store(self):
        r = self.r
        last = len(block_axes()) - 1
        ff = r.d_gate_all.shape[1]
        k_width = r.k_raw.shape[1]

        def store_a(total):
            r.grad_gate[...] = total[:, :ff]
            r.grad_o[...] = total[:, ff:]

        def store_b(total):
            r.grad_up[...] = total[:, :ff]
            r.grad_down[...] = total[:, ff:]

        def store_q(total):
            r.grad_q[...] = total

        def store_kv(total):
            r.grad_k[...] = total[:, :k_width]
            r.grad_v[...] = total[:, k_width:]

        self.early[0].fold(last, store_a)
        self.early[1].fold(last, store_b)
        self.late[0].fold(last, store_q)
        self.late[1].fold(last, store_kv)

    def late_slabs(self, s):
        for i in range(2):
            self.r.arrived(self.plan.late_slabs[0], "attn_low_all") if i == 0 else None

            @pl.when(s == self.plan.late_slabs[i])
            def _():
                self.qkv_slabs(i * self.slabs // 2, (i + 1) * self.slabs // 2)

        @pl.when(s == self.plan.late_slabs[1])
        def _():
            self.each(self.late, lambda scatter: scatter.send(0))

    def run(self, s):
        rate, lag, count = self.plan.slabs
        self.r.arrived(lag, *GRAD_OPERANDS)
        at_chunk(s, self.plan.slabs, self.mlp_slab)

        @pl.when(s == lag + rate * (count - 1))
        def _():
            self.each(self.early, lambda scatter: scatter.send(0))

        for k in range(len(block_axes()) - 1):

            def move(scatter):
                scatter.fold(k)
                scatter.send(k + 1)

            @pl.when(s == self.plan.early(k))
            def _():
                self.each(self.early, move)

            @pl.when(s == self.plan.late(k))
            def _():
                self.each(self.late, move)

    def finish(self):
        self.each(self.early + self.late, lambda scatter: scatter.finish())


def slab_count(chunks):
    return min(4, max(1, chunks // 2))


def grads_ins(a, rows, width, when):
    slab = pl.BlockSpec((rows, width // when[2]), lambda s: (0, chunk_index(when, s)))
    return dict(
        mlp_low_slab=(a.mlp_low, slab),
        mid_low_slab=(a.mid_low, slab),
        g_low_slab=(a.g_low, slab),
        attn_low_all=(a.attn_low, Late()),
        d_gate_all=(a.d_gate, Late()),
        d_up_all=(a.d_up, Late()),
        context_all=(a.context, Late()),
        act_all=(a.act, Late()),
    )


def grads_outs(width, q_width, k_width, ff):
    per = width // (1 << len(block_axes()))
    return dict(
        grad_q=((per, q_width), F32, WHOLE),
        grad_k=((per, k_width), F32, WHOLE),
        grad_v=((per, k_width), F32, WHOLE),
        grad_o=((per, q_width), F32, WHOLE),
        grad_gate=((per, ff), F32, WHOLE),
        grad_up=((per, ff), F32, WHOLE),
        grad_down=((per, ff), F32, WHOLE),
    )


def attention_grads_ins(a, w, layer, tables, when):
    rows, k_width = a.k_raw.shape
    own = pl.BlockSpec((2, rows // when[2], k_width), lambda s: (0, chunk_index(when, s), 0))
    return dict(
        d_q=(a.d_q, when),
        d_own=(a.d_own, own),
        d_prev=(a.d_prev, HBM),
        q_raw=(a.q_raw, when),
        k_raw=(a.k_raw, when),
        cosine=(tables[0], when),
        sine=(tables[1], when),
        w_q=of_layer(w.w_q, layer),
        w_k=of_layer(w.w_k, layer),
        w_v=of_layer(w.w_v, layer),
        q_gain=of_layer(w.q_gain, layer),
        k_gain=of_layer(w.k_gain, layer),
        attn_gain=of_layer(w.attn_gain, layer),
    )


def between_backward(a, below, g_mid, w, layer, tables, reach, chunks, collective_id):
    rows, width = g_mid.shape
    q_width, k_width, ff = w.w_q.shape[2], w.w_k.shape[2], w.w_gate.shape[2]
    pieces = chunks * PIECES
    first, second, third = (PIECES, 0, chunks), (PIECES, 4, chunks), (PIECES, 10, chunks)
    steps = PIECES * (chunks - 1) + third[1] + 1
    chunk = rows // chunks
    after = PIECES * (chunks - 1) + 1
    plan = types.SimpleNamespace(
        slabs=(PIECES, 4, slab_count(chunks)),
        early=lambda k: min(after - 2 + 6 * k, steps - 2),
        late_slabs=(after, after + 2),
        late=lambda k: min(after + 5 + 2 * k, steps - 2),
    )

    def body(r, s):
        back = KeyValueReturn(r, reach)
        attn, mlp = LineSum(r.attn), LineSum(r.mlp)
        grads = WeightGrads(r, plan)

        @pl.when(s == 0)
        def _():
            enter(attn.neighbours() + back.neighbours() + grads.neighbours())
            back.start()
            r.gain_grad[...] = jnp.zeros_like(r.gain_grad)
            r.head_gain[...] = jnp.zeros_like(r.head_gain)

        def send_attn(c):
            attention_grads(r, back, attn, c)

        def feed_forward(c):
            hat, inverse = norm_parts(r.hidden[...])
            d_in = attn.total(c, chunk)
            r.gain_grad[0:1, :] += row_sums(d_in * hat)
            g = r.g_above[...] + norm_back(d_in, r.attn_gain[...].astype(F32), hat, inverse)
            r.g_held[lax.rem(c, 4)] = g
            g_low = g.astype(BF)
            r.g_low[...] = g_low
            gate = r.gate[...]
            d_gate, d_up, part = mlp_back(r, g_low, gate, r.up[...], jax.nn.sigmoid(gate))
            r.d_gate[...] = d_gate
            r.d_up[...] = d_up
            mlp.put(c, part)

        def middle_grad(c):
            hat, inverse = norm_parts(r.hidden_mid[...])
            d_in = mlp.total(c, chunk)
            r.gain_grad[1:2, :] += row_sums(d_in * hat)
            g_mid = r.g_held[lax.rem(c, 4)] + norm_back(d_in, r.mlp_gain[...].astype(F32), hat, inverse)
            r.g_mid[...] = g_mid
            mid_low = g_mid.astype(BF)
            r.mid_low[...] = mid_low
            r.d_context[...] = dot(mid_low, r.w_o[...], NT).astype(BF)

        at_chunk(s, first, send_attn)
        grads.late_slabs(s)
        at_chunk(s, (1, 2, pieces), attn.relay)
        at_chunk(s, (1, 3, pieces), attn.meet)
        r.arrived(second[1], *MLP_WEIGHTS)
        at_chunk(s, second, feed_forward)
        at_chunk(s, (1, 7, pieces), mlp.relay)
        at_chunk(s, (1, 8, pieces), mlp.meet)
        r.arrived(third[1], "w_o")
        at_chunk(s, third, middle_grad)
        grads.run(s)

        @pl.when(s == steps - 1)
        def _():
            grads.store()
            attn.finish()
            mlp.finish()
            back.finish()
            grads.finish()

    return step_kernel(
        between_backward, body, steps,
        attention_grads_ins(a, w, layer, tables, first)
        | grads_ins(a, rows, width, plan.slabs)
        | dict(
            hidden=(a.hidden, second),
            g_above=(g_mid, second),
            gate=(below.gate, second),
            up=(below.up, second),
            hidden_mid=(below.hidden_mid, third),
            mlp_gain=of_layer(w.mlp_gain, layer - 1),
            w_gate=(w.w_gate, Late(layer - 1)),
            w_up=(w.w_up, Late(layer - 1)),
            w_down=(w.w_down, Late(layer - 1)),
            w_o=(w.w_o, Late(layer - 1)),
        ),
        dict(
            g_low=((rows, width), BF, second),
            d_gate=((rows, ff), BF, second),
            d_up=((rows, ff), BF, second),
            g_mid=((rows, width), F32, third),
            mid_low=((rows, width), BF, third),
            d_context=((rows, q_width), BF, third),
            gain_grad=((8, width), F32, WHOLE),
            head_gain=((8, 2 * HEAD), F32, WHOLE),
        )
        | grads_outs(width, q_width, k_width, ff),
        dict(
            attn=LineSum.scratch(rows, width, pieces),
            mlp=LineSum.scratch(rows, width, pieces),
            kr=KeyValueReturn.scratch(rows, k_width, chunks, reach),
            **WeightGrads.scratch(rows, width, q_width, k_width, ff),
            g_held=pltpu.VMEM((4, rows // chunks, width), F32),
        ),
        collective_id)


def last_backward(a, top, top_total, g_mid, gain_parts, w, tables, reach, chunks, collective_id):
    rows, width = g_mid.shape
    q_width, k_width, ff = w.w_q.shape[2], w.w_k.shape[2], w.w_gate.shape[2]
    layer = 0
    pieces = chunks * PIECES
    pairs = max(1, chunks // 2)
    half = rows // 2
    half_pieces = pieces // 2
    first, second, third = (PIECES, 0, pairs), (PIECES, 8, chunks), (PIECES, 5, chunks)
    steps = PIECES * (chunks - 1) + second[1] + 1
    chunk = rows // chunks
    after = PIECES * pairs
    plan = types.SimpleNamespace(
        slabs=(PIECES, 1, slab_count(chunks)),
        early=lambda k: min(after + 1 + 4 * k, steps - 2),
        late_slabs=(after, after + 1),
        late=lambda k: min(after + 5 + 5 * k, steps - 2),
    )

    def body(r, s):
        back = KeyValueReturn(r, reach)
        attn, upper, lower = LineSum(r.attn), LineSum(r.upper, r.upper_part), Spread(r.lower, r.lower_total)
        grads = WeightGrads(r, plan)
        sums = Butterfly(r.sums)

        @pl.when(s == 0)
        def _():
            enter(attn.neighbours() + back.neighbours() + sums.neighbours())
            back.start()
            lower.start()
            r.head_gain[...] = jnp.zeros_like(r.head_gain)
            r.gain_held[...] = jnp.zeros_like(r.gain_held)

        def send_attn(c):
            part = attention_grads(r, back, attn, c)
            hat, _ = norm_parts(r.hidden[...].astype(F32))
            r.gain_held[...] += row_sums(part * hat)

        def give_output(c):
            @pl.when(c < chunks // 2)
            def _():
                r.output[...] = (r.hidden_mid[...] + lower.total(c, chunk)).astype(BF)

            @pl.when(c >= chunks // 2)
            def _():
                r.output[...] = (r.hidden_mid[...] + upper.total(c - chunks // 2, chunk)).astype(BF)

        def push_upper(j):
            upper.push(j, 2 * upper.rows)

        def give_input(c):
            hat, inverse = norm_parts(r.hidden_late[...].astype(F32))
            r.input_grad[...] = r.g_above[...] + norm_back(attn.total(c, chunk), r.attn_gain[...].astype(F32), hat, inverse)

        at_chunk(s, (1, 0, half_pieces // 2), push_upper)
        at_chunk(s, first, send_attn)
        grads.late_slabs(s)
        at_chunk(s, (1, 3, half_pieces), upper.relay)
        at_chunk(s, (1, 3, pieces), attn.relay)
        at_chunk(s, (1, 5, half_pieces), upper.meet)
        at_chunk(s, (1, 5, pieces), attn.meet)
        at_chunk(s, third, give_output)
        at_chunk(s, second, give_input)
        grads.run(s)

        @pl.when(s == after)
        def _():
            row = lax.broadcasted_iota(jnp.int32, (8, width), 0)
            pad = jnp.zeros((1, width - 2 * HEAD), F32)
            heads = jnp.concatenate([r.head_gain[0:1, :], pad], 1)
            packet = r.gain_parts[...] + jnp.where(row == 0, r.gain_held[...], 0.0) + jnp.where(row == 4, heads, 0.0)
            sums.put(packet)

        for k in range(len(sums.axes)):

            @pl.when(s == min(after + 2 + 2 * k, steps - 1))
            def _():
                sums.fold(k)

        @pl.when(s == steps - 1)
        def _():
            grads.store()
            r.gains[...] = sums.total()
            attn.finish()
            upper.finish()
            lower.finish()
            back.finish()
            grads.finish()
            sums.finish()

    return step_kernel(
        last_backward, body, steps,
        attention_grads_ins(a, w, layer, tables, first)
        | grads_ins(a, rows, width, plan.slabs)
        | dict(
            hidden=(a.hidden, first),
            hidden_late=(a.hidden, second),
            g_above=(g_mid, second),
            gain_parts=(gain_parts, WHOLE),
            upper_part=(top.mlp_part, pl.BlockSpec((half, width), lambda s: (1, 0), pipeline_mode=pl.Buffered(1))),
            lower_total=(top_total, WHOLE),
            hidden_mid=(top.hidden_mid, third),
        ),
        dict(
            input_grad=((rows, width), F32, second),
            output=((rows, width), BF, third),
            gains=((8, width), F32, WHOLE),
        )
        | grads_outs(width, q_width, k_width, ff),
        dict(
            attn=LineSum.scratch(rows, width, pieces),
            upper=Spread.scratch(half, width, half_pieces),
            lower=Spread.scratch(half, width, half_pieces),
            kr=KeyValueReturn.scratch(rows, k_width, pairs, reach),
            **WeightGrads.scratch(rows, width, q_width, k_width, ff),
            sums=Butterfly.scratch((8, width)),
            head_gain=pltpu.VMEM((8, 2 * HEAD), F32),
            gain_held=pltpu.VMEM((1, width), F32),
        ),
        collective_id)


def shifted(array, axis, by):
    devices = lax.axis_size(axis)
    pairs = [(i, i + by) for i in range(devices) if 0 <= i + by < devices]
    return lax.ppermute(array, axis, pairs)


def middle_sum(part):
    n = lax.axis_size("tensor")
    half = n // 2
    total = part
    for hop in range(half - 1):
        moved = lax.ppermute(total, "tensor", [(hop, hop + 1), (n - 1 - hop, n - 2 - hop)])
        total = (part.astype(F32) + moved.astype(F32)).astype(BF)
    if n > 1:
        moved = lax.ppermute(total, "tensor", [(half - 1, half), (half, half - 1)])
        total = (total.astype(F32) + moved.astype(F32)).astype(BF)
    return total


def rope_tables(places):
    halves = HEAD // 2
    frequency = THETA ** (-(jnp.arange(halves, dtype=F32) * 2.0) / HEAD)
    angle = places.astype(F32)[:, None] * frequency
    cosine, sine = jnp.cos(angle), jnp.sin(angle)
    return jnp.concatenate([cosine, cosine], -1), jnp.concatenate([-sine, sine], -1)


def lowest_keys(segments, reach):
    seqs_here, stretch = segments.shape
    place = lax.axis_index("seq")
    docs = [segments]
    for back in range(1, reach + 1):
        docs.insert(0, jnp.where(place >= back, shifted(segments, "seq", back), -1))
    docs = jnp.concatenate(docs, 1)
    start = jnp.sum((docs < 0).astype(jnp.int32), 1, keepdims=True)
    low = jnp.broadcast_to(start, segments.shape)
    for d in range(1, 4):
        start = jnp.sum((docs < d).astype(jnp.int32), 1, keepdims=True)
        low = jnp.where(segments >= d, start, low)
    index = jnp.arange(stretch, dtype=jnp.int32)
    return jnp.maximum(low, reach * stretch + index - (WINDOW - 1)).reshape(-1)


def per_device(
    tokens, cotangent, segments, positions, attn_gain, w_query, key_projection, value_projection, query_gain, key_gain,
    w_output, mlp_gain, w_gate, w_up, w_down,
):
    seqs_here, stretch, width = tokens.shape
    rows = seqs_here * stretch
    reach = min(lax.axis_size("seq") - 1, (WINDOW + stretch - 2) // stretch)
    chunks = rows // min(CHUNK, stretch)

    w = types.SimpleNamespace(
        attn_gain=attn_gain[:, None], mlp_gain=mlp_gain[:, None], q_gain=query_gain[:, None], k_gain=key_gain[:, None],
        w_q=w_query, w_k=key_projection, w_v=value_projection, w_o=w_output, w_gate=w_gate, w_up=w_up, w_down=w_down,
    )
    tables = rope_tables(positions.reshape(rows))
    low = lowest_keys(segments, reach)
    block = min(512, stretch)
    first = low[::block]
    tokens = tokens.reshape(rows, width)
    cotangent = cotangent.reshape(rows, width)

    a0 = first_projection(tokens, w, tables, reach, chunks, 1)
    a0.hidden = tokens
    a0.context, a0.lse = attn_fwd(a0.queries, a0.window, first, low, stretch, block, block)
    mid = between_forward(a0.context, tokens, w, 0, tables, reach, chunks, 2)
    a1 = types.SimpleNamespace(
        attn_low=mid.attn_low, q_raw=mid.q_raw, k_raw=mid.k_raw, queries=mid.queries, window=mid.window,
        hidden=mid.hidden_next)
    a1.context, a1.lse = attn_fwd(a1.queries, a1.window, first, low, stretch, block, block)
    turn = turn_around(a1.context, a1.hidden, cotangent, w, 1, chunks, 3)
    top_total = middle_sum(turn.mlp_part[: rows // 2])
    a1.mlp_low, a1.act, a1.d_gate, a1.d_up = turn.mlp_low, turn.act, turn.d_gate, turn.d_up
    a1.mid_low, a1.g_low = turn.mid_low, cotangent
    a1.d_q, a1.d_own, a1.d_prev = attn_bwd(
        a1.queries, turn.d_context, a1.context, a1.window, first, low, a1.lse, stretch, block, block)
    down = between_backward(a1, mid, turn.g_mid, w, 1, tables, reach, chunks, 4)
    a0.mlp_low, a0.act, a0.d_gate, a0.d_up = mid.mlp_low, mid.act, down.d_gate, down.d_up
    a0.mid_low, a0.g_low = down.mid_low, down.g_low
    a0.d_q, a0.d_own, a0.d_prev = attn_bwd(
        a0.queries, down.d_context, a0.context, a0.window, first, low, a0.lse, stretch, block, block)

    once = lax.axis_index("tensor") == 0
    shared = jnp.concatenate([
        jnp.zeros((1, width), F32), down.gain_grad[0:1], down.gain_grad[1:2], turn.gain_grad[0:1],
        jnp.zeros((4, width), F32)], 0)
    heads = jnp.pad(down.head_gain[0:1], ((4, 3), (2 * HEAD, width - 4 * HEAD)))
    gain_parts = jnp.where(once, shared, 0.0) + heads
    end = last_backward(a0, turn, top_total, down.g_mid, gain_parts, w, tables, reach, chunks, 5)
    gains = end.gains

    def both(pick, turned=False):
        lower, upper = pick(end), pick(down)
        return jnp.stack([lower.T, upper.T] if turned else [lower, upper])

    head_rows = gains[4, : 4 * HEAD].reshape(2, 2, HEAD)
    shape = (seqs_here, stretch, width)
    return (
        end.output.reshape(shape), end.input_grad.reshape(shape), gains[0:2], both(lambda k: k.grad_q), both(lambda k: k.grad_k),
        both(lambda k: k.grad_v), head_rows[:, 0], head_rows[:, 1], both(lambda k: k.grad_o, True), gains[2:4], both(lambda k: k.grad_gate),
        both(lambda k: k.grad_up), both(lambda k: k.grad_down, True),
    )


def solution(mesh):
    placed = (
        P("dp", "seq", None), P("dp", "seq", None), P("dp", "seq"), P("dp", "seq"), P(), P(None, None, "tensor"),
        P(None, None, "tensor"), P(None, None, "tensor"), P(), P(), P(None, "tensor", None), P(),
        P(None, None, "tensor"), P(None, None, "tensor"), P(None, "tensor", None),
    )
    by_rows = P(None, ("dp", "seq"), "tensor")
    by_columns = P(None, "tensor", ("dp", "seq"))
    return jax.shard_map(
        per_device,
        mesh=mesh,
        in_specs=placed,
        out_specs=(
            P("dp", "seq", None), P("dp", "seq", None), P(), by_rows, by_rows, by_rows, P(), P(), by_columns, P(),
            by_rows, by_rows, by_columns,
        ),
        check_vma=False,
    )
```

```python
import functools
import types

import jax
import jax.numpy as jnp
from jax import lax
from jax.experimental import pallas as pl
from jax.experimental.pallas import tpu as pltpu
from jax.sharding import PartitionSpec as P

HEAD = 128
LAYER_COUNT = 2
WINDOW = 1024
EPS = 1e-06
THETA = 1000000.0
LOG2E = 1.4426950408889634
SCALE = HEAD ** (-0.5)
CHUNK = 128
PIECES = 2
MESH = pl.DeviceIdType.MESH
BF = jnp.bfloat16
F32 = jnp.float32

NT = (((1,), (1,)), ((), ()))
NN = (((1,), (0,)), ((), ()))
TN = (((0,), (0,)), ((), ()))


def dot(a, b, dims=NN):
    return lax.dot_general(a, b, dims, preferred_element_type=F32)


def attn_bwd_kernel(offset, low_ref, lse_ref, q_ref, do_ref, o_ref, k_ref, v_ref, dq_ref, own_ref, prev_ref,
                    dk_ref, dv_ref):
    step = pl.program_id(2)
    qb = q_ref.shape[0]
    heads = q_ref.shape[1] // HEAD
    span = k_ref.shape[0]
    length = min(WINDOW + qb, span)
    q_start = step * qb + offset
    start = jnp.clip(q_start + qb - length, 0, span - length)
    here = pl.ds(pl.multiple_of(start, HEAD), length)

    @pl.when(step == 0)
    def _():
        dk_ref[...] = jnp.zeros_like(dk_ref)
        dv_ref[...] = jnp.zeros_like(dv_ref)

    def stack(ref):
        return jnp.concatenate([ref[:, h * HEAD : (h + 1) * HEAD] for h in range(heads)], 0)

    queries = stack(q_ref)
    d_out = stack(do_ref)
    lse = jnp.concatenate([lse_ref[h : h + 1, :] for h in range(heads)], 1)
    product = d_out.astype(F32) * stack(o_ref).astype(F32)
    delta = jnp.sum(product.T, 0, keepdims=True)
    keys = k_ref[here, :]
    values = v_ref[here, :]
    key_index = start + lax.broadcasted_iota(jnp.int32, (length, qb), 0)
    q_index = q_start + lax.broadcasted_iota(jnp.int32, (1, qb), 1)
    mask = (key_index >= low_ref[...]) & (key_index <= q_index)
    mask = jnp.concatenate([mask] * heads, 1)
    s = dot(keys, queries, NT) * (SCALE * LOG2E) - lse
    p = jnp.where(mask, jnp.exp2(s), 0.0)
    ds = (p * (dot(values, d_out, NT) - delta)).astype(BF)
    dv_ref[here, :] += dot(p.astype(BF), d_out)
    dk_ref[here, :] += dot(ds, queries)
    dq = dot(ds, keys, TN) * SCALE
    for h in range(heads):
        dq_ref[:, h * HEAD : (h + 1) * HEAD] = dq[h * qb : (h + 1) * qb]

    @pl.when(step == pl.num_programs(2) - 1)
    def _():
        own_ref[0] = dk_ref[offset:, :] * SCALE
        own_ref[1] = dv_ref[offset:, :]
        stretch = own_ref.shape[1]
        for j in range(offset // stretch):
            prev_ref[j, 0] = (dk_ref[j * stretch : (j + 1) * stretch, :] * SCALE).astype(BF)
            prev_ref[j, 1] = dv_ref[j * stretch : (j + 1) * stretch, :].astype(BF)


def attn_bwd(q, d_out, o, window, low, lse, stretch):
    rows = q.shape[0]
    kv_heads = window.shape[1] // (2 * HEAD)
    width = q.shape[1] // kv_heads
    group = width // HEAD
    qb = min(2 * CHUNK, stretch)
    steps = stretch // qb
    span = window.shape[0] // (rows // stretch)
    reach = span // stretch - 1
    held = max(reach, 1)
    row_spec = pl.BlockSpec((qb, width), lambda s, g, i: (s * steps + i, g))
    return pl.pallas_call(
        functools.partial(attn_bwd_kernel, reach * stretch),
        grid=(rows // stretch, kv_heads, steps),
        in_specs=[
            pl.BlockSpec((1, qb), lambda s, g, i: (0, s * steps + i)),
            pl.BlockSpec((None, group, qb), lambda s, g, i: (g, 0, s * steps + i)),
            row_spec,
            row_spec,
            row_spec,
            pl.BlockSpec((span, HEAD), lambda s, g, i: (s, g)),
            pl.BlockSpec((span, HEAD), lambda s, g, i: (s, kv_heads + g)),
        ],
        out_specs=[
            row_spec,
            pl.BlockSpec((2, stretch, HEAD), lambda s, g, i: (0, s, g)),
            pl.BlockSpec((held, 2, stretch, HEAD), lambda s, g, i: (0, 0, s, g)),
        ],
        out_shape=[
            jax.ShapeDtypeStruct(q.shape, F32),
            jax.ShapeDtypeStruct((2, rows, kv_heads * HEAD), F32),
            jax.ShapeDtypeStruct((held, 2, rows, kv_heads * HEAD), BF),
        ],
        scratch_shapes=[pltpu.VMEM((span, HEAD), F32), pltpu.VMEM((span, HEAD), F32)],
        name=attn_bwd.__name__,
        cost_estimate=pl.CostEstimate(flops=3 * 10**10, bytes_accessed=12 * 2**20, transcendentals=4 * 2**20),
        compiler_params=pltpu.CompilerParams(vmem_limit_bytes=62 << 20),
    )(low, lse, q, d_out, o, window, window)


def chunk_index(schedule, s):
    rate, lag, count = schedule
    return jnp.clip((s - lag) // rate, 0, count - 1)


def rows_spec(schedule, shape):
    return pl.BlockSpec((shape[0] // schedule[2], shape[1]), lambda s: (chunk_index(schedule, s), 0))


WHOLE, HBM = object(), object()
MLP_WEIGHTS = ("w_gate", "w_up", "w_down")
QKV_WEIGHTS = ("w_q", "w_k", "w_v")
GRAD_OPERANDS = ("d_gate_all", "d_up_all", "context_all", "act_all")


def of_layer(array, layer):
    shape = array.shape[1:]
    zeros = (0,) * len(shape)
    return array, pl.BlockSpec((None,) + shape, lambda s: (layer,) + zeros, pipeline_mode=pl.Buffered(1))


class Row:
    def __init__(self, layer):
        self.layer = layer


class Late:
    def __init__(self, layer=None):
        self.layer = layer

    def shape(self, array):
        return array.shape if self.layer is None else array.shape[1:]

    def copy(self, source, held, sem):
        return pltpu.make_async_copy(source if self.layer is None else source.at[self.layer], held, sem)


def step_kernel(owner, body, steps, ins, outs, scratch, collective_id, vmem=62):
    def spec(shape, where, is_in):
        if isinstance(where, pl.BlockSpec):
            return where
        if where is HBM or isinstance(where, Late):
            return pl.BlockSpec(memory_space=pl.ANY)
        if where is WHOLE or isinstance(where, Row):
            zeros = (0,) * len(shape)
            if is_in:
                return pl.BlockSpec(shape, lambda s: zeros, pipeline_mode=pl.Buffered(1))
            return pl.BlockSpec(memory_space=pltpu.VMEM)
        return rows_spec(where, shape)

    late = {name: where for name, (_, where) in ins.items() if isinstance(where, Late)}
    held = {name: pltpu.VMEM(where.shape(ins[name][0]), ins[name][0].dtype) for name, where in late.items()}
    flat, tree = jax.tree.flatten((scratch, held, {name: pltpu.SemaphoreType.DMA(()) for name in late}))

    def kernel(*refs):
        named = dict(zip(ins, refs))
        named.update(zip(outs, refs[len(ins) :]))
        own, held_refs, sems = jax.tree.unflatten(tree, refs[len(ins) + len(outs) :])
        copies = {name: where.copy(named[name], held_refs[name], sems[name]) for name, where in late.items()}
        for name, ref in own.items():
            named[name] = types.SimpleNamespace(**ref) if isinstance(ref, dict) else ref
        named.update(held_refs)
        for name, (_, where) in ins.items():
            if isinstance(where, Row):
                named[name] = named[name].at[where.layer : where.layer + 1]
        s = pl.program_id(0)

        @pl.when(s == 0)
        def _():
            for copy in copies.values():
                copy.start()

        def arrived(step, *names):
            @pl.when(s == step)
            def _():
                for name in names:
                    copies[name].wait()

        body(types.SimpleNamespace(arrived=arrived, **named), s)

    results = pl.pallas_call(
        kernel,
        grid=(steps,),
        in_specs=[spec(a.shape, w, True) for a, w in ins.values()],
        out_specs=[spec(shape, w, False) for shape, _, w in outs.values()],
        out_shape=[jax.ShapeDtypeStruct(shape, dtype) for shape, dtype, _ in outs.values()],
        scratch_shapes=flat,
        name=owner.__name__,
        compiler_params=pltpu.CompilerParams(
            collective_id=collective_id, has_side_effects=True, vmem_limit_bytes=vmem << 20
        ),
    )(*[a for a, _ in ins.values()])
    return types.SimpleNamespace(**dict(zip(outs, results)))


def at_chunk(s, schedule, work):
    rate, lag, count = schedule
    moved = s - lag
    here = (moved >= 0) & (moved < rate * count)
    if rate > 1:
        here = here & (lax.rem(moved, rate) == 0)

    @pl.when(here)
    def _():
        work(moved // rate if rate > 1 else moved)


def enter(devices):
    barrier = pltpu.get_barrier_semaphore()
    count = 0
    for device, exists in devices:
        if exists is True:
            pl.semaphore_signal(barrier, inc=1, device_id=device, device_id_type=MESH)
            count = count + 1
        else:

            @pl.when(exists)
            def _():
                pl.semaphore_signal(barrier, inc=1, device_id=device, device_id_type=MESH)

            count = count + jnp.where(exists, 1, 0)
    pl.semaphore_wait(barrier, count)


class LineSum:
    def __init__(self, refs, x=None):
        self.x, self.land = refs.x if x is None else x, refs.land
        self.send_sem, self.land_sem, self.out_sem = refs.send, refs.arrive, refs.out
        self.pieces = self.send_sem.shape[0]
        self.rows = self.x.shape[0] // self.pieces
        n = lax.axis_size("tensor")
        z = lax.axis_index("tensor")
        half = n // 2
        self.middle = (z == half - 1) | (z == half)
        self.has_outer = (z > 0) & (z < n - 1)
        self.inner = jnp.where(z < half, z + 1, z - 1)
        self.outer = jnp.clip(jnp.where(z < half, z - 1, z + 1), 0, n - 1)
        self.slot = jnp.where(self.middle, 1, 0)

    @staticmethod
    def scratch(rows, width, pieces):
        return dict(
            x=pltpu.VMEM((rows, width), BF),
            land=pltpu.VMEM((2, rows, width), BF),
            send=pltpu.SemaphoreType.DMA((pieces,)),
            arrive=pltpu.SemaphoreType.DMA((2, pieces)),
            out=pltpu.SemaphoreType.DMA((pieces,)),
        )

    def neighbours(self):
        return [({"tensor": self.inner}, True), ({"tensor": self.outer}, self.has_outer)]

    def at(self, j, rows=None):
        rows = rows or self.rows
        return pl.ds(pl.multiple_of(j * rows, rows), rows)

    def inward(self, source, j, slot):
        return pltpu.make_async_remote_copy(
            source.at[self.at(j)], self.land.at[slot, self.at(j)], self.send_sem.at[j], self.land_sem.at[slot, j],
            device_id={"tensor": self.inner}, device_id_type=MESH)

    def outward(self, j):
        return pltpu.make_async_remote_copy(
            self.land.at[1, self.at(j)], self.land.at[1, self.at(j)], self.out_sem.at[j], self.land_sem.at[1, j],
            device_id={"tensor": self.outer}, device_id_type=MESH)

    def put(self, c, value):
        rows = value.shape[0]
        self.x[self.at(c, rows), :] = value.astype(BF)
        self.push(c, rows)

    def push(self, c, rows):
        @pl.when(jnp.logical_not(self.has_outer))
        def _():
            for i in range(rows // self.rows):
                self.inward(self.x, c * (rows // self.rows) + i, self.slot).start()

    def add(self, j, source, slot):
        self.land[slot, self.at(j), :] = (
            source[self.at(j), :].astype(F32) + self.land[slot, self.at(j), :].astype(F32)
        ).astype(BF)

    def relay(self, j):
        @pl.when(self.has_outer)
        def _():
            self.inward(self.x, j, 0).wait_recv()
            self.add(j, self.x, 0)
            self.inward(self.land.at[0], j, self.slot).start()

    def meet(self, j):
        @pl.when(self.middle)
        def _():
            self.inward(self.x, j, 1).wait_recv()

            @pl.when(self.has_outer)
            def _():
                self.add(j, self.land.at[0], 1)
                self.outward(j).start()

            @pl.when(jnp.logical_not(self.has_outer))
            def _():
                self.add(j, self.x, 1)

    def total(self, c, rows):
        @pl.when(jnp.logical_not(self.middle))
        def _():
            for i in range(rows // self.rows):
                j = c * (rows // self.rows) + i
                self.inward(self.x, j, 1).wait_recv()

                @pl.when(self.has_outer)
                def _():
                    self.outward(j).start()

        return self.land[1, self.at(c, rows), :].astype(F32)

    def finish(self):
        @pl.when(self.has_outer)
        def _():
            @pl.loop(0, self.pieces)
            def _(j):
                self.inward(self.land.at[0], j, self.slot).wait_send()
                self.outward(j).wait_send()

        @pl.when(jnp.logical_not(self.has_outer))
        def _():
            @pl.loop(0, self.pieces)
            def _(j):
                self.inward(self.x, j, self.slot).wait_send()


class Spread(LineSum):
    @staticmethod
    def scratch(rows, width, pieces):
        return dict(
            land=pltpu.VMEM((2, rows, width), BF),
            send=pltpu.SemaphoreType.DMA((pieces,)),
            arrive=pltpu.SemaphoreType.DMA((2, pieces)),
            out=pltpu.SemaphoreType.DMA((pieces,)),
        )

    def start(self, other):
        @pl.when(self.middle)
        def _():
            @pl.loop(0, self.pieces)
            def _(j):
                self.land[1, self.at(j), :] = (
                    self.x[self.at(j), :].astype(F32) + other[self.at(j), :].astype(F32)
                ).astype(BF)

                @pl.when(self.has_outer)
                def _():
                    self.outward(j).start()

    def finish(self):
        @pl.when(self.has_outer)
        def _():
            @pl.loop(0, self.pieces)
            def _(j):
                self.outward(j).wait_send()


class KeyValueSend:
    def __init__(self, refs, reach, stretch):
        self.held, self.zeros, self.window = refs.kv.held, refs.kv.zeros, refs.window
        self.copy_sem, self.send_sem, self.land_sem = refs.kv.copy, refs.kv.send, refs.kv.land
        self.chunks = self.copy_sem.shape[0]
        self.rows = self.held.shape[0] // self.chunks
        self.reach, self.stretch = reach, stretch
        self.place = lax.axis_index("seq")
        self.count = lax.axis_size("seq")

    @staticmethod
    def scratch(rows, width, chunks, reach):
        held = max(reach, 1)
        return dict(
            held=pltpu.VMEM((rows, width), BF),
            zeros=pltpu.VMEM((rows // chunks, width), BF),
            copy=pltpu.SemaphoreType.DMA((chunks,)),
            send=pltpu.SemaphoreType.DMA((held, chunks)),
            land=pltpu.SemaphoreType.DMA((held, chunks)),
        )

    def neighbours(self):
        found = []
        for back in range(1, self.reach + 1):
            found.append(({"seq": jnp.minimum(self.place + back, self.count - 1)}, self.place + back < self.count))
            found.append(({"seq": jnp.maximum(self.place - back, 0)}, self.place >= back))
        return found

    def at(self, c):
        return pl.ds(pl.multiple_of(c * self.rows, self.rows), self.rows)

    def there(self, back, c):
        per = self.stretch // self.rows
        chunk = ((c // per) * (self.reach + 1) + self.reach - back) * per + lax.rem(c, per)
        return self.window.at[self.at(chunk)]

    def own(self, c):
        return pltpu.make_async_copy(self.held.at[self.at(c)], self.there(0, c), self.copy_sem.at[c])

    def blank(self, back, c):
        return pltpu.make_async_copy(self.zeros, self.there(back, c), self.land_sem.at[back - 1, c])

    def remote(self, back, c):
        return pltpu.make_async_remote_copy(
            self.held.at[self.at(c)], self.there(back, c), self.send_sem.at[back - 1, c],
            self.land_sem.at[back - 1, c],
            device_id={"seq": jnp.minimum(self.place + back, self.count - 1)}, device_id_type=MESH)

    def start(self):
        self.zeros[...] = jnp.zeros_like(self.zeros)

    def send(self, c):
        self.own(c).start()
        for back in range(1, self.reach + 1):

            @pl.when(self.place + back < self.count)
            def _():
                self.remote(back, c).start()

            @pl.when(self.place < back)
            def _():
                self.blank(back, c).start()

    def finish(self):
        @pl.loop(0, self.chunks)
        def _(c):
            self.own(c).wait()
            for back in range(1, self.reach + 1):

                @pl.when(self.place + back < self.count)
                def _():
                    self.remote(back, c).wait_send()

                @pl.when(self.place >= back)
                def _():
                    self.remote(back, c).wait_recv()

                @pl.when(self.place < back)
                def _():
                    self.blank(back, c).wait()


class KeyValueReturn:
    def __init__(self, refs, reach):
        self.prev, self.land = refs.d_prev, refs.kr.land
        self.send_sem, self.land_sem = refs.kr.send, refs.kr.arrive
        self.chunks = self.send_sem.shape[1]
        self.rows = self.land.shape[2] // self.chunks
        self.reach = reach
        self.place = lax.axis_index("seq")
        self.count = lax.axis_size("seq")

    @staticmethod
    def scratch(rows, width, chunks, reach):
        held = max(reach, 1)
        return dict(
            land=pltpu.VMEM((held, 2, rows, width), BF),
            send=pltpu.SemaphoreType.DMA((held, chunks)),
            arrive=pltpu.SemaphoreType.DMA((held, chunks)),
        )

    neighbours = KeyValueSend.neighbours
    at = KeyValueSend.at

    def copy(self, back, c):
        return pltpu.make_async_remote_copy(
            self.prev.at[self.reach - back, :, self.at(c)], self.land.at[back - 1, :, self.at(c)],
            self.send_sem.at[back - 1, c], self.land_sem.at[back - 1, c],
            device_id={"seq": jnp.maximum(self.place - back, 0)}, device_id_type=MESH)

    def start(self):
        for back in range(1, self.reach + 1):

            @pl.when(self.place >= back)
            def _():
                @pl.loop(0, self.chunks)
                def _(c):
                    self.copy(back, c).start()

    def add(self, own, c):
        for back in range(1, self.reach + 1):
            exists = self.place + back < self.count

            @pl.when(exists)
            def _():
                self.copy(back, c).wait_recv()

            own = own + jnp.where(exists, self.land[back - 1, :, self.at(c), :].astype(F32), 0.0)
        return own

    def finish(self):
        for back in range(1, self.reach + 1):

            @pl.when(self.place >= back)
            def _():
                @pl.loop(0, self.chunks)
                def _(c):
                    self.copy(back, c).wait_send()


def device_bit(axis):
    name, b = axis
    return lax.rem(lax.axis_index(name) // (1 << b), 2)


def device_partner(axis):
    name, b = axis
    return {name: lax.axis_index(name) + (1 - 2 * device_bit(axis)) * (1 << b)}


def bits_of(name):
    return lax.axis_size(name).bit_length() - 1


def block_axes():
    return [(name, b) for name in ("dp", "seq") for b in reversed(range(bits_of(name)))]


class Scatter:
    def __init__(self, refs, swapped):
        self.axes = block_axes()
        phases = len(self.axes)
        near = [k for k in range(phases) if self.axes[k][0] == "seq"][::-1]
        far = [k for k in range(phases) if self.axes[k][0] == "dp"]
        self.order = near + (far if swapped else far[::-1])
        self.buffer, self.lands = refs.held, refs.lands
        self.send_sem, self.land_sem = refs.send, refs.arrive

    @staticmethod
    def scratch(rows, width):
        phases = len(block_axes())
        return dict(
            held=pltpu.VMEM((2,) * phases + (rows, width), BF),
            lands=[pltpu.VMEM((2,) * (phases - k - 1) + (rows, width), BF) for k in range(phases)],
            send=pltpu.SemaphoreType.DMA((phases,)),
            arrive=pltpu.SemaphoreType.DMA((phases,)),
        )

    def neighbours(self):
        return [(device_partner(axis), True) for axis in self.axes]

    def put(self, block, columns, value):
        phases = len(self.axes)
        place = tuple(lax.rem(block // (1 << (phases - 1 - k)), 2) for k in range(phases))
        self.buffer[place + (slice(None), columns)] = value.astype(BF)

    def view(self, k, mine):
        index = [slice(None)] * len(self.axes)
        for earlier in self.order[:k]:
            index[earlier] = device_bit(self.axes[earlier])
        bit = device_bit(self.axes[self.order[k]])
        index[self.order[k]] = bit if mine else 1 - bit
        return tuple(index)

    def copy(self, k):
        return pltpu.make_async_remote_copy(
            self.buffer.at[self.view(k, False)], self.lands[k], self.send_sem.at[k], self.land_sem.at[k],
            device_id=device_partner(self.axes[self.order[k]]), device_id_type=MESH)

    def send(self, k):
        self.copy(k).start()

    def fold(self, k, store=None):
        self.copy(k).wait_recv()
        index = self.view(k, True)
        free = [i for i, v in enumerate(index) if isinstance(v, slice)]
        for j in range(1 << len(free)):
            place = [(j >> (len(free) - 1 - i)) & 1 for i in range(len(free))]
            here = list(index)
            for i, axis in enumerate(free):
                here[axis] = place[i]
            here = tuple(here)
            total = self.buffer[here].astype(F32) + self.lands[k][tuple(place)].astype(F32)
            if store is None:
                self.buffer[here] = total.astype(BF)
            else:
                store(total)

    def finish(self):
        for k in range(len(self.axes)):
            self.copy(k).wait_send()


class Butterfly:
    def __init__(self, refs):
        self.axes = [(name, b) for name in ("seq", "dp", "tensor") for b in range(bits_of(name))]
        self.held, self.land = refs.held, refs.land
        self.send_sem, self.land_sem = refs.send, refs.arrive

    @staticmethod
    def scratch(shape):
        phases = bits_of("seq") + bits_of("dp") + bits_of("tensor")
        return dict(
            held=pltpu.VMEM((phases + 1,) + shape, F32),
            land=pltpu.VMEM((phases,) + shape, F32),
            send=pltpu.SemaphoreType.DMA((phases,)),
            arrive=pltpu.SemaphoreType.DMA((phases,)),
        )

    def neighbours(self):
        return [(device_partner(axis), True) for axis in self.axes]

    def copy(self, k):
        return pltpu.make_async_remote_copy(
            self.held.at[k], self.land.at[k], self.send_sem.at[k], self.land_sem.at[k],
            device_id=device_partner(self.axes[k]), device_id_type=MESH)

    def put(self, value):
        self.held[0] = value
        self.copy(0).start()

    def fold(self, k):
        self.copy(k).wait_recv()
        self.held[k + 1] = self.held[k] + self.land[k]
        if k + 1 < len(self.axes):
            self.copy(k + 1).start()

    def total(self):
        return self.held[len(self.axes)]

    def finish(self):
        for k in range(len(self.axes)):
            self.copy(k).wait_send()


def norm_parts(value):
    inverse = lax.rsqrt(jnp.mean(value * value, -1, keepdims=True) + EPS)
    return value * inverse, inverse


def norm_back(grad, gain, hat, inverse):
    scaled = grad * gain
    inner = jnp.mean(scaled * hat, -1, keepdims=True)
    return inverse * (scaled - hat * inner)


def row_sums(value):
    return jnp.sum(value, 0, keepdims=True)


def heads_of(value):
    return [value[:, h * HEAD : (h + 1) * HEAD] for h in range(value.shape[1] // HEAD)]


def rope(value, cosine, signed_sine):
    return value * cosine + pltpu.roll(value, HEAD // 2, 1) * signed_sine


def rope_back(grad, cosine, signed_sine):
    return grad * cosine - pltpu.roll(grad, HEAD // 2, 1) * signed_sine


def attend(r, c, stretch):
    rows, span = r.queries_in.shape[0], r.window_in.shape[0] // (r.low.shape[1] // stretch)
    offset = span - stretch
    per = stretch // rows
    length = min(WINDOW + rows, span)
    q_start = offset + lax.rem(c, per) * rows
    start = jnp.clip(q_start + rows - length, 0, span - length)
    here = pl.ds(pl.multiple_of((c // per) * span + start, rows), length)
    group = r.queries_in.shape[1] * 2 // r.window_in.shape[1]
    low = r.low[:, pl.ds(pl.multiple_of(c * rows, rows), rows)].astype(F32)
    low = jnp.broadcast_to(low, (HEAD, rows)).T[:, :1]
    key_index = (start + lax.broadcasted_iota(jnp.int32, (rows, length), 1)).astype(F32)
    q_index = (q_start + lax.broadcasted_iota(jnp.int32, (rows, 1), 0)).astype(F32)
    mask = (key_index >= low) & (key_index <= q_index)
    mask = jnp.concatenate([mask] * group, 0)
    queries = heads_of(r.queries_in[...])
    kv_heads = len(queries) // group
    outs = []
    for g in range(kv_heads):
        keys = r.window_in[here, g * HEAD : (g + 1) * HEAD]
        values = r.window_in[here, (kv_heads + g) * HEAD : (kv_heads + g + 1) * HEAD]
        s = dot(jnp.concatenate(queries[g * group : (g + 1) * group], 0), keys, NT) * (SCALE * LOG2E)
        p = jnp.where(mask, jnp.exp2(s), 0.0)
        part = p[:, :HEAD]
        for k in range(1, length // HEAD):
            part = part + p[:, k * HEAD : (k + 1) * HEAD]
        total = jnp.sum(part, 1, keepdims=True)
        o = (dot(p.astype(BF), values) / total).astype(BF)
        log_total = jnp.broadcast_to(jnp.log2(total), (group * rows, HEAD))
        for h in range(group):
            outs.append(o[h * rows : (h + 1) * rows])
            r.lse[g, h : h + 1, :] = log_total[h * rows : (h + 1) * rows].T[0:1, :]
    context = jnp.concatenate(outs, 1)
    r.context[...] = context
    return context


def attend_ins(a, low, when):
    return dict(
        queries_in=(a.queries, when),
        window_in=(a.window, WHOLE),
        low=(low, WHOLE),
    )


def attend_outs(a, when):
    kv_heads = a.window.shape[1] // (2 * HEAD)
    rows, width = a.queries.shape
    shape = (kv_heads, width // (kv_heads * HEAD), rows)
    return dict(
        context=((rows, width), BF, when),
        lse=(shape, F32, pl.BlockSpec(shape[:2] + (rows // when[2],), lambda s: (0, 0, chunk_index(when, s)))),
    )


def project(r, hidden, kv, c):
    hat, _ = norm_parts(hidden)
    low = (hat * r.attn_gain[...].astype(F32)).astype(BF)
    r.attn_low[...] = low
    q_raw = dot(low, r.w_q[...])
    k_raw = dot(low, r.w_k[...])
    values = dot(low, r.w_v[...])
    r.q_raw[...] = q_raw
    r.k_raw[...] = k_raw
    cosine, sine = r.cosine[...], r.sine[...]

    def turned(raw, gain):
        return jnp.concatenate(
            [rope(norm_parts(u)[0] * gain, cosine, sine).astype(BF) for u in heads_of(raw)], 1)

    r.queries[...] = turned(q_raw, r.q_gain[...].astype(F32))
    kv.held[kv.at(c), :] = jnp.concatenate([turned(k_raw, r.k_gain[...].astype(F32)), values.astype(BF)], 1)
    kv.send(c)


def project_outs(rows, width, w, stretch, reach, when):
    q_width, k_width = w.w_q.shape[2], w.w_k.shape[2]
    return dict(
        attn_low=((rows, width), BF, when),
        q_raw=((rows, q_width), F32, when),
        k_raw=((rows, k_width), F32, when),
        queries=((rows, q_width), BF, when),
        window=((rows // stretch * (reach + 1) * stretch, k_width + w.w_v.shape[2]), BF, HBM),
    )


def project_ins(w, layer, tables, when, late):
    def weight(array):
        return (array, Late(layer)) if late else of_layer(array, layer)

    return dict(
        attn_gain=(w.attn_gain, Row(layer)),
        w_q=weight(w.w_q),
        w_k=weight(w.w_k),
        w_v=weight(w.w_v),
        q_gain=(w.q_gain, Row(layer)),
        k_gain=(w.k_gain, Row(layer)),
    ) | (dict(cosine=(tables[0], when), sine=(tables[1], when)) if tables else {})


def mlp_gates(r, low):
    gate = dot(low, r.w_gate[...])
    up = dot(low, r.w_up[...])
    sigma = jax.nn.sigmoid(gate)
    return gate, up, sigma


def mlp_back(r, g_low, gate, up, sigma):
    d_act = dot(g_low, r.w_down[...], NT)
    d_gate = (d_act * up * sigma * (1.0 + gate * (1.0 - sigma))).astype(BF)
    d_up = (d_act * gate * sigma).astype(BF)
    return d_gate, d_up, dot(d_gate, r.w_gate[...], NT) + dot(d_up, r.w_up[...], NT)


def first_projection(hidden, segments, positions, w, stretch, reach, chunks, collective_id):
    rows, width = hidden.shape
    when = (1, 0, chunks)
    kv_width = w.w_k.shape[2] + w.w_v.shape[2]

    held = max(reach, 1)
    seqs = rows // stretch

    def body(r, s):
        kv = KeyValueSend(r, reach, stretch)

        def documents(back):
            return pltpu.make_async_remote_copy(
                r.segments, r.docs.at[back - 1], r.doc_send.at[back - 1], r.doc_land.at[back - 1],
                device_id={"seq": jnp.minimum(kv.place + back, kv.count - 1)}, device_id_type=MESH)

        @pl.when(s == 0)
        def _():
            r.docs[...] = jnp.full_like(r.docs, -1)
            enter(kv.neighbours())
            kv.start()
            for back in range(1, reach + 1):

                @pl.when(kv.place + back < kv.count)
                def _():
                    documents(back).start()

        angle = jnp.broadcast_to(r.positions[...].astype(F32), (HEAD, rows // chunks)).T * r.frequency[...]
        lane = lax.broadcasted_iota(jnp.int32, angle.shape, 1)
        sine = jnp.sin(angle)
        r.cosine[...] = jnp.cos(angle)
        r.sine[...] = jnp.where(lane < HEAD // 2, -sine, sine)
        project(r, r.hidden[...].astype(F32), kv, s)

        @pl.when(s == chunks - 1)
        def _():
            kv.finish()
            for back in range(1, reach + 1):

                @pl.when(kv.place + back < kv.count)
                def _():
                    documents(back).wait_send()

                @pl.when(kv.place >= back)
                def _():
                    documents(back).wait_recv()

            for q in range(seqs):
                here = slice(q * stretch, (q + 1) * stretch)
                own = r.segments[:, here]
                docs = [r.docs[back - 1, :, here] for back in range(1, reach + 1)]

                def first_of(document):
                    counts = [jnp.sum((d < document).astype(jnp.int32), 1, keepdims=True) for d in docs + [own]]
                    return functools.reduce(jnp.add, counts)

                low = jnp.broadcast_to(first_of(0), own.shape)
                for document in range(1, 4):
                    low = jnp.where(own >= document, first_of(document), low)
                index = lax.broadcasted_iota(jnp.int32, own.shape, 1)
                r.low[:, here] = jnp.maximum(low, reach * stretch + index - (WINDOW - 1))

    frequency = THETA ** (-(jnp.arange(HEAD // 2, dtype=F32) * 2.0) / HEAD)
    return step_kernel(
        first_projection, body, chunks,
        dict(
            hidden=(hidden, when),
            segments=(segments.reshape(1, rows), WHOLE),
            positions=(
                positions.reshape(1, rows), pl.BlockSpec((1, rows // chunks), lambda s: (0, chunk_index(when, s)))),
            frequency=(jnp.concatenate([frequency, frequency])[None], WHOLE),
        )
        | project_ins(w, 0, None, when, False),
        project_outs(rows, width, w, stretch, reach, when)
        | dict(
            cosine=((rows, HEAD), F32, when),
            sine=((rows, HEAD), F32, when),
            low=((1, rows), jnp.int32, WHOLE),
        ),
        dict(
            kv=KeyValueSend.scratch(rows, kv_width, chunks, reach),
            docs=pltpu.VMEM((held, 1, rows), jnp.int32),
            doc_send=pltpu.SemaphoreType.DMA((held,)),
            doc_land=pltpu.SemaphoreType.DMA((held,)),
        ),
        collective_id)


def between_forward(a, low, w, layer, tables, stretch, reach, chunks, collective_id):
    hidden = a.hidden
    rows, width = hidden.shape
    kv_width = w.w_k.shape[2] + w.w_v.shape[2]
    ff = w.w_gate.shape[2]
    pieces = chunks * PIECES
    first, second, third = (PIECES, 0, chunks), (PIECES, 4, chunks), (PIECES, 8, chunks)
    steps = PIECES * (chunks - 1) + third[1] + 1
    chunk = rows // chunks

    def body(r, s):
        kv = KeyValueSend(r, reach, stretch)
        attn, mlp = LineSum(r.attn), LineSum(r.mlp)

        @pl.when(s == 0)
        def _():
            enter(attn.neighbours() + kv.neighbours())
            kv.start()

        def send_attn(c):
            attn.put(c, dot(attend(r, c, stretch), r.w_o[...]))

        def feed_forward(c):
            middle = r.hidden[...].astype(F32) + attn.total(c, chunk)
            r.hidden_mid[...] = middle
            r.mid_held[attn.at(c, chunk), :] = middle
            hat, _ = norm_parts(middle)
            low = (hat * r.mlp_gain[...].astype(F32)).astype(BF)
            r.mlp_low[...] = low
            gate, up, sigma = mlp_gates(r, low)
            r.gate[...] = gate
            r.up[...] = up
            act = (gate * sigma * up).astype(BF)
            r.act[...] = act
            mlp.put(c, dot(act, r.w_down[...]))

        def next_layer(c):
            hidden_next = r.mid_held[mlp.at(c, chunk), :] + mlp.total(c, chunk)
            r.hidden_next[...] = hidden_next
            project(r, hidden_next, kv, c)

        at_chunk(s, first, send_attn)
        at_chunk(s, (1, 1, pieces), attn.relay)
        at_chunk(s, (1, 2, pieces), attn.meet)
        r.arrived(second[1], *MLP_WEIGHTS)
        at_chunk(s, second, feed_forward)
        at_chunk(s, (1, 6, pieces), mlp.relay)
        at_chunk(s, (1, 7, pieces), mlp.meet)
        r.arrived(third[1], *QKV_WEIGHTS)
        at_chunk(s, third, next_layer)

        @pl.when(s == steps - 1)
        def _():
            attn.finish()
            mlp.finish()
            kv.finish()

    return step_kernel(
        between_forward, body, steps,
        attend_ins(a, low, first)
        | dict(
            w_o=of_layer(w.w_o, layer),
            hidden=(hidden, second),
            mlp_gain=(w.mlp_gain, Row(layer)),
            w_gate=(w.w_gate, Late(layer)),
            w_up=(w.w_up, Late(layer)),
            w_down=(w.w_down, Late(layer)),
        )
        | project_ins(w, layer + 1, tables, third, True),
        attend_outs(a, first)
        | dict(
            hidden_mid=((rows, width), F32, second),
            mlp_low=((rows, width), BF, second),
            gate=((rows, ff), F32, second),
            up=((rows, ff), F32, second),
            act=((rows, ff), BF, second),
            hidden_next=((rows, width), F32, third),
        )
        | project_outs(rows, width, w, stretch, reach, third),
        dict(
            attn=LineSum.scratch(rows, width, pieces),
            mlp=LineSum.scratch(rows, width, pieces),
            kv=KeyValueSend.scratch(rows, kv_width, chunks, reach),
            mid_held=pltpu.VMEM((rows, width), F32),
        ),
        collective_id)


def turn_around(a, low, cotangent, w, layer, stretch, chunks, collective_id):
    hidden = a.hidden
    rows, width = hidden.shape
    ff = w.w_gate.shape[2]
    pieces = chunks * PIECES
    first, second, third = (PIECES, 0, chunks), (PIECES, 6, chunks), (PIECES, 12, chunks)
    steps = PIECES * (chunks - 1) + third[1] + 1
    chunk = rows // chunks

    def body(r, s):
        attn, back = LineSum(r.attn), LineSum(r.back)

        @pl.when(s == 0)
        def _():
            enter(attn.neighbours())
            r.gain_grad[...] = jnp.zeros_like(r.gain_grad)

        def send_attn(c):
            attn.put(c, dot(attend(r, c, stretch), r.w_o[...]))

        def feed_forward(c):
            middle = r.hidden[...] + attn.total(c, chunk)
            r.hidden_mid[...] = middle
            r.mid_held[attn.at(c, chunk), :] = middle
            hat, _ = norm_parts(middle)
            low = (hat * r.mlp_gain[...].astype(F32)).astype(BF)
            r.mlp_low[...] = low
            gate, up, sigma = mlp_gates(r, low)
            d_gate, d_up, part = mlp_back(r, r.cotangent[...], gate, up, sigma)
            back.put(c, part)
            r.d_gate[...] = d_gate
            r.d_up[...] = d_up
            act = (gate * sigma * up).astype(BF)
            r.act[...] = act
            part = dot(act, r.w_down[...]).astype(BF)

            @pl.when(c < chunks // 2)
            def _():
                r.lower_part[...] = part

            @pl.when(c >= chunks // 2)
            def _():
                r.upper_part[...] = part

        def middle_grad(c):
            hat, inverse = norm_parts(r.mid_held[back.at(c, chunk), :])
            d_in = back.total(c, chunk)
            r.gain_grad[0:1, :] += row_sums(d_in * hat)
            g_mid = r.cotangent_late[...].astype(F32) + norm_back(d_in, r.mlp_gain[...].astype(F32), hat, inverse)
            r.g_mid[...] = g_mid
            mid_low = g_mid.astype(BF)
            r.mid_low[...] = mid_low
            r.d_context[...] = dot(mid_low, r.w_o[...], NT).astype(BF)

        at_chunk(s, first, send_attn)
        at_chunk(s, (1, 3, pieces), attn.relay)
        at_chunk(s, (1, 4, pieces), attn.meet)
        r.arrived(second[1], *MLP_WEIGHTS)
        at_chunk(s, second, feed_forward)
        at_chunk(s, (1, 9, pieces), back.relay)
        at_chunk(s, (1, 10, pieces), back.meet)
        at_chunk(s, third, middle_grad)

        @pl.when(s == steps - 1)
        def _():
            attn.finish()
            back.finish()

    return step_kernel(
        turn_around, body, steps,
        attend_ins(a, low, first)
        | dict(
            w_o=of_layer(w.w_o, layer),
            hidden=(hidden, second),
            cotangent=(cotangent, second),
            cotangent_late=(cotangent, third),
            mlp_gain=(w.mlp_gain, Row(layer)),
            w_gate=(w.w_gate, Late(layer)),
            w_up=(w.w_up, Late(layer)),
            w_down=(w.w_down, Late(layer)),
        ),
        attend_outs(a, first)
        | dict(
            mlp_low=((rows, width), BF, second),
            act=((rows, ff), BF, second),
            hidden_mid=((rows, width), F32, second),
            lower_part=((rows // 2, width), BF, (PIECES, second[1], chunks // 2)),
            upper_part=((rows // 2, width), BF, (PIECES, second[1] + PIECES * (chunks // 2), chunks // 2)),
            d_gate=((rows, ff), BF, second),
            d_up=((rows, ff), BF, second),
            g_mid=((rows, width), F32, third),
            mid_low=((rows, width), BF, third),
            d_context=(a.queries.shape, BF, third),
            gain_grad=((8, width), F32, WHOLE),
        ),
        dict(
            attn=LineSum.scratch(rows, width, pieces),
            back=LineSum.scratch(rows, width, pieces),
            mid_held=pltpu.VMEM((rows, width), F32),
        ),
        collective_id)


def attention_grads(r, back, line, c):
    cosine, sine = r.cosine[...], r.sine[...]
    both = back.add(r.d_own[...], c)

    def raw_back(grads, raws, gain):
        lows, gains = [], 0.0
        for grad, raw in zip(heads_of(grads), heads_of(raws)):
            grad = rope_back(grad, cosine, sine)
            hat, inverse = norm_parts(raw)
            gains = gains + row_sums(grad * hat)
            lows.append(norm_back(grad, gain, hat, inverse).astype(BF))
        return jnp.concatenate(lows, 1), gains

    d_q, q_gain = raw_back(r.d_q[...], r.q_raw[...], r.q_gain[...].astype(F32))
    d_k, k_gain = raw_back(both[0], r.k_raw[...], r.k_gain[...].astype(F32))
    d_v = both[1].astype(BF)
    r.head_gain[0:1, 0:HEAD] += q_gain
    r.head_gain[0:1, HEAD : 2 * HEAD] += k_gain
    r.d_held[line.at(c, d_q.shape[0]), :] = jnp.concatenate([d_q, d_k, d_v], 1)
    part = dot(d_q, r.w_q[...], NT) + dot(d_k, r.w_k[...], NT) + dot(d_v, r.w_v[...], NT)
    line.put(c, part)
    return part


class WeightGrads:
    def __init__(self, r, plan):
        self.r = r
        self.plan = plan
        self.slabs = plan.slabs[2]
        self.late = Scatter(r.sc_q, False), Scatter(r.sc_kv, True)
        self.early = Scatter(r.sc_a, False), Scatter(r.sc_b, True)
        self.blocks = 1 << len(block_axes())

    @staticmethod
    def scratch(rows, width, q_width, k_width, ff):
        per = width // (1 << len(block_axes()))
        return dict(
            sc_a=Scatter.scratch(per, ff + q_width),
            sc_b=Scatter.scratch(per, 2 * ff),
            sc_q=Scatter.scratch(per, q_width),
            sc_kv=Scatter.scratch(per, 2 * k_width),
            d_held=pltpu.VMEM((rows, q_width + 2 * k_width), BF),
        )

    def neighbours(self):
        return self.late[0].neighbours()

    def put(self, scatter, slab, columns, value):
        per = self.blocks // self.slabs
        rows = value.shape[0] // per
        for j in range(per):
            scatter.put(slab * per + j, columns, value[j * rows : (j + 1) * rows])

    def mlp_slab(self, slab):
        r = self.r
        ff = r.d_gate_all.shape[1]
        q_width = r.context_all.shape[1]
        mlp_low = r.mlp_low_slab[...]
        self.put(self.early[0], slab, slice(0, ff), dot(mlp_low, r.d_gate_all[...], TN))
        self.put(self.early[0], slab, slice(ff, ff + q_width), dot(r.mid_low_slab[...], r.context_all[...], TN))
        self.put(self.early[1], slab, slice(0, ff), dot(mlp_low, r.d_up_all[...], TN))
        self.put(self.early[1], slab, slice(ff, 2 * ff), dot(r.g_low_slab[...], r.act_all[...], TN))

    def qkv_slabs(self, begin, end):
        r = self.r
        slab_width = r.attn_low_all.shape[1] // self.slabs
        q_width = r.d_q.shape[1]

        @pl.loop(begin, end)
        def _(slab):
            columns = pl.ds(pl.multiple_of(slab * slab_width, slab_width), slab_width)
            value = dot(r.attn_low_all[:, columns], r.d_held[...], TN)
            self.put(self.late[0], slab, slice(None), value[:, :q_width])
            self.put(self.late[1], slab, slice(None), value[:, q_width:])

    def each(self, scatters, work):
        for scatter in scatters:
            work(scatter)

    def store(self):
        r = self.r
        last = len(block_axes()) - 1
        ff = r.d_gate_all.shape[1]
        k_width = r.k_raw.shape[1]

        def store_a(total):
            r.grad_gate[...] = total[:, :ff]
            r.grad_o[...] = total[:, ff:]

        def store_b(total):
            r.grad_up[...] = total[:, :ff]
            r.grad_down[...] = total[:, ff:]

        def store_q(total):
            r.grad_q[...] = total

        def store_kv(total):
            r.grad_k[...] = total[:, :k_width]
            r.grad_v[...] = total[:, k_width:]

        self.early[0].fold(last, store_a)
        self.early[1].fold(last, store_b)
        self.late[0].fold(last, store_q)
        self.late[1].fold(last, store_kv)

    def late_slabs(self, s):
        for i in range(2):
            self.r.arrived(self.plan.late_slabs[0], "attn_low_all") if i == 0 else None

            @pl.when(s == self.plan.late_slabs[i])
            def _():
                self.qkv_slabs(i * self.slabs // 2, (i + 1) * self.slabs // 2)

        @pl.when(s == self.plan.late_slabs[1])
        def _():
            self.each(self.late, lambda scatter: scatter.send(0))

    def run(self, s):
        rate, lag, count = self.plan.slabs
        self.r.arrived(lag, *GRAD_OPERANDS)
        at_chunk(s, self.plan.slabs, self.mlp_slab)

        @pl.when(s == lag + rate * (count - 1))
        def _():
            self.each(self.early, lambda scatter: scatter.send(0))

        for k in range(len(block_axes()) - 1):

            def move(scatter):
                scatter.fold(k)
                scatter.send(k + 1)

            @pl.when(s == self.plan.early(k))
            def _():
                self.each(self.early, move)

            @pl.when(s == self.plan.late(k))
            def _():
                self.each(self.late, move)

    def finish(self):
        self.each(self.early + self.late, lambda scatter: scatter.finish())


def slab_count(chunks):
    return min(4, max(1, chunks // 2))


def grads_ins(a, rows, width, when):
    slab = pl.BlockSpec((rows, width // when[2]), lambda s: (0, chunk_index(when, s)))
    return dict(
        mlp_low_slab=(a.mlp_low, slab),
        mid_low_slab=(a.mid_low, slab),
        g_low_slab=(a.g_low, slab),
        attn_low_all=(a.attn_low, Late()),
        d_gate_all=(a.d_gate, Late()),
        d_up_all=(a.d_up, Late()),
        context_all=(a.context, Late()),
        act_all=(a.act, Late()),
    )


def grads_outs(width, q_width, k_width, ff):
    per = width // (1 << len(block_axes()))
    return dict(
        grad_q=((per, q_width), F32, WHOLE),
        grad_k=((per, k_width), F32, WHOLE),
        grad_v=((per, k_width), F32, WHOLE),
        grad_o=((per, q_width), F32, WHOLE),
        grad_gate=((per, ff), F32, WHOLE),
        grad_up=((per, ff), F32, WHOLE),
        grad_down=((per, ff), F32, WHOLE),
    )


def attention_grads_ins(a, w, layer, tables, when):
    rows, k_width = a.k_raw.shape
    own = pl.BlockSpec((2, rows // when[2], k_width), lambda s: (0, chunk_index(when, s), 0))
    return dict(
        d_q=(a.d_q, when),
        d_own=(a.d_own, own),
        d_prev=(a.d_prev, HBM),
        q_raw=(a.q_raw, when),
        k_raw=(a.k_raw, when),
        cosine=(tables[0], when),
        sine=(tables[1], when),
        w_q=of_layer(w.w_q, layer),
        w_k=of_layer(w.w_k, layer),
        w_v=of_layer(w.w_v, layer),
        q_gain=(w.q_gain, Row(layer)),
        k_gain=(w.k_gain, Row(layer)),
        attn_gain=(w.attn_gain, Row(layer)),
    )


def between_backward(a, below, g_mid, w, layer, tables, reach, chunks, collective_id):
    rows, width = g_mid.shape
    q_width, k_width, ff = w.w_q.shape[2], w.w_k.shape[2], w.w_gate.shape[2]
    pieces = chunks * PIECES
    first, second, third = (PIECES, 0, chunks), (PIECES, 4, chunks), (PIECES, 10, chunks)
    steps = PIECES * (chunks - 1) + third[1] + 1
    chunk = rows // chunks
    after = PIECES * (chunks - 1) + 1
    plan = types.SimpleNamespace(
        slabs=(PIECES, 2, slab_count(chunks)),
        early=lambda k: min(after - 3 + 4 * k, steps - 2),
        late_slabs=(after, after + 1),
        late=lambda k: min(after + 3 + 2 * k, steps - 2),
    )

    def body(r, s):
        back = KeyValueReturn(r, reach)
        attn, mlp = LineSum(r.attn), LineSum(r.mlp)
        grads = WeightGrads(r, plan)

        @pl.when(s == 0)
        def _():
            enter(attn.neighbours() + back.neighbours() + grads.neighbours())
            back.start()
            r.gain_grad[...] = jnp.zeros_like(r.gain_grad)
            r.head_gain[...] = jnp.zeros_like(r.head_gain)

        def send_attn(c):
            attention_grads(r, back, attn, c)

        def feed_forward(c):
            hat, inverse = norm_parts(r.hidden[...])
            d_in = attn.total(c, chunk)
            r.gain_grad[0:1, :] += row_sums(d_in * hat)
            g = r.g_above[...] + norm_back(d_in, r.attn_gain[...].astype(F32), hat, inverse)
            r.g_held[lax.rem(c, 4)] = g
            g_low = g.astype(BF)
            r.g_low[...] = g_low
            gate = r.gate[...]
            d_gate, d_up, part = mlp_back(r, g_low, gate, r.up[...], jax.nn.sigmoid(gate))
            r.d_gate[...] = d_gate
            r.d_up[...] = d_up
            mlp.put(c, part)

        def middle_grad(c):
            hat, inverse = norm_parts(r.hidden_mid[...])
            d_in = mlp.total(c, chunk)
            r.gain_grad[1:2, :] += row_sums(d_in * hat)
            g_mid = r.g_held[lax.rem(c, 4)] + norm_back(d_in, r.mlp_gain[...].astype(F32), hat, inverse)
            r.g_mid[...] = g_mid
            mid_low = g_mid.astype(BF)
            r.mid_low[...] = mid_low
            r.d_context[...] = dot(mid_low, r.w_o[...], NT).astype(BF)

        at_chunk(s, first, send_attn)
        grads.late_slabs(s)
        at_chunk(s, (1, 1, pieces), attn.relay)
        at_chunk(s, (1, 2, pieces), attn.meet)
        r.arrived(second[1], *MLP_WEIGHTS)
        at_chunk(s, second, feed_forward)
        at_chunk(s, (1, 6, pieces), mlp.relay)
        at_chunk(s, (1, 7, pieces), mlp.meet)
        r.arrived(third[1], "w_o")
        at_chunk(s, third, middle_grad)
        grads.run(s)

        @pl.when(s == steps - 1)
        def _():
            grads.store()
            attn.finish()
            mlp.finish()
            back.finish()
            grads.finish()

    return step_kernel(
        between_backward, body, steps,
        attention_grads_ins(a, w, layer, tables, first)
        | grads_ins(a, rows, width, plan.slabs)
        | dict(
            hidden=(a.hidden, second),
            g_above=(g_mid, second),
            gate=(below.gate, second),
            up=(below.up, second),
            hidden_mid=(below.hidden_mid, third),
            mlp_gain=(w.mlp_gain, Row(layer - 1)),
            w_gate=(w.w_gate, Late(layer - 1)),
            w_up=(w.w_up, Late(layer - 1)),
            w_down=(w.w_down, Late(layer - 1)),
            w_o=(w.w_o, Late(layer - 1)),
        ),
        dict(
            g_low=((rows, width), BF, second),
            d_gate=((rows, ff), BF, second),
            d_up=((rows, ff), BF, second),
            g_mid=((rows, width), F32, third),
            mid_low=((rows, width), BF, third),
            d_context=((rows, q_width), BF, third),
            gain_grad=((8, width), F32, WHOLE),
            head_gain=((8, 2 * HEAD), F32, WHOLE),
        )
        | grads_outs(width, q_width, k_width, ff),
        dict(
            attn=LineSum.scratch(rows, width, pieces),
            mlp=LineSum.scratch(rows, width, pieces),
            kr=KeyValueReturn.scratch(rows, k_width, chunks, reach),
            **WeightGrads.scratch(rows, width, q_width, k_width, ff),
            g_held=pltpu.VMEM((4, rows // chunks, width), F32),
        ),
        collective_id)


def last_backward(a, top, top_halves, above, w, tables, reach, chunks, collective_id):
    g_mid = above.g_mid
    rows, width = g_mid.shape
    q_width, k_width, ff = w.w_q.shape[2], w.w_k.shape[2], w.w_gate.shape[2]
    layer = 0
    pieces = chunks * PIECES
    pairs = max(1, chunks // 2)
    half = rows // 2
    half_pieces = pieces // 2
    first, second, third = (PIECES, 0, pairs), (PIECES, 8, chunks), (PIECES, 5, chunks)
    steps = PIECES * (chunks - 1) + second[1] + 1
    chunk = rows // chunks
    after = PIECES * pairs
    plan = types.SimpleNamespace(
        slabs=(PIECES, 1, slab_count(chunks)),
        early=lambda k: min(after + 1 + 4 * k, steps - 2),
        late_slabs=(after, after + 1),
        late=lambda k: min(after + 5 + 5 * k, steps - 2),
    )

    def body(r, s):
        back = KeyValueReturn(r, reach)
        attn, upper, lower = LineSum(r.attn), LineSum(r.upper, r.upper_part), Spread(r.lower, r.lower_here)
        grads = WeightGrads(r, plan)
        sums = Butterfly(r.sums)

        @pl.when(s == 0)
        def _():
            enter(attn.neighbours() + back.neighbours() + sums.neighbours())
            back.start()
            lower.start(r.lower_there)
            r.head_gain[...] = jnp.zeros_like(r.head_gain)
            r.gain_held[...] = jnp.zeros_like(r.gain_held)

        def send_attn(c):
            part = attention_grads(r, back, attn, c)
            hat, _ = norm_parts(r.hidden[...].astype(F32))
            r.gain_held[...] += row_sums(part * hat)

        def give_output(c):
            @pl.when(c < chunks // 2)
            def _():
                r.output[...] = (r.hidden_mid[...] + lower.total(c, chunk)).astype(BF)

            @pl.when(c >= chunks // 2)
            def _():
                r.output[...] = (r.hidden_mid[...] + upper.total(c - chunks // 2, chunk)).astype(BF)

        def push_upper(j):
            upper.push(j, 2 * upper.rows)

        def give_input(c):
            hat, inverse = norm_parts(r.hidden_late[...].astype(F32))
            r.input_grad[...] = r.g_above[...] + norm_back(attn.total(c, chunk), r.attn_gain[...].astype(F32), hat, inverse)

        at_chunk(s, (1, 0, half_pieces // 2), push_upper)
        at_chunk(s, first, send_attn)
        grads.late_slabs(s)
        at_chunk(s, (1, 3, half_pieces), upper.relay)
        at_chunk(s, (1, 3, pieces), attn.relay)
        at_chunk(s, (1, 5, half_pieces), upper.meet)
        at_chunk(s, (1, 5, pieces), attn.meet)
        at_chunk(s, third, give_output)
        at_chunk(s, second, give_input)
        grads.run(s)

        @pl.when(s == after)
        def _():
            row = lax.broadcasted_iota(jnp.int32, (8, width), 0)
            once = jnp.where(lax.axis_index("tensor") == 0, 1.0, 0.0)
            heads = [r.head_gain[0:1, :], r.above_head_gain[0:1, :], jnp.zeros((1, width - 4 * HEAD), F32)]
            packet = jnp.zeros((8, width), F32)
            for place, part in enumerate([
                r.gain_held[...], r.above_gain[0:1, :] * once, r.above_gain[1:2, :] * once, r.top_gain[0:1, :] * once,
                jnp.concatenate(heads, 1),
            ]):
                packet = jnp.where(row == place, part, packet)
            sums.put(packet)

        for k in range(len(sums.axes)):

            @pl.when(s == min(after + 2 + 2 * k, steps - 1))
            def _():
                sums.fold(k)

        @pl.when(s == steps - 1)
        def _():
            grads.store()
            r.gains[...] = sums.total()
            attn.finish()
            upper.finish()
            lower.finish()
            back.finish()
            grads.finish()
            sums.finish()

    return step_kernel(
        last_backward, body, steps,
        attention_grads_ins(a, w, layer, tables, first)
        | grads_ins(a, rows, width, plan.slabs)
        | dict(
            hidden=(a.hidden, first),
            hidden_late=(a.hidden, second),
            g_above=(g_mid, second),
            above_gain=(above.gain_grad, WHOLE),
            above_head_gain=(above.head_gain, WHOLE),
            top_gain=(top.gain_grad, WHOLE),
            upper_part=(top.upper_part, WHOLE),
            lower_here=(top_halves[0], WHOLE),
            lower_there=(top_halves[1], WHOLE),
            hidden_mid=(top.hidden_mid, third),
        ),
        dict(
            input_grad=((rows, width), F32, second),
            output=((rows, width), BF, third),
            gains=((8, width), F32, WHOLE),
        )
        | grads_outs(width, q_width, k_width, ff),
        dict(
            attn=LineSum.scratch(rows, width, pieces),
            upper=Spread.scratch(half, width, half_pieces),
            lower=Spread.scratch(half, width, half_pieces),
            kr=KeyValueReturn.scratch(rows, k_width, pairs, reach),
            **WeightGrads.scratch(rows, width, q_width, k_width, ff),
            sums=Butterfly.scratch((8, width)),
            head_gain=pltpu.VMEM((8, 2 * HEAD), F32),
            gain_held=pltpu.VMEM((1, width), F32),
        ),
        collective_id)


def collect_kernel(count, output_in, input_in, gains, *refs):
    ins, (output, input_grad, attn, mlp, q_gain, k_gain), outs = refs[: 2 * count], refs[2 * count : 2 * count + 6], refs[2 * count + 6 :]
    output[...] = output_in[...]
    input_grad[...] = input_in[...]
    s = pl.program_id(0)

    @pl.when(s == 0)
    def _():
        attn[...] = gains[0:2, :]
        mlp[...] = gains[2:4, :]
        for layer in range(2):
            at = 2 * layer * HEAD
            q_gain[layer : layer + 1, :] = gains[4:5, at : at + HEAD]
            k_gain[layer : layer + 1, :] = gains[4:5, at + HEAD : at + 2 * HEAD]

    for g in range(count):
        for layer in range(2):
            value = ins[2 * g + layer]
            if outs[g].shape[1] == value.shape[0]:
                outs[g][layer] = value[...]
            else:

                @pl.when(s == 0)
                def _():
                    outs[g][layer] = value[...].T


def collect(end, above):
    rows, width = end.output.shape
    straight = [(k.grad_q, k.grad_k, k.grad_v, k.grad_gate, k.grad_up) for k in (end, above)]
    turned = [(k.grad_o, k.grad_down) for k in (end, above)]
    per = straight[0][0].shape[0]
    steps = max(1, min(8, per // 8))
    whole = pl.BlockSpec(memory_space=pltpu.VMEM)

    def blocks(array):
        return pl.BlockSpec((array.shape[0] // steps, array.shape[1]), lambda s: (s, 0))

    ins = [end.output, end.input_grad, end.gains]
    in_specs = [blocks(end.output), blocks(end.input_grad), whole]
    outs = [
        ((rows, width), BF, blocks(end.output)), ((rows, width), F32, blocks(end.input_grad)),
        ((2, width), F32, whole), ((2, width), F32, whole), ((2, HEAD), F32, whole), ((2, HEAD), F32, whole),
    ]
    for pair in zip(*straight):
        ins += pair
        in_specs += [blocks(a) for a in pair]
        shape = pair[0].shape
        outs.append(((2,) + shape, F32, pl.BlockSpec((2, per // steps, shape[1]), lambda s: (0, s, 0))))
    for pair in zip(*turned):
        ins += pair
        in_specs += [whole, whole]
        outs.append(((2,) + pair[0].shape[::-1], F32, whole))
    return pl.pallas_call(
        functools.partial(collect_kernel, 7),
        grid=(steps,),
        in_specs=in_specs,
        out_specs=[o[2] for o in outs],
        out_shape=[jax.ShapeDtypeStruct(o[0], o[1]) for o in outs],
        name=collect.__name__,
        compiler_params=pltpu.CompilerParams(vmem_limit_bytes=62 << 20),
    )(*ins)


def middle_terms(part):
    n = lax.axis_size("tensor")
    half = n // 2
    total = part
    for hop in range(half - 1):
        moved = lax.ppermute(total, "tensor", [(hop, hop + 1), (n - 1 - hop, n - 2 - hop)])
        total = (part.astype(F32) + moved.astype(F32)).astype(BF)
    return total, lax.ppermute(total, "tensor", [(half - 1, half), (half, half - 1)])


def per_device(
    tokens, cotangent, segments, positions, attn_gain, w_query, key_projection, value_projection, query_gain, key_gain,
    w_output, mlp_gain, w_gate, w_up, w_down,
):
    seqs_here, stretch, width = tokens.shape
    rows = seqs_here * stretch
    reach = min(lax.axis_size("seq") - 1, (WINDOW + stretch - 2) // stretch)
    chunks = rows // min(CHUNK, stretch)

    w = types.SimpleNamespace(
        attn_gain=attn_gain, mlp_gain=mlp_gain, q_gain=query_gain, k_gain=key_gain,
        w_q=w_query, w_k=key_projection, w_v=value_projection, w_o=w_output, w_gate=w_gate, w_up=w_up, w_down=w_down,
    )
    tokens = tokens.reshape(rows, width)
    cotangent = cotangent.reshape(rows, width)

    a0 = first_projection(tokens, segments, positions, w, stretch, reach, chunks, 1)
    tables, low = (a0.cosine, a0.sine), a0.low
    a0.hidden = tokens
    mid = between_forward(a0, low, w, 0, tables, stretch, reach, chunks, 2)
    a0.context, a0.lse = mid.context, mid.lse
    a1 = types.SimpleNamespace(
        attn_low=mid.attn_low, q_raw=mid.q_raw, k_raw=mid.k_raw, queries=mid.queries, window=mid.window,
        hidden=mid.hidden_next)
    turn = turn_around(a1, low, cotangent, w, 1, stretch, chunks, 3)
    a1.context, a1.lse = turn.context, turn.lse
    top_halves = middle_terms(turn.lower_part)
    a1.mlp_low, a1.act, a1.d_gate, a1.d_up = turn.mlp_low, turn.act, turn.d_gate, turn.d_up
    a1.mid_low, a1.g_low = turn.mid_low, cotangent
    a1.d_q, a1.d_own, a1.d_prev = attn_bwd(
        a1.queries, turn.d_context, a1.context, a1.window, low, a1.lse, stretch)
    down = between_backward(a1, mid, turn.g_mid, w, 1, tables, reach, chunks, 4)
    a0.mlp_low, a0.act, a0.d_gate, a0.d_up = mid.mlp_low, mid.act, down.d_gate, down.d_up
    a0.mid_low, a0.g_low = down.mid_low, down.g_low
    a0.d_q, a0.d_own, a0.d_prev = attn_bwd(
        a0.queries, down.d_context, a0.context, a0.window, low, a0.lse, stretch)

    end = last_backward(a0, turn, top_halves, down, w, tables, reach, chunks, 5)
    output, input_grad, attn, mlp, q_gain, k_gain, d_q, d_k, d_v, d_gate, d_up, d_o, d_down = collect(end, down)
    shape = (seqs_here, stretch, width)
    return (
        output.reshape(shape), input_grad.reshape(shape), attn, d_q, d_k, d_v, q_gain, k_gain, d_o, mlp, d_gate, d_up,
        d_down,
    )


def solution(mesh):
    placed = (
        P("dp", "seq", None), P("dp", "seq", None), P("dp", "seq"), P("dp", "seq"), P(), P(None, None, "tensor"),
        P(None, None, "tensor"), P(None, None, "tensor"), P(), P(), P(None, "tensor", None), P(),
        P(None, None, "tensor"), P(None, None, "tensor"), P(None, "tensor", None),
    )
    by_rows = P(None, ("dp", "seq"), "tensor")
    by_columns = P(None, "tensor", ("dp", "seq"))
    return jax.shard_map(
        per_device,
        mesh=mesh,
        in_specs=placed,
        out_specs=(
            P("dp", "seq", None), P("dp", "seq", None), P(), by_rows, by_rows, by_rows, P(), P(), by_columns, P(),
            by_rows, by_rows, by_columns,
        ),
        check_vma=False,
    )
```

```python
import functools
import types

import jax
import jax.numpy as jnp
import numpy as np
from jax import lax
from jax.experimental import pallas as pl
from jax.experimental.pallas import tpu as pltpu
from jax.sharding import PartitionSpec as P

HEAD = 128
LAYER_COUNT = 2
WINDOW = 1024
EPS = 1e-06
THETA = 1000000.0
LOG2E = 1.4426950408889634
SCALE = HEAD ** (-0.5)
CHUNK = 128
PIECES = 2
FINE = 4
MESH = pl.DeviceIdType.MESH
BF = jnp.bfloat16
F32 = jnp.float32

NT = (((1,), (1,)), ((), ()))
NN = (((1,), (0,)), ((), ()))
TN = (((0,), (0,)), ((), ()))


def dot(a, b, dims=NN):
    return lax.dot_general(a, b, dims, preferred_element_type=F32)


def chunk_index(schedule, s):
    rate, lag, count = schedule
    return jnp.clip((s - lag) // rate, 0, count - 1)


def rows_spec(schedule, shape):
    return pl.BlockSpec((shape[0] // schedule[2], shape[1]), lambda s: (chunk_index(schedule, s), 0))


WHOLE, HBM = object(), object()
MLP_WEIGHTS = ("w_gate", "w_up", "w_down")
QKV_WEIGHTS = ("w_q", "w_k", "w_v")
GRAD_OPERANDS = ("d_gates_all", "context_all", "act_all")


class Row:
    def __init__(self, layer):
        self.layer = layer


class Late:
    def __init__(self, layer=None):
        self.layer = layer

    def shape(self, array):
        return array.shape if self.layer is None else array.shape[1:]

    def copy(self, source, held, sem):
        return pltpu.make_async_copy(source if self.layer is None else source.at[self.layer], held, sem)


def step_kernel(owner, body, steps, ins, outs, scratch, collective_id, vmem=62):
    def spec(shape, where, is_in):
        if isinstance(where, pl.BlockSpec):
            return where
        if where is HBM or isinstance(where, Late):
            return pl.BlockSpec(memory_space=pl.ANY)
        if where is WHOLE or isinstance(where, Row):
            zeros = (0,) * len(shape)
            if is_in:
                return pl.BlockSpec(shape, lambda s: zeros, pipeline_mode=pl.Buffered(1))
            return pl.BlockSpec(memory_space=pltpu.VMEM)
        return rows_spec(where, shape)

    late = {name: where for name, (_, where) in ins.items() if isinstance(where, Late)}
    held = {name: pltpu.VMEM(where.shape(ins[name][0]), ins[name][0].dtype) for name, where in late.items()}
    flat, tree = jax.tree.flatten((scratch, held, {name: pltpu.SemaphoreType.DMA(()) for name in late}))

    def kernel(*refs):
        named = dict(zip(ins, refs))
        named.update(zip(outs, refs[len(ins) :]))
        own, held_refs, sems = jax.tree.unflatten(tree, refs[len(ins) + len(outs) :])
        copies = {name: where.copy(named[name], held_refs[name], sems[name]) for name, where in late.items()}
        for name, ref in own.items():
            named[name] = types.SimpleNamespace(**ref) if isinstance(ref, dict) else ref
        named.update(held_refs)
        for name, (_, where) in ins.items():
            if isinstance(where, Row):
                named[name] = named[name].at[where.layer : where.layer + 1]
        s = pl.program_id(0)

        @pl.when(s == 0)
        def _():
            for copy in copies.values():
                copy.start()

        def arrived(step, *names):
            @pl.when(s == step)
            def _():
                for name in names:
                    copies[name].wait()

        body(types.SimpleNamespace(arrived=arrived, **named), s)

    results = pl.pallas_call(
        kernel,
        grid=(steps,),
        in_specs=[spec(a.shape, w, True) for a, w in ins.values()],
        out_specs=[spec(shape, w, False) for shape, _, w in outs.values()],
        out_shape=[jax.ShapeDtypeStruct(shape, dtype) for shape, dtype, _ in outs.values()],
        scratch_shapes=flat,
        name=owner.__name__,
        compiler_params=pltpu.CompilerParams(
            collective_id=collective_id, has_side_effects=True, vmem_limit_bytes=vmem << 20
        ),
    )(*[a for a, _ in ins.values()])
    return types.SimpleNamespace(**dict(zip(outs, results)))


def at_chunk(s, schedule, work):
    rate, lag, count = schedule
    moved = s - lag
    here = (moved >= 0) & (moved < rate * count)
    if rate > 1:
        here = here & (lax.rem(moved, rate) == 0)

    @pl.when(here)
    def _():
        work(moved // rate if rate > 1 else moved)


def enter(devices):
    barrier = pltpu.get_barrier_semaphore()
    count = 0
    for device, exists in devices:
        if exists is True:
            pl.semaphore_signal(barrier, inc=1, device_id=device, device_id_type=MESH)
            count = count + 1
        else:

            @pl.when(exists)
            def _():
                pl.semaphore_signal(barrier, inc=1, device_id=device, device_id_type=MESH)

            count = count + jnp.where(exists, 1, 0)
    pl.semaphore_wait(barrier, count)


class LineSum:
    def __init__(self, refs, x=None):
        self.x, self.land = refs.x if x is None else x, refs.land
        self.send_sem, self.land_sem, self.out_sem = refs.send, refs.arrive, refs.out
        self.pieces = self.send_sem.shape[0]
        self.rows = self.x.shape[0] // self.pieces
        n = lax.axis_size("tensor")
        z = lax.axis_index("tensor")
        half = n // 2
        self.middle = (z == half - 1) | (z == half)
        self.has_outer = (z > 0) & (z < n - 1)
        self.inner = jnp.where(z < half, z + 1, z - 1)
        self.outer = jnp.clip(jnp.where(z < half, z - 1, z + 1), 0, n - 1)
        self.slot = jnp.where(self.middle, 1, 0)

    @staticmethod
    def scratch(rows, width, pieces, own=True):
        held = dict(x=pltpu.VMEM((rows, width), BF)) if own else {}
        return held | dict(
            land=pltpu.VMEM((2, rows, width), BF),
            send=pltpu.SemaphoreType.DMA((pieces,)),
            arrive=pltpu.SemaphoreType.DMA((2, pieces)),
            out=pltpu.SemaphoreType.DMA((pieces,)),
        )

    def neighbours(self):
        return [({"tensor": self.inner}, True), ({"tensor": self.outer}, self.has_outer)]

    def at(self, j, rows=None):
        rows = rows or self.rows
        return pl.ds(pl.multiple_of(j * rows, rows), rows)

    def inward(self, source, j, slot):
        return pltpu.make_async_remote_copy(
            source.at[self.at(j)], self.land.at[slot, self.at(j)], self.send_sem.at[j], self.land_sem.at[slot, j],
            device_id={"tensor": self.inner}, device_id_type=MESH)

    def outward(self, j):
        return pltpu.make_async_remote_copy(
            self.land.at[1, self.at(j)], self.land.at[1, self.at(j)], self.out_sem.at[j], self.land_sem.at[1, j],
            device_id={"tensor": self.outer}, device_id_type=MESH)

    def put(self, c, value):
        rows = value.shape[0]
        self.x[self.at(c, rows), :] = value.astype(BF)
        self.push(c, rows)

    def push(self, c, rows):
        @pl.when(jnp.logical_not(self.has_outer))
        def _():
            for i in range(rows // self.rows):
                self.inward(self.x, c * (rows // self.rows) + i, self.slot).start()

    def add(self, j, source, slot):
        self.land[slot, self.at(j), :] = (
            source[self.at(j), :].astype(F32) + self.land[slot, self.at(j), :].astype(F32)
        ).astype(BF)

    def relay(self, j):
        @pl.when(self.has_outer)
        def _():
            self.inward(self.x, j, 0).wait_recv()
            self.add(j, self.x, 0)
            self.inward(self.land.at[0], j, self.slot).start()

    def meet(self, j):
        @pl.when(self.middle)
        def _():
            self.inward(self.x, j, 1).wait_recv()

            @pl.when(self.has_outer)
            def _():
                self.add(j, self.land.at[0], 1)
                self.outward(j).start()

            @pl.when(jnp.logical_not(self.has_outer))
            def _():
                self.add(j, self.x, 1)

    def total(self, c, rows):
        @pl.when(jnp.logical_not(self.middle))
        def _():
            for i in range(rows // self.rows):
                j = c * (rows // self.rows) + i
                self.inward(self.x, j, 1).wait_recv()

                @pl.when(self.has_outer)
                def _():
                    self.outward(j).start()

        return self.land[1, self.at(c, rows), :].astype(F32)

    def finish(self):
        @pl.when(self.has_outer)
        def _():
            @pl.loop(0, self.pieces)
            def _(j):
                self.inward(self.land.at[0], j, self.slot).wait_send()
                self.outward(j).wait_send()

        @pl.when(jnp.logical_not(self.has_outer))
        def _():
            @pl.loop(0, self.pieces)
            def _(j):
                self.inward(self.x, j, self.slot).wait_send()


class KeyValueSend:
    def __init__(self, refs, reach, stretch):
        self.held, self.zeros, self.window = refs.kv.held, refs.kv.zeros, refs.window
        self.copy_sem, self.send_sem, self.land_sem = refs.kv.copy, refs.kv.send, refs.kv.land
        self.chunks = self.copy_sem.shape[0]
        self.rows = self.held.shape[0] // self.chunks
        self.reach, self.stretch = reach, stretch
        self.place = lax.axis_index("seq")
        self.count = lax.axis_size("seq")

    @staticmethod
    def scratch(rows, width, chunks, reach):
        held = max(reach, 1)
        return dict(
            held=pltpu.VMEM((rows, width), BF),
            zeros=pltpu.VMEM((rows // chunks, width), BF),
            copy=pltpu.SemaphoreType.DMA((chunks,)),
            send=pltpu.SemaphoreType.DMA((held, chunks)),
            land=pltpu.SemaphoreType.DMA((held, chunks)),
        )

    def neighbours(self):
        found = []
        for back in range(1, self.reach + 1):
            found.append(({"seq": jnp.minimum(self.place + back, self.count - 1)}, self.place + back < self.count))
            found.append(({"seq": jnp.maximum(self.place - back, 0)}, self.place >= back))
        return found

    def at(self, c):
        return pl.ds(pl.multiple_of(c * self.rows, self.rows), self.rows)

    def there(self, back, c):
        per = self.stretch // self.rows
        chunk = ((c // per) * (self.reach + 1) + self.reach - back) * per + lax.rem(c, per)
        return self.window.at[self.at(chunk)]

    def own(self, c):
        return pltpu.make_async_copy(self.held.at[self.at(c)], self.there(0, c), self.copy_sem.at[c])

    def blank(self, back, c):
        return pltpu.make_async_copy(self.zeros, self.there(back, c), self.land_sem.at[back - 1, c])

    def remote(self, back, c):
        return pltpu.make_async_remote_copy(
            self.held.at[self.at(c)], self.there(back, c), self.send_sem.at[back - 1, c],
            self.land_sem.at[back - 1, c],
            device_id={"seq": jnp.minimum(self.place + back, self.count - 1)}, device_id_type=MESH)

    def start(self):
        self.zeros[...] = jnp.zeros_like(self.zeros)

    def send(self, c):
        self.own(c).start()
        for back in range(1, self.reach + 1):

            @pl.when(self.place + back < self.count)
            def _():
                self.remote(back, c).start()

            @pl.when(self.place < back)
            def _():
                self.blank(back, c).start()

    def finish(self):
        @pl.loop(0, self.chunks)
        def _(c):
            self.own(c).wait()
            for back in range(1, self.reach + 1):

                @pl.when(self.place + back < self.count)
                def _():
                    self.remote(back, c).wait_send()

                @pl.when(self.place >= back)
                def _():
                    self.remote(back, c).wait_recv()

                @pl.when(self.place < back)
                def _():
                    self.blank(back, c).wait()


class KeyValueReturn:
    def __init__(self, refs, reach):
        self.prev, self.land = refs.d_prev, refs.kr.land
        self.send_sem, self.land_sem = refs.kr.send, refs.kr.arrive
        self.chunks = self.send_sem.shape[1]
        self.rows = self.land.shape[2] // self.chunks
        self.reach = reach
        self.place = lax.axis_index("seq")
        self.count = lax.axis_size("seq")

    @staticmethod
    def scratch(rows, width, chunks, reach):
        held = max(reach, 1)
        return dict(
            land=pltpu.VMEM((held, 2, rows, width), BF),
            send=pltpu.SemaphoreType.DMA((held, chunks)),
            arrive=pltpu.SemaphoreType.DMA((held, chunks)),
        )

    neighbours = KeyValueSend.neighbours
    at = KeyValueSend.at

    def copy(self, back, c):
        return pltpu.make_async_remote_copy(
            self.prev.at[self.reach - back, :, self.at(c)], self.land.at[back - 1, :, self.at(c)],
            self.send_sem.at[back - 1, c], self.land_sem.at[back - 1, c],
            device_id={"seq": jnp.maximum(self.place - back, 0)}, device_id_type=MESH)

    def start(self):
        for back in range(1, self.reach + 1):

            @pl.when(self.place >= back)
            def _():
                @pl.loop(0, self.chunks)
                def _(c):
                    self.copy(back, c).start()

    def add(self, own, c):
        for back in range(1, self.reach + 1):
            exists = self.place + back < self.count

            @pl.when(exists)
            def _():
                self.copy(back, c).wait_recv()

            own = own + jnp.where(exists, self.land[back - 1, :, self.at(c), :].astype(F32), 0.0)
        return own

    def finish(self):
        for back in range(1, self.reach + 1):

            @pl.when(self.place >= back)
            def _():
                @pl.loop(0, self.chunks)
                def _(c):
                    self.copy(back, c).wait_send()


def device_bit(axis):
    name, b = axis
    return lax.rem(lax.axis_index(name) // (1 << b), 2)


def device_partner(axis):
    name, b = axis
    return {name: lax.axis_index(name) + (1 - 2 * device_bit(axis)) * (1 << b)}


def bits_of(name):
    return lax.axis_size(name).bit_length() - 1


def block_axes():
    return [(name, b) for name in ("dp", "seq") for b in reversed(range(bits_of(name)))]


class Scatter:
    def __init__(self, refs, swapped):
        self.axes = block_axes()
        phases = len(self.axes)
        near = [k for k in range(phases) if self.axes[k][0] == "seq"][::-1]
        far = [k for k in range(phases) if self.axes[k][0] == "dp"]
        self.order = near + (far if swapped else far[::-1])
        self.buffer, self.lands = refs.held, refs.lands
        self.send_sem, self.land_sem = refs.send, refs.arrive

    @staticmethod
    def scratch(rows, width):
        phases = len(block_axes())
        return dict(
            held=pltpu.VMEM((2,) * phases + (rows, width), BF),
            lands=[pltpu.VMEM((2,) * (phases - k - 1) + (rows, width), BF) for k in range(phases)],
            send=pltpu.SemaphoreType.DMA((phases,)),
            arrive=pltpu.SemaphoreType.DMA((phases,)),
        )

    def neighbours(self):
        return [(device_partner(axis), True) for axis in self.axes]

    def put(self, block, columns, value):
        phases = len(self.axes)
        place = tuple(lax.rem(block // (1 << (phases - 1 - k)), 2) for k in range(phases))
        self.buffer[place + (slice(None), columns)] = value.astype(BF)

    def view(self, k, mine):
        index = [slice(None)] * len(self.axes)
        for earlier in self.order[:k]:
            index[earlier] = device_bit(self.axes[earlier])
        bit = device_bit(self.axes[self.order[k]])
        index[self.order[k]] = bit if mine else 1 - bit
        return tuple(index)

    def copy(self, k):
        return pltpu.make_async_remote_copy(
            self.buffer.at[self.view(k, False)], self.lands[k], self.send_sem.at[k], self.land_sem.at[k],
            device_id=device_partner(self.axes[self.order[k]]), device_id_type=MESH)

    def send(self, k):
        self.copy(k).start()

    def fold(self, k, store=None):
        self.copy(k).wait_recv()
        index = self.view(k, True)
        free = [i for i, v in enumerate(index) if isinstance(v, slice)]
        for j in range(1 << len(free)):
            place = [(j >> (len(free) - 1 - i)) & 1 for i in range(len(free))]
            here = list(index)
            for i, axis in enumerate(free):
                here[axis] = place[i]
            here = tuple(here)
            total = self.buffer[here].astype(F32) + self.lands[k][tuple(place)].astype(F32)
            if store is None:
                self.buffer[here] = total.astype(BF)
            else:
                store(total)

    def finish(self):
        for k in range(len(self.axes)):
            self.copy(k).wait_send()


class Butterfly:
    def __init__(self, refs):
        self.axes = [(name, b) for name in ("seq", "dp", "tensor") for b in range(bits_of(name))]
        self.held, self.land = refs.held, refs.land
        self.send_sem, self.land_sem = refs.send, refs.arrive

    @staticmethod
    def scratch(shape):
        phases = bits_of("seq") + bits_of("dp") + bits_of("tensor")
        return dict(
            held=pltpu.VMEM((phases + 1,) + shape, F32),
            land=pltpu.VMEM((phases,) + shape, F32),
            send=pltpu.SemaphoreType.DMA((phases,)),
            arrive=pltpu.SemaphoreType.DMA((phases,)),
        )

    def neighbours(self):
        return [(device_partner(axis), True) for axis in self.axes]

    def copy(self, k):
        return pltpu.make_async_remote_copy(
            self.held.at[k], self.land.at[k], self.send_sem.at[k], self.land_sem.at[k],
            device_id=device_partner(self.axes[k]), device_id_type=MESH)

    def put(self, value):
        self.held[0] = value
        self.copy(0).start()

    def fold(self, k):
        self.copy(k).wait_recv()
        self.held[k + 1] = self.held[k] + self.land[k]
        if k + 1 < len(self.axes):
            self.copy(k + 1).start()

    def total(self):
        return self.held[len(self.axes)]

    def finish(self):
        for k in range(len(self.axes)):
            self.copy(k).wait_send()


def norm_parts(value):
    inverse = lax.rsqrt(jnp.mean(value * value, -1, keepdims=True) + EPS)
    return value * inverse, inverse


def norm_back(grad, gain, hat, inverse):
    scaled = grad * gain
    inner = jnp.mean(scaled * hat, -1, keepdims=True)
    return inverse * (scaled - hat * inner)


def row_sums(value):
    return jnp.sum(value, 0, keepdims=True)


def heads_of(value):
    return [value[:, h * HEAD : (h + 1) * HEAD] for h in range(value.shape[1] // HEAD)]


def rope(value, cosine, signed_sine):
    return value * cosine + pltpu.roll(value, HEAD // 2, 1) * signed_sine


def rope_back(grad, cosine, signed_sine):
    return grad * cosine - pltpu.roll(grad, HEAD // 2, 1) * signed_sine


def attend(r, c, stretch):
    rows, span = r.queries_in.shape[0], r.window_in.shape[0] // (r.low.shape[1] // stretch)
    offset = span - stretch
    per = stretch // rows
    length = min(WINDOW + rows, span)
    q_start = offset + lax.rem(c, per) * rows
    start = jnp.clip(q_start + rows - length, 0, span - length)
    here = pl.ds(pl.multiple_of((c // per) * span + start, rows), length)
    group = r.queries_in.shape[1] * 2 // r.window_in.shape[1]
    low = r.low[:, pl.ds(pl.multiple_of(c * rows, rows), rows)].astype(F32)
    low = jnp.broadcast_to(low, (HEAD, rows)).T[:, :1]
    key_index = (start + lax.broadcasted_iota(jnp.int32, (rows, length), 1)).astype(F32)
    q_index = (q_start + lax.broadcasted_iota(jnp.int32, (rows, 1), 0)).astype(F32)
    mask = (key_index >= low) & (key_index <= q_index)
    mask = jnp.concatenate([mask] * group, 0)
    queries = heads_of(r.queries_in[...])
    kv_heads = len(queries) // group
    outs = []
    for g in range(kv_heads):
        keys = r.window_in[here, g * HEAD : (g + 1) * HEAD]
        values = r.window_in[here, (kv_heads + g) * HEAD : (kv_heads + g + 1) * HEAD]
        s = dot(jnp.concatenate(queries[g * group : (g + 1) * group], 0), keys, NT) * (SCALE * LOG2E)
        p = jnp.where(mask, jnp.exp2(s), 0.0)
        part = p[:, :HEAD]
        for k in range(1, length // HEAD):
            part = part + p[:, k * HEAD : (k + 1) * HEAD]
        total = jnp.sum(part, 1, keepdims=True)
        o = (dot(p.astype(BF), values) / total).astype(BF)
        log_total = jnp.broadcast_to(jnp.log2(total), (group * rows, HEAD))
        for h in range(group):
            outs.append(o[h * rows : (h + 1) * rows])
            r.lse[g, h : h + 1, :] = log_total[h * rows : (h + 1) * rows].T[0:1, :]
    context = jnp.concatenate(outs, 1)
    r.context[...] = context
    return context


def attend_ins(a, low, when):
    return dict(
        queries_in=(a.queries, when),
        window_in=(a.window, Late()),
        low=(low, WHOLE),
    )


def attend_outs(a, when):
    kv_heads = a.window.shape[1] // (2 * HEAD)
    rows, width = a.queries.shape
    shape = (kv_heads, width // (kv_heads * HEAD), rows)
    return dict(
        context=((rows, width), BF, when),
        lse=(shape, F32, pl.BlockSpec(shape[:2] + (rows // when[2],), lambda s: (0, 0, chunk_index(when, s)))),
    )


def project(r, hidden, kv, c):
    hat, _ = norm_parts(hidden)
    low = (hat * r.attn_gain[...].astype(F32)).astype(BF)
    r.attn_low[...] = low
    q_raw = dot(low, r.w_q[...])
    k_raw = dot(low, r.w_k[...])
    values = dot(low, r.w_v[...])
    r.raw[...] = jnp.concatenate([q_raw, k_raw], 1)
    cosine, sine = r.tables[:, :HEAD], r.tables[:, HEAD:]

    def turned(raw, gain):
        return jnp.concatenate(
            [rope(norm_parts(u)[0] * gain, cosine, sine).astype(BF) for u in heads_of(raw)], 1)

    r.queries[...] = turned(q_raw, r.q_gain[...].astype(F32))
    kv.held[kv.at(c), :] = jnp.concatenate([turned(k_raw, r.k_gain[...].astype(F32)), values.astype(BF)], 1)
    kv.send(c)


def project_outs(rows, width, w, stretch, reach, when):
    q_width, k_width = w.w_q.shape[2], w.w_k.shape[2]
    return dict(
        attn_low=((rows, width), BF, when),
        raw=((rows, q_width + k_width), F32, when),
        queries=((rows, q_width), BF, when),
        window=((rows // stretch * (reach + 1) * stretch, k_width + w.w_v.shape[2]), BF, HBM),
    )


def project_ins(w, layer, tables, when):
    def weight(array):
        if tables is not None:
            return array, Late(layer)
        shape = array.shape[1:]
        return array, pl.BlockSpec((None,) + shape, lambda s: (layer, 0, 0), pipeline_mode=pl.Buffered(1))

    return dict(
        attn_gain=(w.attn_gain, Row(layer)),
        w_q=weight(w.w_q),
        w_k=weight(w.w_k),
        w_v=weight(w.w_v),
        q_gain=(w.q_gain, Row(layer)),
        k_gain=(w.k_gain, Row(layer)),
    ) | ({} if tables is None else dict(tables=(tables, when)))


def mlp_gates(r, low):
    gate = dot(low, r.w_gate[...])
    up = dot(low, r.w_up[...])
    sigma = jax.nn.sigmoid(gate)
    return gate, up, sigma


def mlp_back(r, g_low, gate, up, sigma):
    d_act = dot(g_low, r.w_down[...], NT)
    d_gate = (d_act * up * sigma * (1.0 + gate * (1.0 - sigma))).astype(BF)
    d_up = (d_act * gate * sigma).astype(BF)
    return jnp.concatenate([d_gate, d_up], 1), dot(d_gate, r.w_gate[...], NT) + dot(d_up, r.w_up[...], NT)


def first_projection(hidden, segments, positions, w, stretch, reach, chunks, collective_id):
    rows, width = hidden.shape
    when = (1, 0, chunks)
    kv_width = w.w_k.shape[2] + w.w_v.shape[2]

    held = max(reach, 1)
    seqs = rows // stretch

    def body(r, s):
        kv = KeyValueSend(r, reach, stretch)

        def documents(back):
            return pltpu.make_async_remote_copy(
                r.segments, r.docs.at[back - 1], r.doc_send.at[back - 1], r.doc_land.at[back - 1],
                device_id={"seq": jnp.minimum(kv.place + back, kv.count - 1)}, device_id_type=MESH)

        @pl.when(s == 0)
        def _():
            r.docs[...] = jnp.full_like(r.docs, -1)
            enter(kv.neighbours())
            kv.start()
            for back in range(1, reach + 1):

                @pl.when(kv.place + back < kv.count)
                def _():
                    documents(back).start()

        angle = jnp.broadcast_to(r.positions[...].astype(F32), (HEAD, rows // chunks)).T * r.frequency[...]
        lane = lax.broadcasted_iota(jnp.int32, angle.shape, 1)
        sine = jnp.sin(angle)
        r.tables[...] = jnp.concatenate([jnp.cos(angle), jnp.where(lane < HEAD // 2, -sine, sine)], 1)
        project(r, r.hidden[...].astype(F32), kv, s)

        @pl.when(s == chunks - 1)
        def _():
            kv.finish()
            for back in range(1, reach + 1):

                @pl.when(kv.place + back < kv.count)
                def _():
                    documents(back).wait_send()

                @pl.when(kv.place >= back)
                def _():
                    documents(back).wait_recv()

            for q in range(seqs):
                here = slice(q * stretch, (q + 1) * stretch)
                own = r.segments[:, here]
                docs = [r.docs[back - 1, :, here] for back in range(1, reach + 1)]

                def first_of(document):
                    counts = [jnp.sum((d < document).astype(jnp.int32), 1, keepdims=True) for d in docs + [own]]
                    return functools.reduce(jnp.add, counts)

                low = jnp.broadcast_to(first_of(0), own.shape)
                for document in range(1, 4):
                    low = jnp.where(own >= document, first_of(document), low)
                index = lax.broadcasted_iota(jnp.int32, own.shape, 1)
                r.low[:, here] = jnp.maximum(low, reach * stretch + index - (WINDOW - 1))

    frequency = (THETA ** (-np.arange(0, HEAD, 2) / HEAD)).astype(np.float32)
    return step_kernel(
        first_projection, body, chunks,
        dict(
            hidden=(hidden, when),
            segments=(segments.reshape(1, rows), WHOLE),
            positions=(
                positions.reshape(1, rows), pl.BlockSpec((1, rows // chunks), lambda s: (0, chunk_index(when, s)))),
            frequency=(jnp.asarray(np.concatenate([frequency, frequency])[None]), WHOLE),
        )
        | project_ins(w, 0, None, when),
        project_outs(rows, width, w, stretch, reach, when)
        | dict(
            tables=((rows, 2 * HEAD), F32, when),
            low=((1, rows), jnp.int32, WHOLE),
        ),
        dict(
            kv=KeyValueSend.scratch(rows, kv_width, chunks, reach),
            docs=pltpu.VMEM((held, 1, rows), jnp.int32),
            doc_send=pltpu.SemaphoreType.DMA((held,)),
            doc_land=pltpu.SemaphoreType.DMA((held,)),
        ),
        collective_id)


def between_forward(a, low, w, layer, tables, stretch, reach, chunks, collective_id):
    hidden = a.hidden
    rows, width = hidden.shape
    kv_width = w.w_k.shape[2] + w.w_v.shape[2]
    ff = w.w_gate.shape[2]
    pieces = chunks * FINE
    first, second, third = (FINE, 0, chunks), (FINE, 8, chunks), (FINE, 17, chunks)
    steps = FINE * (chunks - 1) + third[1] + 1
    chunk = rows // chunks

    def body(r, s):
        kv = KeyValueSend(r, reach, stretch)
        attn, mlp = LineSum(r.attn), LineSum(r.mlp)

        @pl.when(s == 0)
        def _():
            enter(attn.neighbours() + kv.neighbours())
            kv.start()

        def send_attn(c):
            attn.put(c, dot(attend(r, c, stretch), r.w_o[...]))

        def feed_forward(c):
            middle = r.hidden[...].astype(F32) + attn.total(c, chunk)
            r.hidden_mid[...] = middle
            r.mid_held[attn.at(c, chunk), :] = middle
            hat, _ = norm_parts(middle)
            low = (hat * r.mlp_gain[...].astype(F32)).astype(BF)
            r.mlp_low[...] = low
            gate, up, sigma = mlp_gates(r, low)
            r.gates[...] = jnp.concatenate([gate, up], 1)
            act = (gate * sigma * up).astype(BF)
            r.act[...] = act
            mlp.put(c, dot(act, r.w_down[...]))

        def next_layer(c):
            hidden_next = r.mid_held[mlp.at(c, chunk), :] + mlp.total(c, chunk)
            r.hidden_next[...] = hidden_next
            project(r, hidden_next, kv, c)

        r.arrived(0, "window_in", "w_o")
        at_chunk(s, first, send_attn)
        at_chunk(s, (1, 2, pieces), attn.relay)
        at_chunk(s, (1, 4, pieces), attn.meet)
        r.arrived(second[1], *MLP_WEIGHTS)
        at_chunk(s, second, feed_forward)
        at_chunk(s, (1, 12, pieces), mlp.relay)
        at_chunk(s, (1, 14, pieces), mlp.meet)
        r.arrived(third[1], *QKV_WEIGHTS)
        at_chunk(s, third, next_layer)

        @pl.when(s == steps - 1)
        def _():
            attn.finish()
            mlp.finish()
            kv.finish()

    return step_kernel(
        between_forward, body, steps,
        attend_ins(a, low, first)
        | dict(
            w_o=(w.w_o, Late(layer)),
            hidden=(hidden, second),
            mlp_gain=(w.mlp_gain, Row(layer)),
            w_gate=(w.w_gate, Late(layer)),
            w_up=(w.w_up, Late(layer)),
            w_down=(w.w_down, Late(layer)),
        )
        | project_ins(w, layer + 1, tables, third),
        attend_outs(a, first)
        | dict(
            hidden_mid=((rows, width), F32, second),
            mlp_low=((rows, width), BF, second),
            gates=((rows, 2 * ff), F32, second),
            act=((rows, ff), BF, second),
            hidden_next=((rows, width), F32, third),
        )
        | project_outs(rows, width, w, stretch, reach, third),
        dict(
            attn=LineSum.scratch(rows, width, pieces),
            mlp=LineSum.scratch(rows, width, pieces),
            kv=KeyValueSend.scratch(rows, kv_width, chunks, reach),
            mid_held=pltpu.VMEM((rows, width), F32),
        ),
        collective_id)


def turn_around(a, low, cotangent, w, layer, stretch, chunks, collective_id):
    hidden = a.hidden
    rows, width = hidden.shape
    ff = w.w_gate.shape[2]
    pieces = chunks * FINE
    first, second, third = (FINE, 0, chunks), (FINE, 9, chunks), (FINE, 17, chunks)
    steps = FINE * (chunks - 1) + third[1] + 1
    chunk = rows // chunks

    def body(r, s):
        attn, back = LineSum(r.attn), LineSum(r.back)

        @pl.when(s == 0)
        def _():
            enter(attn.neighbours())
            r.gain_grad[...] = jnp.zeros_like(r.gain_grad)

        def send_attn(c):
            attn.put(c, dot(attend(r, c, stretch), r.w_o[...]))

        def feed_forward(c):
            middle = r.hidden[...] + attn.total(c, chunk)
            r.hidden_mid[...] = middle
            r.mid_held[attn.at(c, chunk), :] = middle
            hat, _ = norm_parts(middle)
            low = (hat * r.mlp_gain[...].astype(F32)).astype(BF)
            r.mlp_low[...] = low
            gate, up, sigma = mlp_gates(r, low)
            d_gates, part = mlp_back(r, r.cotangent[...], gate, up, sigma)
            back.put(c, part)
            r.d_gates[...] = d_gates
            act = (gate * sigma * up).astype(BF)
            r.act[...] = act
            part = dot(act, r.w_down[...]).astype(BF)

            @pl.when(c < chunks // 2)
            def _():
                r.lower_part[...] = part

            @pl.when(c >= chunks // 2)
            def _():
                r.upper_part[...] = part

        def middle_grad(c):
            hat, inverse = norm_parts(r.mid_held[back.at(c, chunk), :])
            d_in = back.total(c, chunk)
            r.gain_grad[0:1, :] += row_sums(d_in * hat)
            g_mid = r.cotangent_late[...].astype(F32) + norm_back(d_in, r.mlp_gain[...].astype(F32), hat, inverse)
            r.g_mid[...] = g_mid
            mid_low = g_mid.astype(BF)
            r.mid_low[...] = mid_low
            r.d_context[...] = dot(mid_low, r.w_o[...], NT).astype(BF)

        r.arrived(0, "window_in", "w_o")
        at_chunk(s, first, send_attn)
        at_chunk(s, (1, 2, pieces), attn.relay)
        at_chunk(s, (1, 4, pieces), attn.meet)
        r.arrived(second[1], *MLP_WEIGHTS)
        at_chunk(s, second, feed_forward)
        at_chunk(s, (1, 12, pieces), back.relay)
        at_chunk(s, (1, 14, pieces), back.meet)
        at_chunk(s, third, middle_grad)

        @pl.when(s == steps - 1)
        def _():
            attn.finish()
            back.finish()

    return step_kernel(
        turn_around, body, steps,
        attend_ins(a, low, first)
        | dict(
            w_o=(w.w_o, Late(layer)),
            hidden=(hidden, second),
            cotangent=(cotangent, second),
            cotangent_late=(cotangent, third),
            mlp_gain=(w.mlp_gain, Row(layer)),
            w_gate=(w.w_gate, Late(layer)),
            w_up=(w.w_up, Late(layer)),
            w_down=(w.w_down, Late(layer)),
        ),
        attend_outs(a, first)
        | dict(
            mlp_low=((rows, width), BF, second),
            act=((rows, ff), BF, second),
            hidden_mid=((rows, width), F32, second),
            lower_part=((rows // 2, width), BF, (FINE, second[1], chunks // 2)),
            upper_part=((rows // 2, width), BF, (FINE, second[1] + FINE * (chunks // 2), chunks // 2)),
            d_gates=((rows, 2 * ff), BF, second),
            g_mid=((rows, width), F32, third),
            mid_low=((rows, width), BF, third),
            d_context=(a.queries.shape, BF, third),
            gain_grad=((8, width), F32, WHOLE),
        ),
        dict(
            attn=LineSum.scratch(rows, width, pieces),
            back=LineSum.scratch(rows, width, pieces),
            mid_held=pltpu.VMEM((rows, width), F32),
        ),
        collective_id)


def attention_backward(a, d_context, low, part, quarter, stretch, pieces, collective_id):
    rows = a.queries.shape[0]
    kv_heads = a.window.shape[1] // (2 * HEAD)
    width = a.queries.shape[1] // kv_heads
    group = width // HEAD
    qb = min(2 * CHUNK, stretch)
    count = stretch // qb
    seqs = rows // stretch
    span = a.window.shape[0] // seqs
    reach = span // stretch - 1
    held = max(reach, 1)
    offset = reach * stretch
    length = min(WINDOW + qb, span)
    steps = seqs * kv_heads * count

    def places(s):
        return s // (kv_heads * count), lax.rem(s // count, kv_heads), lax.rem(s, count)

    def block(shape, index):
        return pl.BlockSpec(shape, lambda s: index(*places(s)))

    def body(r, s):
        seq, g, i = places(s)
        line = LineSum(r.line, r.part)
        q_start = i * qb + offset
        start = jnp.clip(q_start + qb - length, 0, span - length)
        here = pl.ds(pl.multiple_of(start, HEAD), length)

        @pl.when(s == 0)
        def _():
            enter(line.neighbours())
            line.push(0, line.x.shape[0])

        @pl.when(i == 0)
        def _():
            r.d_keys[...] = jnp.zeros_like(r.d_keys)
            r.d_values[...] = jnp.zeros_like(r.d_values)

        for j in range(pieces):

            @pl.when(s == min(2 + j // 2, steps - 1))
            def _():
                line.relay(j)

        for j in range(pieces):

            @pl.when(s == min(4 + j // 2, steps - 1))
            def _():
                line.meet(j)

        def stack(ref):
            return jnp.concatenate([ref[:, h * HEAD : (h + 1) * HEAD] for h in range(group)], 0)

        queries = stack(r.queries)
        d_out = stack(r.d_context)
        lse = jnp.concatenate([r.lse[h : h + 1, :] for h in range(group)], 1)
        product = d_out.astype(F32) * stack(r.context).astype(F32)
        delta = jnp.sum(product.T, 0, keepdims=True)
        keys = r.keys[here, :]
        values = r.values[here, :]
        key_index = start + lax.broadcasted_iota(jnp.int32, (length, qb), 0)
        q_index = q_start + lax.broadcasted_iota(jnp.int32, (1, qb), 1)
        mask = (key_index >= r.low[...]) & (key_index <= q_index)
        mask = jnp.concatenate([mask] * group, 1)
        scores = dot(keys, queries, NT) * (SCALE * LOG2E) - lse
        p = jnp.where(mask, jnp.exp2(scores), 0.0)
        ds = (p * (dot(values, d_out, NT) - delta)).astype(BF)
        r.d_values[here, :] += dot(p.astype(BF), d_out)
        r.d_keys[here, :] += dot(ds, queries)
        dq = (dot(keys, ds, TN) * SCALE).T
        for h in range(group):
            r.d_q[:, h * HEAD : (h + 1) * HEAD] = dq[h * qb : (h + 1) * qb]

        @pl.when(i == count - 1)
        def _():
            r.d_own[0] = r.d_keys[offset:, :] * SCALE
            r.d_own[1] = r.d_values[offset:, :]
            for j in range(reach):
                r.d_prev[j, 0] = (r.d_keys[j * stretch : (j + 1) * stretch, :] * SCALE).astype(BF)
                r.d_prev[j, 1] = r.d_values[j * stretch : (j + 1) * stretch, :].astype(BF)

        @pl.when(s == steps - 1)
        def _():
            r.total[...] = line.total(0, line.x.shape[0]).astype(BF)
            line.finish()

    by_rows = block((qb, width), lambda seq, g, i: (seq * count + i, g))
    part_rows = part.shape[0] // 2
    return step_kernel(
        attention_backward, body, steps,
        dict(
            low=(low, block((1, qb), lambda seq, g, i: (0, seq * count + i))),
            lse=(a.lse, block((None, group, qb), lambda seq, g, i: (g, 0, seq * count + i))),
            queries=(a.queries, by_rows),
            d_context=(d_context, by_rows),
            context=(a.context, by_rows),
            keys=(a.window, block((span, HEAD), lambda seq, g, i: (seq, g))),
            values=(a.window, block((span, HEAD), lambda seq, g, i: (seq, kv_heads + g))),
            part=(part, pl.BlockSpec(
                (part_rows, part.shape[1]), lambda s: (quarter, 0), pipeline_mode=pl.Buffered(1))),
        ),
        dict(
            d_q=(a.queries.shape, F32, by_rows),
            d_own=((2, rows, kv_heads * HEAD), F32, block((2, stretch, HEAD), lambda seq, g, i: (0, seq, g))),
            d_prev=(
                (held, 2, rows, kv_heads * HEAD), BF,
                block((held, 2, stretch, HEAD), lambda seq, g, i: (0, 0, seq, g))),
            total=((part_rows, part.shape[1]), BF, WHOLE),
        ),
        dict(
            line=LineSum.scratch(part_rows, part.shape[1], pieces, False),
            d_keys=pltpu.VMEM((span, HEAD), F32),
            d_values=pltpu.VMEM((span, HEAD), F32),
        ),
        collective_id)


def attention_grads(r, back, line, c):
    cosine, sine = r.tables[:, :HEAD], r.tables[:, HEAD:]
    both = back.add(r.d_own[...], c)

    def raw_back(grads, raws, gain):
        lows, gains = [], 0.0
        for grad, raw in zip(heads_of(grads), heads_of(raws)):
            grad = rope_back(grad, cosine, sine)
            hat, inverse = norm_parts(raw)
            gains = gains + row_sums(grad * hat)
            lows.append(norm_back(grad, gain, hat, inverse).astype(BF))
        return jnp.concatenate(lows, 1), gains

    q_width = r.d_q.shape[1]
    d_q, q_gain = raw_back(r.d_q[...], r.raw[:, :q_width], r.q_gain[...].astype(F32))
    d_k, k_gain = raw_back(both[0], r.raw[:, q_width:], r.k_gain[...].astype(F32))
    d_v = both[1].astype(BF)
    r.head_gain[0:1, 0:HEAD] += q_gain
    r.head_gain[0:1, HEAD : 2 * HEAD] += k_gain
    r.d_held[line.at(c, d_q.shape[0]), :] = jnp.concatenate([d_q, d_k, d_v], 1)
    part = dot(d_q, r.w_q[...], NT) + dot(d_k, r.w_k[...], NT) + dot(d_v, r.w_v[...], NT)
    line.put(c, part)
    return part


class WeightGrads:
    def __init__(self, r, plan):
        self.r = r
        self.plan = plan
        self.slabs = plan.slabs[2]
        self.late = Scatter(r.sc_q, False), Scatter(r.sc_kv, True)
        self.early = Scatter(r.sc_a, False), Scatter(r.sc_b, True)
        self.blocks = 1 << len(block_axes())

    @staticmethod
    def scratch(rows, width, q_width, k_width, ff):
        per = width // (1 << len(block_axes()))
        return dict(
            sc_a=Scatter.scratch(per, ff + q_width),
            sc_b=Scatter.scratch(per, 2 * ff),
            sc_q=Scatter.scratch(per, q_width),
            sc_kv=Scatter.scratch(per, 2 * k_width),
            d_held=pltpu.VMEM((rows, q_width + 2 * k_width), BF),
        )

    def neighbours(self):
        return self.late[0].neighbours()

    def put(self, scatter, slab, columns, value):
        per = self.blocks // self.slabs
        rows = value.shape[0] // per
        for j in range(per):
            scatter.put(slab * per + j, columns, value[j * rows : (j + 1) * rows])

    def mlp_slab(self, slab):
        r = self.r
        ff = r.act_all.shape[1]
        q_width = r.context_all.shape[1]
        both = dot(r.mlp_low_slab[...], r.d_gates_all[...], TN)
        self.put(self.early[0], slab, slice(0, ff), both[:, :ff])
        self.put(self.early[0], slab, slice(ff, ff + q_width), dot(r.mid_low_slab[...], r.context_all[...], TN))
        self.put(self.early[1], slab, slice(0, ff), both[:, ff:])
        self.put(self.early[1], slab, slice(ff, 2 * ff), dot(r.g_low_slab[...], r.act_all[...], TN))

    def qkv_slab(self, slab):
        r = self.r
        slab_width = r.attn_low_all.shape[1] // self.slabs
        q_width = r.d_q.shape[1]
        columns = pl.ds(pl.multiple_of(slab * slab_width, slab_width), slab_width)
        value = dot(r.attn_low_all[:, columns], r.d_held[...], TN)
        self.put(self.late[0], slab, slice(None), value[:, :q_width])
        self.put(self.late[1], slab, slice(None), value[:, q_width:])

    def each(self, scatters, work):
        for scatter in scatters:
            work(scatter)

    def store(self):
        r = self.r
        last = len(block_axes()) - 1
        ff = r.act_all.shape[1]
        k_width = r.grad_k.shape[1]

        def store_a(total):
            r.grad_gate[...] = total[:, :ff]
            r.grad_o[...] = total[:, ff:]

        def store_b(total):
            r.grad_up[...] = total[:, :ff]
            r.grad_down[...] = total[:, ff:]

        def store_q(total):
            r.grad_q[...] = total

        def store_kv(total):
            r.grad_k[...] = total[:, :k_width]
            r.grad_v[...] = total[:, k_width:]

        self.early[0].fold(last, store_a)
        self.early[1].fold(last, store_b)
        self.late[0].fold(last, store_q)
        self.late[1].fold(last, store_kv)

    def late_slabs(self, s):
        _, lag, count = self.plan.late_slabs
        self.r.arrived(lag, "attn_low_all")
        at_chunk(s, self.plan.late_slabs, self.qkv_slab)

        @pl.when(s == lag + count - 1)
        def _():
            self.each(self.late, lambda scatter: scatter.send(0))

    def run(self, s):
        rate, lag, count = self.plan.slabs
        self.r.arrived(lag, *GRAD_OPERANDS)
        at_chunk(s, self.plan.slabs, self.mlp_slab)

        @pl.when(s == lag + rate * (count - 1))
        def _():
            self.each(self.early, lambda scatter: scatter.send(0))

        for k in range(len(block_axes()) - 1):

            def move(scatter):
                scatter.fold(k)
                scatter.send(k + 1)

            @pl.when(s == self.plan.early(k))
            def _():
                self.each(self.early, move)

            @pl.when(s == self.plan.late(k))
            def _():
                self.each(self.late, move)

    def finish(self):
        self.each(self.early + self.late, lambda scatter: scatter.finish())


def slab_count(chunks):
    return min(4, max(1, chunks // 2))


def grads_ins(a, rows, width, when):
    slab = pl.BlockSpec((rows, width // when[2]), lambda s: (0, chunk_index(when, s)))
    return dict(
        mlp_low_slab=(a.mlp_low, slab),
        mid_low_slab=(a.mid_low, slab),
        g_low_slab=(a.g_low, slab),
        attn_low_all=(a.attn_low, Late()),
        d_gates_all=(a.d_gates, Late()),
        context_all=(a.context, Late()),
        act_all=(a.act, Late()),
    )


def grads_outs(width, q_width, k_width, ff):
    per = width // (1 << len(block_axes()))
    return dict(
        grad_q=((per, q_width), F32, WHOLE),
        grad_k=((per, k_width), F32, WHOLE),
        grad_v=((per, k_width), F32, WHOLE),
        grad_o=((per, q_width), F32, WHOLE),
        grad_gate=((per, ff), F32, WHOLE),
        grad_up=((per, ff), F32, WHOLE),
        grad_down=((per, ff), F32, WHOLE),
    )


def attention_grads_ins(a, w, layer, tables, when):
    rows, k_width = a.raw.shape[0], w.w_k.shape[2]
    own = pl.BlockSpec((2, rows // when[2], k_width), lambda s: (0, chunk_index(when, s), 0))
    return dict(
        d_q=(a.d_q, when),
        d_own=(a.d_own, own),
        d_prev=(a.d_prev, HBM),
        raw=(a.raw, when),
        tables=(tables, when),
        w_q=(w.w_q, Late(layer)),
        w_k=(w.w_k, Late(layer)),
        w_v=(w.w_v, Late(layer)),
        q_gain=(w.q_gain, Row(layer)),
        k_gain=(w.k_gain, Row(layer)),
        attn_gain=(w.attn_gain, Row(layer)),
    )


def between_backward(a, below, g_mid, w, layer, tables, reach, chunks, collective_id):
    rows, width = g_mid.shape
    q_width, k_width, ff = w.w_q.shape[2], w.w_k.shape[2], w.w_gate.shape[2]
    pieces = chunks * PIECES
    first, second, third = (PIECES, 0, chunks), (PIECES, 4, chunks), (PIECES, 10, chunks)
    steps = PIECES * (chunks - 1) + third[1] + 1
    chunk = rows // chunks
    after = PIECES * (chunks - 1) + 1
    plan = types.SimpleNamespace(
        slabs=(PIECES, 2, slab_count(chunks)),
        early=lambda k: min(after - 3 + 4 * k, steps - 2),
        late_slabs=(1, after, slab_count(chunks)),
        late=lambda k: min(after + slab_count(chunks) + 2 * k, steps - 2),
    )

    def body(r, s):
        back = KeyValueReturn(r, reach)
        attn, mlp = LineSum(r.attn), LineSum(r.mlp)
        grads = WeightGrads(r, plan)

        @pl.when(s == 0)
        def _():
            enter(attn.neighbours() + back.neighbours() + grads.neighbours())
            back.start()
            r.gain_grad[...] = jnp.zeros_like(r.gain_grad)
            r.head_gain[...] = jnp.zeros_like(r.head_gain)

        def send_attn(c):
            attention_grads(r, back, attn, c)

        def feed_forward(c):
            hat, inverse = norm_parts(r.hidden[...])
            d_in = attn.total(c, chunk)
            r.gain_grad[0:1, :] += row_sums(d_in * hat)
            g = r.g_above[...] + norm_back(d_in, r.attn_gain[...].astype(F32), hat, inverse)
            r.g_held[lax.rem(c, 4)] = g
            g_low = g.astype(BF)
            r.g_low[...] = g_low
            gate, up = r.gates[:, :ff], r.gates[:, ff:]
            d_gates, part = mlp_back(r, g_low, gate, up, jax.nn.sigmoid(gate))
            r.d_gates[...] = d_gates
            mlp.put(c, part)

        def middle_grad(c):
            hat, inverse = norm_parts(r.hidden_mid[...])
            d_in = mlp.total(c, chunk)
            r.gain_grad[1:2, :] += row_sums(d_in * hat)
            g_mid = r.g_held[lax.rem(c, 4)] + norm_back(d_in, r.mlp_gain[...].astype(F32), hat, inverse)
            r.g_mid[...] = g_mid
            mid_low = g_mid.astype(BF)
            r.mid_low[...] = mid_low
            r.d_context[...] = dot(mid_low, r.w_o[...], NT).astype(BF)

        r.arrived(first[1], *QKV_WEIGHTS)
        at_chunk(s, first, send_attn)
        grads.late_slabs(s)
        at_chunk(s, (1, 1, pieces), attn.relay)
        at_chunk(s, (1, 2, pieces), attn.meet)
        r.arrived(second[1], *MLP_WEIGHTS)
        at_chunk(s, second, feed_forward)
        at_chunk(s, (1, 6, pieces), mlp.relay)
        at_chunk(s, (1, 7, pieces), mlp.meet)
        r.arrived(third[1], "w_o")
        at_chunk(s, third, middle_grad)
        grads.run(s)

        @pl.when(s == steps - 1)
        def _():
            grads.store()
            attn.finish()
            mlp.finish()
            back.finish()
            grads.finish()

    return step_kernel(
        between_backward, body, steps,
        attention_grads_ins(a, w, layer, tables, first)
        | grads_ins(a, rows, width, plan.slabs)
        | dict(
            hidden=(a.hidden, second),
            g_above=(g_mid, second),
            gates=(below.gates, second),
            hidden_mid=(below.hidden_mid, third),
            mlp_gain=(w.mlp_gain, Row(layer - 1)),
            w_gate=(w.w_gate, Late(layer - 1)),
            w_up=(w.w_up, Late(layer - 1)),
            w_down=(w.w_down, Late(layer - 1)),
            w_o=(w.w_o, Late(layer - 1)),
        ),
        dict(
            g_low=((rows, width), BF, second),
            d_gates=((rows, 2 * ff), BF, second),
            g_mid=((rows, width), F32, third),
            mid_low=((rows, width), BF, third),
            d_context=((rows, q_width), BF, third),
            gain_grad=((8, width), F32, WHOLE),
            head_gain=((8, 2 * HEAD), F32, WHOLE),
        )
        | grads_outs(width, q_width, k_width, ff),
        dict(
            attn=LineSum.scratch(rows, width, pieces),
            mlp=LineSum.scratch(rows, width, pieces),
            kr=KeyValueReturn.scratch(rows, k_width, chunks, reach),
            **WeightGrads.scratch(rows, width, q_width, k_width, ff),
            g_held=pltpu.VMEM((4, rows // chunks, width), F32),
        ),
        collective_id)


def last_backward(a, top, quarters, above, w, tables, reach, chunks, collective_id):
    g_mid = above.g_mid
    rows, width = g_mid.shape
    q_width, k_width, ff = w.w_q.shape[2], w.w_k.shape[2], w.w_gate.shape[2]
    layer = 0
    pieces = chunks * PIECES
    pairs = max(1, chunks // 2)
    half = rows // 2
    half_pieces = pieces // 2
    out_chunk = min(rows // chunks, half // 2)
    out_count = rows // out_chunk
    first, second = (2, 2, pairs), (PIECES, 15, chunks)
    third = (PIECES * chunks // out_count, 12, out_count)
    steps = PIECES * (chunks - 1) + second[1] + 1
    chunk = rows // chunks
    after = 2 * pairs
    slabs = slab_count(chunks)
    plan = types.SimpleNamespace(
        slabs=(1, 9, slabs),
        early=lambda k: min(slabs + 12 + 7 * k, steps - 2),
        late_slabs=(1, after + 8, slabs),
        late=lambda k: min(after + 10 + slabs + 5 * k, steps - 2),
    )

    def body(r, s):
        back = KeyValueReturn(r, reach)
        attn, upper = LineSum(r.attn), LineSum(r.upper, r.upper_part)
        grads = WeightGrads(r, plan)
        sums = Butterfly(r.sums)

        @pl.when(s == 0)
        def _():
            enter(attn.neighbours() + back.neighbours() + sums.neighbours())
            back.start()
            upper.push(0, half)
            r.head_gain[...] = jnp.zeros_like(r.head_gain)
            r.gain_held[...] = jnp.zeros_like(r.gain_held)

        def send_attn(c):
            part = attention_grads(r, back, attn, c)
            hat, _ = norm_parts(r.hidden[...].astype(F32))
            r.gain_held[...] += row_sums(part * hat)

        def give_output(c):
            per = out_count // 4
            for q in range(2):

                @pl.when((c >= q * per) & (c < (q + 1) * per))
                def _():
                    here = pl.ds(pl.multiple_of(jnp.clip(c - q * per, 0, per - 1) * out_chunk, out_chunk), out_chunk)
                    total = (r.quarter_0, r.quarter_1)[q][here, :].astype(F32)
                    r.output[...] = (r.hidden_mid[...] + total).astype(BF)

            @pl.when(c >= 2 * per)
            def _():
                r.output[...] = (r.hidden_mid[...] + upper.total(c - 2 * per, out_chunk)).astype(BF)

        def give_input(c):
            hat, inverse = norm_parts(r.hidden_late[...].astype(F32))
            r.input_grad[...] = r.g_above[...] + norm_back(attn.total(c, chunk), r.attn_gain[...].astype(F32), hat, inverse)

        r.arrived(first[1], *QKV_WEIGHTS)
        at_chunk(s, first, send_attn)
        grads.late_slabs(s)
        at_chunk(s, (1, 2, half_pieces), upper.relay)
        at_chunk(s, (1, 9, pieces), attn.relay)
        at_chunk(s, (1, 4, half_pieces), upper.meet)
        at_chunk(s, (1, 12, pieces), attn.meet)
        at_chunk(s, third, give_output)
        at_chunk(s, second, give_input)
        grads.run(s)

        @pl.when(s == after + 1)
        def _():
            row = lax.broadcasted_iota(jnp.int32, (8, width), 0)
            once = jnp.where(lax.axis_index("tensor") == 0, 1.0, 0.0)
            heads = [r.head_gain[0:1, :], r.above_head_gain[0:1, :], jnp.zeros((1, width - 4 * HEAD), F32)]
            packet = jnp.zeros((8, width), F32)
            for place, part in enumerate([
                r.gain_held[...], r.above_gain[0:1, :] * once, r.above_gain[1:2, :] * once, r.top_gain[0:1, :] * once,
                jnp.concatenate(heads, 1),
            ]):
                packet = jnp.where(row == place, part, packet)
            sums.put(packet)

        for k in range(len(sums.axes)):

            @pl.when(s == max(steps - len(sums.axes) - 4 + k, after + 2))
            def _():
                sums.fold(k)

        @pl.when(s == steps - 1)
        def _():
            grads.store()
            r.gains[...] = sums.total()
            attn.finish()
            upper.finish()
            back.finish()
            grads.finish()
            sums.finish()

    return step_kernel(
        last_backward, body, steps,
        attention_grads_ins(a, w, layer, tables, first)
        | grads_ins(a, rows, width, plan.slabs)
        | dict(
            hidden=(a.hidden, first),
            hidden_late=(a.hidden, second),
            g_above=(g_mid, second),
            above_gain=(above.gain_grad, WHOLE),
            above_head_gain=(above.head_gain, WHOLE),
            top_gain=(top.gain_grad, WHOLE),
            upper_part=(top.upper_part, WHOLE),
            quarter_0=(quarters[0], WHOLE),
            quarter_1=(quarters[1], WHOLE),
            hidden_mid=(top.hidden_mid, third),
        ),
        dict(
            input_grad=((rows, width), F32, second),
            output=((rows, width), BF, third),
            gains=((8, width), F32, WHOLE),
        )
        | grads_outs(width, q_width, k_width, ff),
        dict(
            attn=LineSum.scratch(rows, width, pieces),
            upper=LineSum.scratch(half, width, half_pieces, False),
            kr=KeyValueReturn.scratch(rows, k_width, pairs, reach),
            **WeightGrads.scratch(rows, width, q_width, k_width, ff),
            sums=Butterfly.scratch((8, width)),
            head_gain=pltpu.VMEM((8, 2 * HEAD), F32),
            gain_held=pltpu.VMEM((1, width), F32),
        ),
        collective_id)


def collect_kernel(count, output_in, input_in, gains, *refs):
    ins, (output, input_grad, attn, mlp, q_gain, k_gain), outs = refs[: 2 * count], refs[2 * count : 2 * count + 6], refs[2 * count + 6 :]
    output[...] = output_in[...]
    input_grad[...] = input_in[...]
    s = pl.program_id(0)

    @pl.when(s == 0)
    def _():
        attn[...] = gains[0:2, :]
        mlp[...] = gains[2:4, :]
        for layer in range(2):
            at = 2 * layer * HEAD
            q_gain[layer : layer + 1, :] = gains[4:5, at : at + HEAD]
            k_gain[layer : layer + 1, :] = gains[4:5, at + HEAD : at + 2 * HEAD]

    for g in range(count):
        for layer in range(2):
            value = ins[2 * g + layer]
            if outs[g].shape[1] == value.shape[0]:
                outs[g][layer] = value[...]
            else:

                @pl.when(s == 0)
                def _():
                    outs[g][layer] = value[...].T


def collect(end, above):
    rows, width = end.output.shape
    straight = [(k.grad_q, k.grad_k, k.grad_v, k.grad_gate, k.grad_up) for k in (end, above)]
    turned = [(k.grad_o, k.grad_down) for k in (end, above)]
    per = straight[0][0].shape[0]
    steps = max(1, min(2, per // 8))
    whole = pl.BlockSpec(memory_space=pltpu.VMEM)

    def blocks(array):
        return pl.BlockSpec((array.shape[0] // steps, array.shape[1]), lambda s: (s, 0))

    ins = [end.output, end.input_grad, end.gains]
    in_specs = [blocks(end.output), blocks(end.input_grad), whole]
    outs = [
        ((rows, width), BF, blocks(end.output)), ((rows, width), F32, blocks(end.input_grad)),
        ((2, width), F32, whole), ((2, width), F32, whole), ((2, HEAD), F32, whole), ((2, HEAD), F32, whole),
    ]
    for pair in zip(*straight):
        ins += pair
        in_specs += [blocks(a) for a in pair]
        shape = pair[0].shape
        outs.append(((2,) + shape, F32, pl.BlockSpec((2, per // steps, shape[1]), lambda s: (0, s, 0))))
    for pair in zip(*turned):
        ins += pair
        in_specs += [whole, whole]
        outs.append(((2,) + pair[0].shape[::-1], F32, whole))
    return pl.pallas_call(
        functools.partial(collect_kernel, 7),
        grid=(steps,),
        in_specs=in_specs,
        out_specs=[o[2] for o in outs],
        out_shape=[jax.ShapeDtypeStruct(o[0], o[1]) for o in outs],
        name=collect.__name__,
        compiler_params=pltpu.CompilerParams(vmem_limit_bytes=62 << 20),
    )(*ins)


def per_device(
    tokens, cotangent, segments, positions, attn_gain, w_query, key_projection, value_projection, query_gain, key_gain,
    w_output, mlp_gain, w_gate, w_up, w_down,
):
    seqs_here, stretch, width = tokens.shape
    rows = seqs_here * stretch
    reach = min(lax.axis_size("seq") - 1, (WINDOW + stretch - 2) // stretch)
    chunks = rows // min(CHUNK, stretch)

    w = types.SimpleNamespace(
        attn_gain=attn_gain, mlp_gain=mlp_gain, q_gain=query_gain, k_gain=key_gain,
        w_q=w_query, w_k=key_projection, w_v=value_projection, w_o=w_output, w_gate=w_gate, w_up=w_up, w_down=w_down,
    )
    tokens = tokens.reshape(rows, width)
    cotangent = cotangent.reshape(rows, width)

    a0 = first_projection(tokens, segments, positions, w, stretch, reach, rows // min(2 * CHUNK, stretch), 1)
    tables, low = a0.tables, a0.low
    a0.hidden = tokens
    mid = between_forward(a0, low, w, 0, tables, stretch, reach, chunks, 2)
    a0.context, a0.lse = mid.context, mid.lse
    a1 = types.SimpleNamespace(
        attn_low=mid.attn_low, raw=mid.raw, queries=mid.queries, window=mid.window,
        hidden=mid.hidden_next)
    turn = turn_around(a1, low, cotangent, w, 1, stretch, chunks, 3)
    a1.context, a1.lse = turn.context, turn.lse
    a1.mlp_low, a1.act, a1.d_gates = turn.mlp_low, turn.act, turn.d_gates
    a1.mid_low, a1.g_low = turn.mid_low, cotangent
    pieces = chunks * FINE // 4
    back = attention_backward(a1, turn.d_context, low, turn.lower_part, 0, stretch, pieces, 6)
    a1.d_q, a1.d_own, a1.d_prev = back.d_q, back.d_own, back.d_prev
    quarters = [back.total]
    down = between_backward(a1, mid, turn.g_mid, w, 1, tables, reach, chunks, 4)
    a0.mlp_low, a0.act, a0.d_gates = mid.mlp_low, mid.act, down.d_gates
    a0.mid_low, a0.g_low = down.mid_low, down.g_low
    back = attention_backward(a0, down.d_context, low, turn.lower_part, 1, stretch, pieces, 7)
    a0.d_q, a0.d_own, a0.d_prev = back.d_q, back.d_own, back.d_prev
    quarters.append(back.total)
    end = last_backward(a0, turn, quarters, down, w, tables, reach, chunks, 5)
    output, input_grad, attn, mlp, q_gain, k_gain, d_q, d_k, d_v, d_gate, d_up, d_o, d_down = collect(end, down)
    shape = (seqs_here, stretch, width)
    return (
        output.reshape(shape), input_grad.reshape(shape), attn, d_q, d_k, d_v, q_gain, k_gain, d_o, mlp, d_gate, d_up,
        d_down,
    )


def solution(mesh):
    placed = (
        P("dp", "seq", None), P("dp", "seq", None), P("dp", "seq"), P("dp", "seq"), P(), P(None, None, "tensor"),
        P(None, None, "tensor"), P(None, None, "tensor"), P(), P(), P(None, "tensor", None), P(),
        P(None, None, "tensor"), P(None, None, "tensor"), P(None, "tensor", None),
    )
    by_rows = P(None, ("dp", "seq"), "tensor")
    by_columns = P(None, "tensor", ("dp", "seq"))
    return jax.shard_map(
        per_device,
        mesh=mesh,
        in_specs=placed,
        out_specs=(
            P("dp", "seq", None), P("dp", "seq", None), P(), by_rows, by_rows, by_rows, P(), P(), by_columns, P(),
            by_rows, by_rows, by_columns,
        ),
        check_vma=False,
    )
```

```python
import functools
import types

import jax
import jax.numpy as jnp
import numpy as np
from jax import lax
from jax.experimental import pallas as pl
from jax.experimental.pallas import tpu as pltpu
from jax.sharding import PartitionSpec as P

HEAD = 128
LAYER_COUNT = 2
WINDOW = 1024
EPS = 1e-06
THETA = 1000000.0
LOG2E = 1.4426950408889634
SCALE = HEAD ** (-0.5)
CHUNK = 128
PIECES = 2
FINE = 4
MESH = pl.DeviceIdType.MESH
BF = jnp.bfloat16
F32 = jnp.float32

NT = (((1,), (1,)), ((), ()))
NN = (((1,), (0,)), ((), ()))
TN = (((0,), (0,)), ((), ()))


def dot(a, b, dims=NN):
    return lax.dot_general(a, b, dims, preferred_element_type=F32)


def chunk_index(schedule, s):
    rate, lag, count = schedule
    return jnp.clip((s - lag) // rate, 0, count - 1)


def rows_spec(schedule, shape):
    return pl.BlockSpec((shape[0] // schedule[2], shape[1]), lambda s: (chunk_index(schedule, s), 0))


WHOLE, HBM = object(), object()
MLP_WEIGHTS = ("w_gate", "w_up", "w_down")
QKV_WEIGHTS = ("w_q", "w_k", "w_v")
GRAD_OPERANDS = ("d_gates_all", "context_all", "act_all")


class Row:
    def __init__(self, layer):
        self.layer = layer


class Late:
    def __init__(self, layer=None):
        self.layer = layer

    def shape(self, array):
        return array.shape if self.layer is None else array.shape[1:]

    def copy(self, source, held, sem):
        return pltpu.make_async_copy(source if self.layer is None else source.at[self.layer], held, sem)


def step_kernel(owner, body, steps, ins, outs, scratch, collective_id, vmem=62):
    def spec(shape, where, is_in):
        if isinstance(where, pl.BlockSpec):
            return where
        if where is HBM or isinstance(where, Late):
            return pl.BlockSpec(memory_space=pl.ANY)
        if where is WHOLE or isinstance(where, Row):
            zeros = (0,) * len(shape)
            if is_in:
                return pl.BlockSpec(shape, lambda s: zeros, pipeline_mode=pl.Buffered(1))
            return pl.BlockSpec(memory_space=pltpu.VMEM)
        return rows_spec(where, shape)

    late = {name: where for name, (_, where) in ins.items() if isinstance(where, Late)}
    held = {name: pltpu.VMEM(where.shape(ins[name][0]), ins[name][0].dtype) for name, where in late.items()}
    flat, tree = jax.tree.flatten((scratch, held, {name: pltpu.SemaphoreType.DMA(()) for name in late}))

    def kernel(*refs):
        named = dict(zip(ins, refs))
        named.update(zip(outs, refs[len(ins) :]))
        own, held_refs, sems = jax.tree.unflatten(tree, refs[len(ins) + len(outs) :])
        copies = {name: where.copy(named[name], held_refs[name], sems[name]) for name, where in late.items()}
        for name, ref in own.items():
            named[name] = types.SimpleNamespace(**ref) if isinstance(ref, dict) else ref
        named.update(held_refs)
        for name, (_, where) in ins.items():
            if isinstance(where, Row):
                named[name] = named[name].at[where.layer : where.layer + 1]
        s = pl.program_id(0)

        @pl.when(s == 0)
        def _():
            for copy in copies.values():
                copy.start()

        def arrived(step, *names):
            @pl.when(s == step)
            def _():
                for name in names:
                    copies[name].wait()

        body(types.SimpleNamespace(arrived=arrived, **named), s)

    results = pl.pallas_call(
        kernel,
        grid=(steps,),
        in_specs=[spec(a.shape, w, True) for a, w in ins.values()],
        out_specs=[spec(shape, w, False) for shape, _, w in outs.values()],
        out_shape=[jax.ShapeDtypeStruct(shape, dtype) for shape, dtype, _ in outs.values()],
        scratch_shapes=flat,
        name=owner.__name__,
        compiler_params=pltpu.CompilerParams(
            collective_id=collective_id, has_side_effects=True, vmem_limit_bytes=vmem << 20
        ),
    )(*[a for a, _ in ins.values()])
    return types.SimpleNamespace(**dict(zip(outs, results)))


def at_chunk(s, schedule, work):
    rate, lag, count = schedule
    moved = s - lag
    here = (moved >= 0) & (moved < rate * count)
    if rate > 1:
        here = here & (lax.rem(moved, rate) == 0)

    @pl.when(here)
    def _():
        work(moved // rate if rate > 1 else moved)


def enter(devices):
    barrier = pltpu.get_barrier_semaphore()
    count = 0
    for device, exists in devices:
        if exists is True:
            pl.semaphore_signal(barrier, inc=1, device_id=device, device_id_type=MESH)
            count = count + 1
        else:

            @pl.when(exists)
            def _():
                pl.semaphore_signal(barrier, inc=1, device_id=device, device_id_type=MESH)

            count = count + jnp.where(exists, 1, 0)
    pl.semaphore_wait(barrier, count)


class LineSum:
    def __init__(self, refs, x=None):
        self.x, self.land = refs.x if x is None else x, refs.land
        self.send_sem, self.land_sem, self.out_sem = refs.send, refs.arrive, refs.out
        self.pieces = self.send_sem.shape[0]
        self.rows = self.x.shape[0] // self.pieces
        n = lax.axis_size("tensor")
        z = lax.axis_index("tensor")
        half = n // 2
        self.middle = (z == half - 1) | (z == half)
        self.has_outer = (z > 0) & (z < n - 1)
        self.inner = jnp.where(z < half, z + 1, z - 1)
        self.outer = jnp.clip(jnp.where(z < half, z - 1, z + 1), 0, n - 1)
        self.slot = jnp.where(self.middle, 1, 0)

    @staticmethod
    def scratch(rows, width, pieces, own=True):
        held = dict(x=pltpu.VMEM((rows, width), BF)) if own else {}
        return held | dict(
            land=pltpu.VMEM((2, rows, width), BF),
            send=pltpu.SemaphoreType.DMA((pieces,)),
            arrive=pltpu.SemaphoreType.DMA((2, pieces)),
            out=pltpu.SemaphoreType.DMA((pieces,)),
        )

    def neighbours(self):
        return [({"tensor": self.inner}, True), ({"tensor": self.outer}, self.has_outer)]

    def at(self, j, rows=None):
        rows = rows or self.rows
        return pl.ds(pl.multiple_of(j * rows, rows), rows)

    def inward(self, source, j, slot):
        return pltpu.make_async_remote_copy(
            source.at[self.at(j)], self.land.at[slot, self.at(j)], self.send_sem.at[j], self.land_sem.at[slot, j],
            device_id={"tensor": self.inner}, device_id_type=MESH)

    def outward(self, j):
        return pltpu.make_async_remote_copy(
            self.land.at[1, self.at(j)], self.land.at[1, self.at(j)], self.out_sem.at[j], self.land_sem.at[1, j],
            device_id={"tensor": self.outer}, device_id_type=MESH)

    def put(self, c, value):
        rows = value.shape[0]
        self.x[self.at(c, rows), :] = value.astype(BF)
        self.push(c, rows)

    def push(self, c, rows):
        @pl.when(jnp.logical_not(self.has_outer))
        def _():
            for i in range(rows // self.rows):
                self.inward(self.x, c * (rows // self.rows) + i, self.slot).start()

    def add(self, j, source, slot):
        self.land[slot, self.at(j), :] = (
            source[self.at(j), :].astype(F32) + self.land[slot, self.at(j), :].astype(F32)
        ).astype(BF)

    def relay(self, j):
        @pl.when(self.has_outer)
        def _():
            self.inward(self.x, j, 0).wait_recv()
            self.add(j, self.x, 0)
            self.inward(self.land.at[0], j, self.slot).start()

    def meet(self, j):
        @pl.when(self.middle)
        def _():
            self.inward(self.x, j, 1).wait_recv()

            @pl.when(self.has_outer)
            def _():
                self.add(j, self.land.at[0], 1)
                self.outward(j).start()

            @pl.when(jnp.logical_not(self.has_outer))
            def _():
                self.add(j, self.x, 1)

    def total(self, c, rows):
        @pl.when(jnp.logical_not(self.middle))
        def _():
            for i in range(rows // self.rows):
                j = c * (rows // self.rows) + i
                self.inward(self.x, j, 1).wait_recv()

                @pl.when(self.has_outer)
                def _():
                    self.outward(j).start()

        return self.land[1, self.at(c, rows), :].astype(F32)

    def finish(self):
        @pl.when(self.has_outer)
        def _():
            @pl.loop(0, self.pieces)
            def _(j):
                self.inward(self.land.at[0], j, self.slot).wait_send()
                self.outward(j).wait_send()

        @pl.when(jnp.logical_not(self.has_outer))
        def _():
            @pl.loop(0, self.pieces)
            def _(j):
                self.inward(self.x, j, self.slot).wait_send()


class KeyValueSend:
    def __init__(self, refs, reach, stretch):
        self.held, self.zeros, self.window = refs.kv.held, refs.kv.zeros, refs.window
        self.copy_sem, self.send_sem, self.land_sem = refs.kv.copy, refs.kv.send, refs.kv.land
        self.chunks = self.copy_sem.shape[0]
        self.rows = self.held.shape[0] // self.chunks
        self.reach, self.stretch = reach, stretch
        self.place = lax.axis_index("seq")
        self.count = lax.axis_size("seq")

    @staticmethod
    def scratch(rows, width, chunks, reach):
        held = max(reach, 1)
        return dict(
            held=pltpu.VMEM((rows, width), BF),
            zeros=pltpu.VMEM((rows // chunks, width), BF),
            copy=pltpu.SemaphoreType.DMA((chunks,)),
            send=pltpu.SemaphoreType.DMA((held, chunks)),
            land=pltpu.SemaphoreType.DMA((held, chunks)),
        )

    def neighbours(self):
        found = []
        for back in range(1, self.reach + 1):
            found.append(({"seq": jnp.minimum(self.place + back, self.count - 1)}, self.place + back < self.count))
            found.append(({"seq": jnp.maximum(self.place - back, 0)}, self.place >= back))
        return found

    def at(self, c):
        return pl.ds(pl.multiple_of(c * self.rows, self.rows), self.rows)

    def there(self, back, c):
        per = self.stretch // self.rows
        chunk = ((c // per) * (self.reach + 1) + self.reach - back) * per + lax.rem(c, per)
        return self.window.at[self.at(chunk)]

    def own(self, c):
        return pltpu.make_async_copy(self.held.at[self.at(c)], self.there(0, c), self.copy_sem.at[c])

    def blank(self, back, c):
        return pltpu.make_async_copy(self.zeros, self.there(back, c), self.land_sem.at[back - 1, c])

    def remote(self, back, c):
        return pltpu.make_async_remote_copy(
            self.held.at[self.at(c)], self.there(back, c), self.send_sem.at[back - 1, c],
            self.land_sem.at[back - 1, c],
            device_id={"seq": jnp.minimum(self.place + back, self.count - 1)}, device_id_type=MESH)

    def start(self):
        self.zeros[...] = jnp.zeros_like(self.zeros)

    def send(self, c):
        self.own(c).start()
        for back in range(1, self.reach + 1):

            @pl.when(self.place + back < self.count)
            def _():
                self.remote(back, c).start()

            @pl.when(self.place < back)
            def _():
                self.blank(back, c).start()

    def finish(self):
        @pl.loop(0, self.chunks)
        def _(c):
            self.own(c).wait()
            for back in range(1, self.reach + 1):

                @pl.when(self.place + back < self.count)
                def _():
                    self.remote(back, c).wait_send()

                @pl.when(self.place >= back)
                def _():
                    self.remote(back, c).wait_recv()

                @pl.when(self.place < back)
                def _():
                    self.blank(back, c).wait()


class KeyValueReturn:
    def __init__(self, refs, reach):
        self.prev, self.land = refs.d_prev, refs.kr.land
        self.send_sem, self.land_sem = refs.kr.send, refs.kr.arrive
        self.chunks = self.send_sem.shape[1]
        self.rows = self.land.shape[2] // self.chunks
        self.reach = reach
        self.place = lax.axis_index("seq")
        self.count = lax.axis_size("seq")

    @staticmethod
    def scratch(rows, width, chunks, reach):
        held = max(reach, 1)
        return dict(
            land=pltpu.VMEM((held, 2, rows, width), BF),
            send=pltpu.SemaphoreType.DMA((held, chunks)),
            arrive=pltpu.SemaphoreType.DMA((held, chunks)),
        )

    neighbours = KeyValueSend.neighbours
    at = KeyValueSend.at

    def copy(self, back, c):
        return pltpu.make_async_remote_copy(
            self.prev.at[self.reach - back, :, self.at(c)], self.land.at[back - 1, :, self.at(c)],
            self.send_sem.at[back - 1, c], self.land_sem.at[back - 1, c],
            device_id={"seq": jnp.maximum(self.place - back, 0)}, device_id_type=MESH)

    def start(self):
        for back in range(1, self.reach + 1):

            @pl.when(self.place >= back)
            def _():
                @pl.loop(0, self.chunks)
                def _(c):
                    self.copy(back, c).start()

    def add(self, own, c):
        for back in range(1, self.reach + 1):
            exists = self.place + back < self.count

            @pl.when(exists)
            def _():
                self.copy(back, c).wait_recv()

            own = own + jnp.where(exists, self.land[back - 1, :, self.at(c), :].astype(F32), 0.0)
        return own

    def finish(self):
        for back in range(1, self.reach + 1):

            @pl.when(self.place >= back)
            def _():
                @pl.loop(0, self.chunks)
                def _(c):
                    self.copy(back, c).wait_send()


def device_bit(axis):
    name, b = axis
    return lax.rem(lax.axis_index(name) // (1 << b), 2)


def device_partner(axis):
    name, b = axis
    return {name: lax.axis_index(name) + (1 - 2 * device_bit(axis)) * (1 << b)}


def bits_of(name):
    return lax.axis_size(name).bit_length() - 1


def block_axes():
    return [(name, b) for name in ("dp", "seq") for b in reversed(range(bits_of(name)))]


class Scatter:
    def __init__(self, refs, swapped):
        self.axes = block_axes()
        phases = len(self.axes)
        near = [k for k in range(phases) if self.axes[k][0] == "seq"][::-1]
        far = [k for k in range(phases) if self.axes[k][0] == "dp"]
        self.order = near + (far if swapped else far[::-1])
        self.buffer, self.lands = refs.held, refs.lands
        self.send_sem, self.land_sem = refs.send, refs.arrive

    @staticmethod
    def scratch(rows, width):
        phases = len(block_axes())
        return dict(
            held=pltpu.VMEM((2,) * phases + (rows, width), BF),
            lands=[pltpu.VMEM((2,) * (phases - k - 1) + (rows, width), BF) for k in range(phases)],
            send=pltpu.SemaphoreType.DMA((phases,)),
            arrive=pltpu.SemaphoreType.DMA((phases,)),
        )

    def neighbours(self):
        return [(device_partner(axis), True) for axis in self.axes]

    def put(self, block, columns, value):
        phases = len(self.axes)
        place = tuple(lax.rem(block // (1 << (phases - 1 - k)), 2) for k in range(phases))
        self.buffer[place + (slice(None), columns)] = value.astype(BF)

    def view(self, k, mine):
        index = [slice(None)] * len(self.axes)
        for earlier in self.order[:k]:
            index[earlier] = device_bit(self.axes[earlier])
        bit = device_bit(self.axes[self.order[k]])
        index[self.order[k]] = bit if mine else 1 - bit
        return tuple(index)

    def copy(self, k):
        return pltpu.make_async_remote_copy(
            self.buffer.at[self.view(k, False)], self.lands[k], self.send_sem.at[k], self.land_sem.at[k],
            device_id=device_partner(self.axes[self.order[k]]), device_id_type=MESH)

    def send(self, k):
        self.copy(k).start()

    def fold(self, k, store=None):
        self.copy(k).wait_recv()
        index = self.view(k, True)
        free = [i for i, v in enumerate(index) if isinstance(v, slice)]
        for j in range(1 << len(free)):
            place = [(j >> (len(free) - 1 - i)) & 1 for i in range(len(free))]
            here = list(index)
            for i, axis in enumerate(free):
                here[axis] = place[i]
            here = tuple(here)
            total = self.buffer[here].astype(F32) + self.lands[k][tuple(place)].astype(F32)
            if store is None:
                self.buffer[here] = total.astype(BF)
            else:
                store(total)

    def finish(self):
        for k in range(len(self.axes)):
            self.copy(k).wait_send()


class Butterfly:
    def __init__(self, refs):
        self.axes = [(name, b) for name in ("seq", "dp", "tensor") for b in range(bits_of(name))]
        self.held, self.land = refs.held, refs.land
        self.send_sem, self.land_sem = refs.send, refs.arrive

    @staticmethod
    def scratch(shape):
        phases = bits_of("seq") + bits_of("dp") + bits_of("tensor")
        return dict(
            held=pltpu.VMEM((phases + 1,) + shape, F32),
            land=pltpu.VMEM((phases,) + shape, F32),
            send=pltpu.SemaphoreType.DMA((phases,)),
            arrive=pltpu.SemaphoreType.DMA((phases,)),
        )

    def neighbours(self):
        return [(device_partner(axis), True) for axis in self.axes]

    def copy(self, k):
        return pltpu.make_async_remote_copy(
            self.held.at[k], self.land.at[k], self.send_sem.at[k], self.land_sem.at[k],
            device_id=device_partner(self.axes[k]), device_id_type=MESH)

    def put(self, value):
        self.held[0] = value
        self.copy(0).start()

    def fold(self, k):
        self.copy(k).wait_recv()
        self.held[k + 1] = self.held[k] + self.land[k]
        if k + 1 < len(self.axes):
            self.copy(k + 1).start()

    def total(self):
        return self.held[len(self.axes)]

    def finish(self):
        for k in range(len(self.axes)):
            self.copy(k).wait_send()


def norm_parts(value):
    inverse = lax.rsqrt(jnp.mean(value * value, -1, keepdims=True) + EPS)
    return value * inverse, inverse


def norm_back(grad, gain, hat, inverse):
    scaled = grad * gain
    inner = jnp.mean(scaled * hat, -1, keepdims=True)
    return inverse * (scaled - hat * inner)


def row_sums(value):
    return jnp.sum(value, 0, keepdims=True)


def heads_of(value):
    return [value[:, h * HEAD : (h + 1) * HEAD] for h in range(value.shape[1] // HEAD)]


def rope(value, cosine, signed_sine):
    return value * cosine + pltpu.roll(value, HEAD // 2, 1) * signed_sine


def rope_back(grad, cosine, signed_sine):
    return grad * cosine - pltpu.roll(grad, HEAD // 2, 1) * signed_sine


def attend(r, c, stretch):
    rows, span = r.queries_in.shape[0], r.window_in.shape[0] // (r.low.shape[1] // stretch)
    offset = span - stretch
    per = stretch // rows
    length = min(WINDOW + rows, span)
    q_start = offset + lax.rem(c, per) * rows
    start = jnp.clip(q_start + rows - length, 0, span - length)
    here = pl.ds(pl.multiple_of((c // per) * span + start, rows), length)
    group = r.queries_in.shape[1] * 2 // r.window_in.shape[1]
    low = r.low[:, pl.ds(pl.multiple_of(c * rows, rows), rows)].astype(F32)
    low = jnp.broadcast_to(low, (HEAD, rows)).T[:, :1]
    key_index = (start + lax.broadcasted_iota(jnp.int32, (rows, length), 1)).astype(F32)
    q_index = (q_start + lax.broadcasted_iota(jnp.int32, (rows, 1), 0)).astype(F32)
    mask = (key_index >= low) & (key_index <= q_index)
    mask = jnp.concatenate([mask] * group, 0)
    queries = heads_of(r.queries_in[...])
    kv_heads = len(queries) // group
    outs = []
    for g in range(kv_heads):
        keys = r.window_in[here, g * HEAD : (g + 1) * HEAD]
        values = r.window_in[here, (kv_heads + g) * HEAD : (kv_heads + g + 1) * HEAD]
        s = dot(jnp.concatenate(queries[g * group : (g + 1) * group], 0), keys, NT) * (SCALE * LOG2E)
        p = jnp.where(mask, jnp.exp2(s), 0.0)
        part = p[:, :HEAD]
        for k in range(1, length // HEAD):
            part = part + p[:, k * HEAD : (k + 1) * HEAD]
        total = jnp.sum(part, 1, keepdims=True)
        o = (dot(p.astype(BF), values) / total).astype(BF)
        log_total = jnp.broadcast_to(jnp.log2(total), (group * rows, HEAD))
        for h in range(group):
            outs.append(o[h * rows : (h + 1) * rows])
            r.lse[g, h : h + 1, :] = log_total[h * rows : (h + 1) * rows].T[0:1, :]
    context = jnp.concatenate(outs, 1)
    r.context[...] = context
    return context


def attend_ins(a, low, when):
    return dict(
        queries_in=(a.queries, when),
        window_in=(a.window, Late()),
        low=(low, WHOLE),
    )


def attend_outs(a, when):
    kv_heads = a.window.shape[1] // (2 * HEAD)
    rows, width = a.queries.shape
    shape = (kv_heads, width // (kv_heads * HEAD), rows)
    return dict(
        context=((rows, width), BF, when),
        lse=(shape, F32, pl.BlockSpec(shape[:2] + (rows // when[2],), lambda s: (0, 0, chunk_index(when, s)))),
    )


def project(r, hidden, kv, c):
    hat, _ = norm_parts(hidden)
    low = (hat * r.attn_gain[...].astype(F32)).astype(BF)
    r.attn_low[...] = low
    q_raw = dot(low, r.w_q[...])
    k_raw = dot(low, r.w_k[...])
    values = dot(low, r.w_v[...])
    r.raw[...] = jnp.concatenate([q_raw, k_raw], 1)
    cosine, sine = r.tables[:, :HEAD], r.tables[:, HEAD:]

    def turned(raw, gain):
        return jnp.concatenate(
            [rope(norm_parts(u)[0] * gain, cosine, sine).astype(BF) for u in heads_of(raw)], 1)

    r.queries[...] = turned(q_raw, r.q_gain[...].astype(F32))
    kv.held[kv.at(c), :] = jnp.concatenate([turned(k_raw, r.k_gain[...].astype(F32)), values.astype(BF)], 1)
    kv.send(c)


def project_outs(rows, width, w, stretch, reach, when):
    q_width, k_width = w.w_q.shape[2], w.w_k.shape[2]
    return dict(
        attn_low=((rows, width), BF, when),
        raw=((rows, q_width + k_width), F32, when),
        queries=((rows, q_width), BF, when),
        window=((rows // stretch * (reach + 1) * stretch, k_width + w.w_v.shape[2]), BF, HBM),
    )


def project_ins(w, layer, tables, when):
    def weight(array):
        if tables is not None:
            return array, Late(layer)
        shape = array.shape[1:]
        return array, pl.BlockSpec((None,) + shape, lambda s: (layer, 0, 0), pipeline_mode=pl.Buffered(1))

    return dict(
        attn_gain=(w.attn_gain, Row(layer)),
        w_q=weight(w.w_q),
        w_k=weight(w.w_k),
        w_v=weight(w.w_v),
        q_gain=(w.q_gain, Row(layer)),
        k_gain=(w.k_gain, Row(layer)),
    ) | ({} if tables is None else dict(tables=(tables, when)))


def mlp_gates(r, low):
    gate = dot(low, r.w_gate[...])
    up = dot(low, r.w_up[...])
    sigma = jax.nn.sigmoid(gate)
    return gate, up, sigma


def mlp_back(r, g_low, gate, up, sigma):
    d_act = dot(g_low, r.w_down[...], NT)
    d_gate = (d_act * up * sigma * (1.0 + gate * (1.0 - sigma))).astype(BF)
    d_up = (d_act * gate * sigma).astype(BF)
    return jnp.concatenate([d_gate, d_up], 1), dot(d_gate, r.w_gate[...], NT) + dot(d_up, r.w_up[...], NT)


def first_projection(hidden, segments, positions, w, stretch, reach, chunks, collective_id):
    rows, width = hidden.shape
    when = (1, 0, chunks)
    kv_width = w.w_k.shape[2] + w.w_v.shape[2]

    held = max(reach, 1)
    seqs = rows // stretch

    def body(r, s):
        kv = KeyValueSend(r, reach, stretch)

        def documents(back):
            return pltpu.make_async_remote_copy(
                r.segments, r.docs.at[back - 1], r.doc_send.at[back - 1], r.doc_land.at[back - 1],
                device_id={"seq": jnp.minimum(kv.place + back, kv.count - 1)}, device_id_type=MESH)

        @pl.when(s == 0)
        def _():
            r.docs[...] = jnp.full_like(r.docs, -1)
            enter(kv.neighbours())
            kv.start()
            for back in range(1, reach + 1):

                @pl.when(kv.place + back < kv.count)
                def _():
                    documents(back).start()

        angle = jnp.broadcast_to(r.positions[...].astype(F32), (HEAD, rows // chunks)).T * r.frequency[...]
        lane = lax.broadcasted_iota(jnp.int32, angle.shape, 1)
        sine = jnp.sin(angle)
        r.tables[...] = jnp.concatenate([jnp.cos(angle), jnp.where(lane < HEAD // 2, -sine, sine)], 1)
        project(r, r.hidden[...].astype(F32), kv, s)

        @pl.when(s == chunks - 1)
        def _():
            kv.finish()
            for back in range(1, reach + 1):

                @pl.when(kv.place + back < kv.count)
                def _():
                    documents(back).wait_send()

                @pl.when(kv.place >= back)
                def _():
                    documents(back).wait_recv()

            for q in range(seqs):
                here = slice(q * stretch, (q + 1) * stretch)
                own = r.segments[:, here]
                docs = [r.docs[back - 1, :, here] for back in range(1, reach + 1)]

                def first_of(document):
                    counts = [jnp.sum((d < document).astype(jnp.int32), 1, keepdims=True) for d in docs + [own]]
                    return functools.reduce(jnp.add, counts)

                low = jnp.broadcast_to(first_of(0), own.shape)
                for document in range(1, 4):
                    low = jnp.where(own >= document, first_of(document), low)
                index = lax.broadcasted_iota(jnp.int32, own.shape, 1)
                r.low[:, here] = jnp.maximum(low, reach * stretch + index - (WINDOW - 1))

    frequency = (THETA ** (-np.arange(0, HEAD, 2) / HEAD)).astype(np.float32)
    return step_kernel(
        first_projection, body, chunks,
        dict(
            hidden=(hidden, when),
            segments=(segments.reshape(1, rows), WHOLE),
            positions=(
                positions.reshape(1, rows), pl.BlockSpec((1, rows // chunks), lambda s: (0, chunk_index(when, s)))),
            frequency=(jnp.asarray(np.concatenate([frequency, frequency])[None]), WHOLE),
        )
        | project_ins(w, 0, None, when),
        project_outs(rows, width, w, stretch, reach, when)
        | dict(
            tables=((rows, 2 * HEAD), F32, when),
            low=((1, rows), jnp.int32, WHOLE),
        ),
        dict(
            kv=KeyValueSend.scratch(rows, kv_width, chunks, reach),
            docs=pltpu.VMEM((held, 1, rows), jnp.int32),
            doc_send=pltpu.SemaphoreType.DMA((held,)),
            doc_land=pltpu.SemaphoreType.DMA((held,)),
        ),
        collective_id)


def between_forward(a, low, w, layer, tables, stretch, reach, chunks, collective_id):
    hidden = a.hidden
    rows, width = hidden.shape
    kv_width = w.w_k.shape[2] + w.w_v.shape[2]
    ff = w.w_gate.shape[2]
    pieces = chunks * FINE
    first, second, third = (FINE, 0, chunks), (FINE, 8, chunks), (FINE, 17, chunks)
    steps = FINE * (chunks - 1) + third[1] + 1
    chunk = rows // chunks

    def body(r, s):
        kv = KeyValueSend(r, reach, stretch)
        attn, mlp = LineSum(r.attn), LineSum(r.mlp)

        @pl.when(s == 0)
        def _():
            enter(attn.neighbours() + kv.neighbours())
            kv.start()

        def send_attn(c):
            attn.put(c, dot(attend(r, c, stretch), r.w_o[...]))

        def feed_forward(c):
            middle = r.hidden[...].astype(F32) + attn.total(c, chunk)
            r.hidden_mid[...] = middle
            r.mid_held[attn.at(c, chunk), :] = middle
            hat, _ = norm_parts(middle)
            low = (hat * r.mlp_gain[...].astype(F32)).astype(BF)
            r.mlp_low[...] = low
            gate, up, sigma = mlp_gates(r, low)
            r.gates[...] = jnp.concatenate([gate, up], 1)
            act = (gate * sigma * up).astype(BF)
            r.act[...] = act
            mlp.put(c, dot(act, r.w_down[...]))

        def next_layer(c):
            hidden_next = r.mid_held[mlp.at(c, chunk), :] + mlp.total(c, chunk)
            r.hidden_next[...] = hidden_next
            project(r, hidden_next, kv, c)

        r.arrived(0, "window_in", "w_o")
        at_chunk(s, first, send_attn)
        at_chunk(s, (1, 2, pieces), attn.relay)
        at_chunk(s, (1, 4, pieces), attn.meet)
        r.arrived(second[1], *MLP_WEIGHTS)
        at_chunk(s, second, feed_forward)
        at_chunk(s, (1, 12, pieces), mlp.relay)
        at_chunk(s, (1, 14, pieces), mlp.meet)
        r.arrived(third[1], *QKV_WEIGHTS)
        at_chunk(s, third, next_layer)

        @pl.when(s == steps - 1)
        def _():
            attn.finish()
            mlp.finish()
            kv.finish()

    return step_kernel(
        between_forward, body, steps,
        attend_ins(a, low, first)
        | dict(
            w_o=(w.w_o, Late(layer)),
            hidden=(hidden, second),
            mlp_gain=(w.mlp_gain, Row(layer)),
            w_gate=(w.w_gate, Late(layer)),
            w_up=(w.w_up, Late(layer)),
            w_down=(w.w_down, Late(layer)),
        )
        | project_ins(w, layer + 1, tables, third),
        attend_outs(a, first)
        | dict(
            hidden_mid=((rows, width), F32, second),
            mlp_low=((rows, width), BF, second),
            gates=((rows, 2 * ff), F32, second),
            act=((rows, ff), BF, second),
            hidden_next=((rows, width), F32, third),
        )
        | project_outs(rows, width, w, stretch, reach, third),
        dict(
            attn=LineSum.scratch(rows, width, pieces),
            mlp=LineSum.scratch(rows, width, pieces),
            kv=KeyValueSend.scratch(rows, kv_width, chunks, reach),
            mid_held=pltpu.VMEM((rows, width), F32),
        ),
        collective_id)


def turn_around(a, low, cotangent, w, layer, stretch, chunks, collective_id):
    hidden = a.hidden
    rows, width = hidden.shape
    ff = w.w_gate.shape[2]
    pieces = chunks * FINE
    first, second, third = (FINE, 0, chunks), (FINE, 9, chunks), (FINE, 17, chunks)
    steps = FINE * (chunks - 1) + third[1] + 1
    chunk = rows // chunks

    def body(r, s):
        attn, back = LineSum(r.attn), LineSum(r.back)

        @pl.when(s == 0)
        def _():
            enter(attn.neighbours())
            r.gain_grad[...] = jnp.zeros_like(r.gain_grad)

        def send_attn(c):
            attn.put(c, dot(attend(r, c, stretch), r.w_o[...]))

        def feed_forward(c):
            middle = r.hidden[...] + attn.total(c, chunk)
            r.hidden_mid[...] = middle
            r.mid_held[attn.at(c, chunk), :] = middle
            hat, _ = norm_parts(middle)
            low = (hat * r.mlp_gain[...].astype(F32)).astype(BF)
            r.mlp_low[...] = low
            gate, up, sigma = mlp_gates(r, low)
            d_gates, part = mlp_back(r, r.cotangent[...], gate, up, sigma)
            back.put(c, part)
            r.d_gates[...] = d_gates
            act = (gate * sigma * up).astype(BF)
            r.act[...] = act
            part = dot(act, r.w_down[...]).astype(BF)

            @pl.when(c < chunks // 2)
            def _():
                r.lower_part[...] = part

            @pl.when(c >= chunks // 2)
            def _():
                r.upper_part[...] = part

        def middle_grad(c):
            hat, inverse = norm_parts(r.mid_held[back.at(c, chunk), :])
            d_in = back.total(c, chunk)
            r.gain_grad[0:1, :] += row_sums(d_in * hat)
            g_mid = r.cotangent_late[...].astype(F32) + norm_back(d_in, r.mlp_gain[...].astype(F32), hat, inverse)
            r.g_mid[...] = g_mid
            mid_low = g_mid.astype(BF)
            r.mid_low[...] = mid_low
            r.d_context[...] = dot(mid_low, r.w_o[...], NT).astype(BF)

        r.arrived(0, "window_in", "w_o")
        at_chunk(s, first, send_attn)
        at_chunk(s, (1, 2, pieces), attn.relay)
        at_chunk(s, (1, 4, pieces), attn.meet)
        r.arrived(second[1], *MLP_WEIGHTS)
        at_chunk(s, second, feed_forward)
        at_chunk(s, (1, 12, pieces), back.relay)
        at_chunk(s, (1, 14, pieces), back.meet)
        at_chunk(s, third, middle_grad)

        @pl.when(s == steps - 1)
        def _():
            attn.finish()
            back.finish()

    return step_kernel(
        turn_around, body, steps,
        attend_ins(a, low, first)
        | dict(
            w_o=(w.w_o, Late(layer)),
            hidden=(hidden, second),
            cotangent=(cotangent, second),
            cotangent_late=(cotangent, third),
            mlp_gain=(w.mlp_gain, Row(layer)),
            w_gate=(w.w_gate, Late(layer)),
            w_up=(w.w_up, Late(layer)),
            w_down=(w.w_down, Late(layer)),
        ),
        attend_outs(a, first)
        | dict(
            mlp_low=((rows, width), BF, second),
            act=((rows, ff), BF, second),
            hidden_mid=((rows, width), F32, second),
            lower_part=((rows // 2, width), BF, (FINE, second[1], chunks // 2)),
            upper_part=((rows // 2, width), BF, (FINE, second[1] + FINE * (chunks // 2), chunks // 2)),
            d_gates=((rows, 2 * ff), BF, second),
            g_mid=((rows, width), F32, third),
            mid_low=((rows, width), BF, third),
            d_context=(a.queries.shape, BF, third),
            gain_grad=((8, width), F32, WHOLE),
        ),
        dict(
            attn=LineSum.scratch(rows, width, pieces),
            back=LineSum.scratch(rows, width, pieces),
            mid_held=pltpu.VMEM((rows, width), F32),
        ),
        collective_id)


def attention_backward(a, d_context, low, part, quarter, stretch, pieces, collective_id):
    rows = a.queries.shape[0]
    kv_heads = a.window.shape[1] // (2 * HEAD)
    width = a.queries.shape[1] // kv_heads
    group = width // HEAD
    qb = min(2 * CHUNK, stretch)
    count = stretch // qb
    seqs = rows // stretch
    span = a.window.shape[0] // seqs
    reach = span // stretch - 1
    held = max(reach, 1)
    offset = reach * stretch
    length = min(WINDOW + qb, span)
    steps = seqs * kv_heads * count

    def places(s):
        return s // (kv_heads * count), lax.rem(s // count, kv_heads), lax.rem(s, count)

    def block(shape, index):
        return pl.BlockSpec(shape, lambda s: index(*places(s)))

    def body(r, s):
        seq, g, i = places(s)
        line = LineSum(r.line, r.part)
        q_start = i * qb + offset
        start = jnp.clip(q_start + qb - length, 0, span - length)
        here = pl.ds(pl.multiple_of(start, HEAD), length)

        @pl.when(s == 0)
        def _():
            enter(line.neighbours())
            line.push(0, line.x.shape[0])

        @pl.when(i == 0)
        def _():
            r.d_keys[...] = jnp.zeros_like(r.d_keys)
            r.d_values[...] = jnp.zeros_like(r.d_values)

        for j in range(pieces):

            @pl.when(s == min(2 + j // 2, steps - 1))
            def _():
                line.relay(j)

        for j in range(pieces):

            @pl.when(s == min(4 + j // 2, steps - 1))
            def _():
                line.meet(j)

        def stack(ref):
            return jnp.concatenate([ref[:, h * HEAD : (h + 1) * HEAD] for h in range(group)], 0)

        queries = stack(r.queries)
        d_out = stack(r.d_context)
        lse = jnp.concatenate([r.lse[h : h + 1, :] for h in range(group)], 1)
        product = d_out.astype(F32) * stack(r.context).astype(F32)
        delta = jnp.sum(product.T, 0, keepdims=True)
        keys = r.keys[here, :]
        values = r.values[here, :]
        key_index = start + lax.broadcasted_iota(jnp.int32, (length, qb), 0)
        q_index = q_start + lax.broadcasted_iota(jnp.int32, (1, qb), 1)
        mask = (key_index >= r.low[...]) & (key_index <= q_index)
        mask = jnp.concatenate([mask] * group, 1)
        scores = dot(keys, queries, NT) * (SCALE * LOG2E) - lse
        p = jnp.where(mask, jnp.exp2(scores), 0.0)
        ds = (p * (dot(values, d_out, NT) - delta)).astype(BF)
        r.d_values[here, :] += dot(p.astype(BF), d_out)
        r.d_keys[here, :] += dot(ds, queries)
        dq = (dot(keys, ds, TN) * SCALE).T
        for h in range(group):
            r.d_q[:, h * HEAD : (h + 1) * HEAD] = dq[h * qb : (h + 1) * qb]

        @pl.when(i == count - 1)
        def _():
            r.d_own[0] = r.d_keys[offset:, :] * SCALE
            r.d_own[1] = r.d_values[offset:, :]
            for j in range(reach):
                r.d_prev[j, 0] = (r.d_keys[j * stretch : (j + 1) * stretch, :] * SCALE).astype(BF)
                r.d_prev[j, 1] = r.d_values[j * stretch : (j + 1) * stretch, :].astype(BF)

        @pl.when(s == steps - 1)
        def _():
            r.total[...] = line.total(0, line.x.shape[0]).astype(BF)
            line.finish()

    by_rows = block((qb, width), lambda seq, g, i: (seq * count + i, g))
    part_rows = part.shape[0] // 2
    return step_kernel(
        attention_backward, body, steps,
        dict(
            low=(low, block((1, qb), lambda seq, g, i: (0, seq * count + i))),
            lse=(a.lse, block((None, group, qb), lambda seq, g, i: (g, 0, seq * count + i))),
            queries=(a.queries, by_rows),
            d_context=(d_context, by_rows),
            context=(a.context, by_rows),
            keys=(a.window, block((span, HEAD), lambda seq, g, i: (seq, g))),
            values=(a.window, block((span, HEAD), lambda seq, g, i: (seq, kv_heads + g))),
            part=(part, pl.BlockSpec(
                (part_rows, part.shape[1]), lambda s: (quarter, 0), pipeline_mode=pl.Buffered(1))),
        ),
        dict(
            d_q=(a.queries.shape, F32, by_rows),
            d_own=((2, rows, kv_heads * HEAD), F32, block((2, stretch, HEAD), lambda seq, g, i: (0, seq, g))),
            d_prev=(
                (held, 2, rows, kv_heads * HEAD), BF,
                block((held, 2, stretch, HEAD), lambda seq, g, i: (0, 0, seq, g))),
            total=((part_rows, part.shape[1]), BF, WHOLE),
        ),
        dict(
            line=LineSum.scratch(part_rows, part.shape[1], pieces, False),
            d_keys=pltpu.VMEM((span, HEAD), F32),
            d_values=pltpu.VMEM((span, HEAD), F32),
        ),
        collective_id)


def attention_grads(r, back, line, c):
    cosine, sine = r.tables[:, :HEAD], r.tables[:, HEAD:]
    both = back.add(r.d_own[...], c)

    def raw_back(grads, raws, gain):
        lows, gains = [], 0.0
        for grad, raw in zip(heads_of(grads), heads_of(raws)):
            grad = rope_back(grad, cosine, sine)
            hat, inverse = norm_parts(raw)
            gains = gains + row_sums(grad * hat)
            lows.append(norm_back(grad, gain, hat, inverse).astype(BF))
        return jnp.concatenate(lows, 1), gains

    q_width = r.d_q.shape[1]
    d_q, q_gain = raw_back(r.d_q[...], r.raw[:, :q_width], r.q_gain[...].astype(F32))
    d_k, k_gain = raw_back(both[0], r.raw[:, q_width:], r.k_gain[...].astype(F32))
    d_v = both[1].astype(BF)
    r.head_gain[0:1, 0:HEAD] += q_gain
    r.head_gain[0:1, HEAD : 2 * HEAD] += k_gain
    r.d_held[line.at(c, d_q.shape[0]), :] = jnp.concatenate([d_q, d_k, d_v], 1)
    part = dot(d_q, r.w_q[...], NT) + dot(d_k, r.w_k[...], NT) + dot(d_v, r.w_v[...], NT)
    line.put(c, part)
    return part


class WeightGrads:
    def __init__(self, r, plan):
        self.r = r
        self.plan = plan
        self.slabs = plan.slabs[2]
        self.late = Scatter(r.sc_q, False), Scatter(r.sc_kv, True)
        self.early = Scatter(r.sc_a, False), Scatter(r.sc_b, True)
        self.blocks = 1 << len(block_axes())

    @staticmethod
    def scratch(rows, width, q_width, k_width, ff):
        per = width // (1 << len(block_axes()))
        return dict(
            sc_a=Scatter.scratch(per, ff + q_width),
            sc_b=Scatter.scratch(per, 2 * ff),
            sc_q=Scatter.scratch(per, q_width),
            sc_kv=Scatter.scratch(per, 2 * k_width),
            d_held=pltpu.VMEM((rows, q_width + 2 * k_width), BF),
        )

    def neighbours(self):
        return self.late[0].neighbours()

    def put(self, scatter, slab, columns, value):
        per = self.blocks // self.slabs
        rows = value.shape[0] // per
        for j in range(per):
            scatter.put(slab * per + j, columns, value[j * rows : (j + 1) * rows])

    def mlp_slab(self, slab):
        r = self.r
        ff = r.act_all.shape[1]
        q_width = r.context_all.shape[1]
        both = dot(r.mlp_low_slab[...], r.d_gates_all[...], TN)
        self.put(self.early[0], slab, slice(0, ff), both[:, :ff])
        self.put(self.early[0], slab, slice(ff, ff + q_width), dot(r.mid_low_slab[...], r.context_all[...], TN))
        self.put(self.early[1], slab, slice(0, ff), both[:, ff:])
        self.put(self.early[1], slab, slice(ff, 2 * ff), dot(r.g_low_slab[...], r.act_all[...], TN))

    def qkv_slab(self, slab):
        r = self.r
        slab_width = r.attn_low_all.shape[1] // self.slabs
        q_width = r.d_q.shape[1]
        columns = pl.ds(pl.multiple_of(slab * slab_width, slab_width), slab_width)
        value = dot(r.attn_low_all[:, columns], r.d_held[...], TN)
        self.put(self.late[0], slab, slice(None), value[:, :q_width])
        self.put(self.late[1], slab, slice(None), value[:, q_width:])

    def each(self, scatters, work):
        for scatter in scatters:
            work(scatter)

    def store(self):
        r = self.r
        last = len(block_axes()) - 1
        ff = r.act_all.shape[1]
        k_width = r.grad_k.shape[1]

        def store_a(total):
            r.grad_gate[...] = total[:, :ff]
            r.grad_o[...] = total[:, ff:]

        def store_b(total):
            r.grad_up[...] = total[:, :ff]
            r.grad_down[...] = total[:, ff:]

        def store_q(total):
            r.grad_q[...] = total

        def store_kv(total):
            r.grad_k[...] = total[:, :k_width]
            r.grad_v[...] = total[:, k_width:]

        self.early[0].fold(last, store_a)
        self.early[1].fold(last, store_b)
        self.late[0].fold(last, store_q)
        self.late[1].fold(last, store_kv)

    def late_slabs(self, s):
        _, lag, count = self.plan.late_slabs
        self.r.arrived(lag, "attn_low_all")
        at_chunk(s, self.plan.late_slabs, self.qkv_slab)

        @pl.when(s == lag + count - 1)
        def _():
            self.each(self.late, lambda scatter: scatter.send(0))

    def run(self, s):
        rate, lag, count = self.plan.slabs
        self.r.arrived(lag, *GRAD_OPERANDS)
        at_chunk(s, self.plan.slabs, self.mlp_slab)

        @pl.when(s == lag + rate * (count - 1))
        def _():
            self.each(self.early, lambda scatter: scatter.send(0))

        for k in range(len(block_axes()) - 1):

            def move(scatter):
                scatter.fold(k)
                scatter.send(k + 1)

            @pl.when(s == self.plan.early(k))
            def _():
                self.each(self.early, move)

            @pl.when(s == self.plan.late(k))
            def _():
                self.each(self.late, move)

    def finish(self):
        self.each(self.early + self.late, lambda scatter: scatter.finish())


def slab_count(chunks):
    return min(4, max(1, chunks // 2))


def grads_ins(a, rows, width, when):
    slab = pl.BlockSpec((rows, width // when[2]), lambda s: (0, chunk_index(when, s)))
    return dict(
        mlp_low_slab=(a.mlp_low, slab),
        mid_low_slab=(a.mid_low, slab),
        g_low_slab=(a.g_low, slab),
        attn_low_all=(a.attn_low, Late()),
        d_gates_all=(a.d_gates, Late()),
        context_all=(a.context, Late()),
        act_all=(a.act, Late()),
    )


def grads_outs(width, q_width, k_width, ff):
    per = width // (1 << len(block_axes()))
    return dict(
        grad_q=((per, q_width), F32, WHOLE),
        grad_k=((per, k_width), F32, WHOLE),
        grad_v=((per, k_width), F32, WHOLE),
        grad_o=((per, q_width), F32, WHOLE),
        grad_gate=((per, ff), F32, WHOLE),
        grad_up=((per, ff), F32, WHOLE),
        grad_down=((per, ff), F32, WHOLE),
    )


def attention_grads_ins(a, w, layer, tables, when):
    rows, k_width = a.raw.shape[0], w.w_k.shape[2]
    own = pl.BlockSpec((2, rows // when[2], k_width), lambda s: (0, chunk_index(when, s), 0))
    return dict(
        d_q=(a.d_q, when),
        d_own=(a.d_own, own),
        d_prev=(a.d_prev, HBM),
        raw=(a.raw, when),
        tables=(tables, when),
        w_q=(w.w_q, Late(layer)),
        w_k=(w.w_k, Late(layer)),
        w_v=(w.w_v, Late(layer)),
        q_gain=(w.q_gain, Row(layer)),
        k_gain=(w.k_gain, Row(layer)),
        attn_gain=(w.attn_gain, Row(layer)),
    )


def between_backward(a, below, g_mid, w, layer, tables, reach, chunks, collective_id):
    rows, width = g_mid.shape
    q_width, k_width, ff = w.w_q.shape[2], w.w_k.shape[2], w.w_gate.shape[2]
    pieces = chunks * PIECES
    first, second, third = (PIECES, 0, chunks), (PIECES, 5, chunks), (PIECES, 11, chunks)
    steps = PIECES * (chunks - 1) + third[1] + 1
    chunk = rows // chunks
    after = PIECES * (chunks - 1) + 1
    slabs = slab_count(chunks)
    plan = types.SimpleNamespace(
        slabs=(2, 2, slabs),
        early=lambda k: min(4 + 2 * slabs + 4 * k, steps - 2),
        late_slabs=(1, after, slabs),
        late=lambda k: min(after + slabs + 2 * k, steps - 2),
    )

    def body(r, s):
        back = KeyValueReturn(r, reach)
        attn, mlp = LineSum(r.attn), LineSum(r.mlp)
        grads = WeightGrads(r, plan)

        @pl.when(s == 0)
        def _():
            enter(attn.neighbours() + back.neighbours() + grads.neighbours())
            back.start()
            r.gain_grad[...] = jnp.zeros_like(r.gain_grad)
            r.head_gain[...] = jnp.zeros_like(r.head_gain)

        def send_attn(c):
            attention_grads(r, back, attn, c)

        def feed_forward(c):
            hat, inverse = norm_parts(r.hidden[...])
            d_in = attn.total(c, chunk)
            r.gain_grad[0:1, :] += row_sums(d_in * hat)
            g = r.g_above[...] + norm_back(d_in, r.attn_gain[...].astype(F32), hat, inverse)
            r.g_held[lax.rem(c, 4)] = g
            g_low = g.astype(BF)
            r.g_low[...] = g_low
            gate, up = r.gates[:, :ff], r.gates[:, ff:]
            d_gates, part = mlp_back(r, g_low, gate, up, jax.nn.sigmoid(gate))
            r.d_gates[...] = d_gates
            mlp.put(c, part)

        def middle_grad(c):
            hat, inverse = norm_parts(r.hidden_mid[...])
            d_in = mlp.total(c, chunk)
            r.gain_grad[1:2, :] += row_sums(d_in * hat)
            g_mid = r.g_held[lax.rem(c, 4)] + norm_back(d_in, r.mlp_gain[...].astype(F32), hat, inverse)
            r.g_mid[...] = g_mid
            mid_low = g_mid.astype(BF)
            r.mid_low[...] = mid_low
            r.d_context[...] = dot(mid_low, r.w_o[...], NT).astype(BF)

        r.arrived(first[1], *QKV_WEIGHTS)
        at_chunk(s, first, send_attn)
        grads.late_slabs(s)
        at_chunk(s, (1, 2, pieces), attn.relay)
        at_chunk(s, (1, 3, pieces), attn.meet)
        r.arrived(second[1], *MLP_WEIGHTS)
        at_chunk(s, second, feed_forward)
        at_chunk(s, (1, 7, pieces), mlp.relay)
        at_chunk(s, (1, 8, pieces), mlp.meet)
        r.arrived(third[1], "w_o")
        at_chunk(s, third, middle_grad)
        grads.run(s)

        @pl.when(s == steps - 1)
        def _():
            grads.store()
            attn.finish()
            mlp.finish()
            back.finish()
            grads.finish()

    return step_kernel(
        between_backward, body, steps,
        attention_grads_ins(a, w, layer, tables, first)
        | grads_ins(a, rows, width, plan.slabs)
        | dict(
            hidden=(a.hidden, second),
            g_above=(g_mid, second),
            gates=(below.gates, second),
            hidden_mid=(below.hidden_mid, third),
            mlp_gain=(w.mlp_gain, Row(layer - 1)),
            w_gate=(w.w_gate, Late(layer - 1)),
            w_up=(w.w_up, Late(layer - 1)),
            w_down=(w.w_down, Late(layer - 1)),
            w_o=(w.w_o, Late(layer - 1)),
        ),
        dict(
            g_low=((rows, width), BF, second),
            d_gates=((rows, 2 * ff), BF, second),
            g_mid=((rows, width), F32, third),
            mid_low=((rows, width), BF, third),
            d_context=((rows, q_width), BF, third),
            gain_grad=((8, width), F32, WHOLE),
            head_gain=((8, 2 * HEAD), F32, WHOLE),
        )
        | grads_outs(width, q_width, k_width, ff),
        dict(
            attn=LineSum.scratch(rows, width, pieces),
            mlp=LineSum.scratch(rows, width, pieces),
            kr=KeyValueReturn.scratch(rows, k_width, chunks, reach),
            **WeightGrads.scratch(rows, width, q_width, k_width, ff),
            g_held=pltpu.VMEM((4, rows // chunks, width), F32),
        ),
        collective_id)


def last_backward(a, top, quarters, above, w, tables, reach, chunks, collective_id):
    g_mid = above.g_mid
    rows, width = g_mid.shape
    q_width, k_width, ff = w.w_q.shape[2], w.w_k.shape[2], w.w_gate.shape[2]
    layer = 0
    pieces = chunks * PIECES
    pairs = max(1, chunks // 2)
    half = rows // 2
    half_pieces = pieces // 2
    out_chunk = min(rows // chunks, half // 2)
    out_count = rows // out_chunk
    first, second = (4, 0, pairs), (PIECES, 13, chunks)
    third = (PIECES * chunks // out_count, 13, out_count)
    steps = max(PIECES * (chunks - 1) + second[1], third[0] * (out_count - 1) + third[1]) + 1
    chunk = rows // chunks
    after = 4 * (pairs - 1)
    slabs = slab_count(chunks)
    plan = types.SimpleNamespace(
        slabs=(2, 0, slabs),
        early=lambda k: min(2 * slabs + 1 + 7 * k, steps - 2),
        late_slabs=(1, after + 3, slabs),
        late=lambda k: min(after + 5 + slabs + 5 * k, steps - 2),
    )

    def body(r, s):
        back = KeyValueReturn(r, reach)
        attn, upper = LineSum(r.attn), LineSum(r.upper, r.upper_part)
        grads = WeightGrads(r, plan)
        sums = Butterfly(r.sums)

        @pl.when(s == 0)
        def _():
            enter(attn.neighbours() + back.neighbours() + sums.neighbours())
            back.start()
            upper.push(0, half)
            r.head_gain[...] = jnp.zeros_like(r.head_gain)
            r.gain_held[...] = jnp.zeros_like(r.gain_held)

        def send_attn(c):
            part = attention_grads(r, back, attn, c)
            hat, _ = norm_parts(r.hidden[...].astype(F32))
            r.gain_held[...] += row_sums(part * hat)

        def give_output(c):
            per = out_count // 4
            for q in range(2):

                @pl.when((c >= q * per) & (c < (q + 1) * per))
                def _():
                    here = pl.ds(pl.multiple_of(jnp.clip(c - q * per, 0, per - 1) * out_chunk, out_chunk), out_chunk)
                    total = (r.quarter_0, r.quarter_1)[q][here, :].astype(F32)
                    r.output[...] = (r.hidden_mid[...] + total).astype(BF)

            @pl.when(c >= 2 * per)
            def _():
                r.output[...] = (r.hidden_mid[...] + upper.total(c - 2 * per, out_chunk)).astype(BF)

        def give_input(c):
            hat, inverse = norm_parts(r.hidden_late[...].astype(F32))
            r.input_grad[...] = r.g_above[...] + norm_back(attn.total(c, chunk), r.attn_gain[...].astype(F32), hat, inverse)

        r.arrived(first[1], *QKV_WEIGHTS)
        at_chunk(s, first, send_attn)
        grads.late_slabs(s)
        at_chunk(s, (1, 0, half_pieces), upper.relay)
        at_chunk(s, (1, 8, pieces), attn.relay)
        at_chunk(s, (1, 2, half_pieces), upper.meet)
        at_chunk(s, (1, 10, pieces), attn.meet)
        at_chunk(s, third, give_output)
        at_chunk(s, second, give_input)
        grads.run(s)

        @pl.when(s == after + 1)
        def _():
            row = lax.broadcasted_iota(jnp.int32, (8, width), 0)
            once = jnp.where(lax.axis_index("tensor") == 0, 1.0, 0.0)
            heads = [r.head_gain[0:1, :], r.above_head_gain[0:1, :], jnp.zeros((1, width - 4 * HEAD), F32)]
            packet = jnp.zeros((8, width), F32)
            for place, part in enumerate([
                r.gain_held[...], r.above_gain[0:1, :] * once, r.above_gain[1:2, :] * once, r.top_gain[0:1, :] * once,
                jnp.concatenate(heads, 1),
            ]):
                packet = jnp.where(row == place, part, packet)
            sums.put(packet)

        for k in range(len(sums.axes)):

            @pl.when(s == max(steps - len(sums.axes) - 4 + k, after + 2))
            def _():
                sums.fold(k)

        @pl.when(s == steps - 1)
        def _():
            grads.store()
            r.gains[...] = sums.total()
            attn.finish()
            upper.finish()
            back.finish()
            grads.finish()
            sums.finish()

    return step_kernel(
        last_backward, body, steps,
        attention_grads_ins(a, w, layer, tables, first)
        | grads_ins(a, rows, width, plan.slabs)
        | dict(
            hidden=(a.hidden, first),
            hidden_late=(a.hidden, second),
            g_above=(g_mid, second),
            above_gain=(above.gain_grad, WHOLE),
            above_head_gain=(above.head_gain, WHOLE),
            top_gain=(top.gain_grad, WHOLE),
            upper_part=(top.upper_part, WHOLE),
            quarter_0=(quarters[0], WHOLE),
            quarter_1=(quarters[1], WHOLE),
            hidden_mid=(top.hidden_mid, third),
        ),
        dict(
            input_grad=((rows, width), F32, second),
            output=((rows, width), BF, third),
            gains=((8, width), F32, WHOLE),
        )
        | grads_outs(width, q_width, k_width, ff),
        dict(
            attn=LineSum.scratch(rows, width, pieces),
            upper=LineSum.scratch(half, width, half_pieces, False),
            kr=KeyValueReturn.scratch(rows, k_width, pairs, reach),
            **WeightGrads.scratch(rows, width, q_width, k_width, ff),
            sums=Butterfly.scratch((8, width)),
            head_gain=pltpu.VMEM((8, 2 * HEAD), F32),
            gain_held=pltpu.VMEM((1, width), F32),
        ),
        collective_id)


def collect_kernel(count, output_in, input_in, gains, *refs):
    ins, (output, input_grad, attn, mlp, q_gain, k_gain), outs = refs[: 2 * count], refs[2 * count : 2 * count + 6], refs[2 * count + 6 :]
    output[...] = output_in[...]
    input_grad[...] = input_in[...]
    s = pl.program_id(0)

    @pl.when(s == 0)
    def _():
        attn[...] = gains[0:2, :]
        mlp[...] = gains[2:4, :]
        for layer in range(2):
            at = 2 * layer * HEAD
            q_gain[layer : layer + 1, :] = gains[4:5, at : at + HEAD]
            k_gain[layer : layer + 1, :] = gains[4:5, at + HEAD : at + 2 * HEAD]

    for g in range(count):
        for layer in range(2):
            value = ins[2 * g + layer]
            if outs[g].shape[1] == value.shape[0]:
                outs[g][layer] = value[...]
            else:

                @pl.when(s == 0)
                def _():
                    outs[g][layer] = value[...].T


def collect(end, above):
    rows, width = end.output.shape
    straight = [(k.grad_q, k.grad_k, k.grad_v, k.grad_gate, k.grad_up) for k in (end, above)]
    turned = [(k.grad_o, k.grad_down) for k in (end, above)]
    per = straight[0][0].shape[0]
    steps = max(1, min(2, per // 8))
    whole = pl.BlockSpec(memory_space=pltpu.VMEM)

    def blocks(array):
        return pl.BlockSpec((array.shape[0] // steps, array.shape[1]), lambda s: (s, 0))

    ins = [end.output, end.input_grad, end.gains]
    in_specs = [blocks(end.output), blocks(end.input_grad), whole]
    outs = [
        ((rows, width), BF, blocks(end.output)), ((rows, width), F32, blocks(end.input_grad)),
        ((2, width), F32, whole), ((2, width), F32, whole), ((2, HEAD), F32, whole), ((2, HEAD), F32, whole),
    ]
    for pair in zip(*straight):
        ins += pair
        in_specs += [blocks(a) for a in pair]
        shape = pair[0].shape
        outs.append(((2,) + shape, F32, pl.BlockSpec((2, per // steps, shape[1]), lambda s: (0, s, 0))))
    for pair in zip(*turned):
        ins += pair
        in_specs += [whole, whole]
        outs.append(((2,) + pair[0].shape[::-1], F32, whole))
    return pl.pallas_call(
        functools.partial(collect_kernel, 7),
        grid=(steps,),
        in_specs=in_specs,
        out_specs=[o[2] for o in outs],
        out_shape=[jax.ShapeDtypeStruct(o[0], o[1]) for o in outs],
        name=collect.__name__,
        compiler_params=pltpu.CompilerParams(vmem_limit_bytes=62 << 20),
    )(*ins)


def per_device(
    tokens, cotangent, segments, positions, attn_gain, w_query, key_projection, value_projection, query_gain, key_gain,
    w_output, mlp_gain, w_gate, w_up, w_down,
):
    seqs_here, stretch, width = tokens.shape
    rows = seqs_here * stretch
    reach = min(lax.axis_size("seq") - 1, (WINDOW + stretch - 2) // stretch)
    chunks = rows // min(CHUNK, stretch)

    w = types.SimpleNamespace(
        attn_gain=attn_gain, mlp_gain=mlp_gain, q_gain=query_gain, k_gain=key_gain,
        w_q=w_query, w_k=key_projection, w_v=value_projection, w_o=w_output, w_gate=w_gate, w_up=w_up, w_down=w_down,
    )
    tokens = tokens.reshape(rows, width)
    cotangent = cotangent.reshape(rows, width)

    a0 = first_projection(tokens, segments, positions, w, stretch, reach, rows // min(2 * CHUNK, stretch), 1)
    tables, low = a0.tables, a0.low
    a0.hidden = tokens
    mid = between_forward(a0, low, w, 0, tables, stretch, reach, chunks, 2)
    a0.context, a0.lse = mid.context, mid.lse
    a1 = types.SimpleNamespace(
        attn_low=mid.attn_low, raw=mid.raw, queries=mid.queries, window=mid.window,
        hidden=mid.hidden_next)
    turn = turn_around(a1, low, cotangent, w, 1, stretch, chunks, 3)
    a1.context, a1.lse = turn.context, turn.lse
    a1.mlp_low, a1.act, a1.d_gates = turn.mlp_low, turn.act, turn.d_gates
    a1.mid_low, a1.g_low = turn.mid_low, cotangent
    pieces = chunks * FINE // 4
    back = attention_backward(a1, turn.d_context, low, turn.lower_part, 0, stretch, pieces, 6)
    a1.d_q, a1.d_own, a1.d_prev = back.d_q, back.d_own, back.d_prev
    quarters = [back.total]
    down = between_backward(a1, mid, turn.g_mid, w, 1, tables, reach, chunks, 4)
    a0.mlp_low, a0.act, a0.d_gates = mid.mlp_low, mid.act, down.d_gates
    a0.mid_low, a0.g_low = down.mid_low, down.g_low
    back = attention_backward(a0, down.d_context, low, turn.lower_part, 1, stretch, pieces, 7)
    a0.d_q, a0.d_own, a0.d_prev = back.d_q, back.d_own, back.d_prev
    quarters.append(back.total)
    end = last_backward(a0, turn, quarters, down, w, tables, reach, chunks, 5)
    output, input_grad, attn, mlp, q_gain, k_gain, d_q, d_k, d_v, d_gate, d_up, d_o, d_down = collect(end, down)
    shape = (seqs_here, stretch, width)
    return (
        output.reshape(shape), input_grad.reshape(shape), attn, d_q, d_k, d_v, q_gain, k_gain, d_o, mlp, d_gate, d_up,
        d_down,
    )


def solution(mesh):
    placed = (
        P("dp", "seq", None), P("dp", "seq", None), P("dp", "seq"), P("dp", "seq"), P(), P(None, None, "tensor"),
        P(None, None, "tensor"), P(None, None, "tensor"), P(), P(), P(None, "tensor", None), P(),
        P(None, None, "tensor"), P(None, None, "tensor"), P(None, "tensor", None),
    )
    by_rows = P(None, ("dp", "seq"), "tensor")
    by_columns = P(None, "tensor", ("dp", "seq"))
    return jax.shard_map(
        per_device,
        mesh=mesh,
        in_specs=placed,
        out_specs=(
            P("dp", "seq", None), P("dp", "seq", None), P(), by_rows, by_rows, by_rows, P(), P(), by_columns, P(),
            by_rows, by_rows, by_columns,
        ),
        check_vma=False,
    )
```

```python
import functools
import types

import jax
import jax.numpy as jnp
import numpy as np
from jax import lax
from jax.experimental import pallas as pl
from jax.experimental.pallas import tpu as pltpu
from jax.sharding import PartitionSpec as P

HEAD = 128
LAYER_COUNT = 2
WINDOW = 1024
EPS = 1e-06
THETA = 1000000.0
LOG2E = 1.4426950408889634
SCALE = HEAD ** (-0.5)
CHUNK = 128
PIECES = 2
FINE = 4
MESH = pl.DeviceIdType.MESH
BF = jnp.bfloat16
F32 = jnp.float32

NT = (((1,), (1,)), ((), ()))
NN = (((1,), (0,)), ((), ()))
TN = (((0,), (0,)), ((), ()))


def dot(a, b, dims=NN):
    return lax.dot_general(a, b, dims, preferred_element_type=F32)


def chunk_index(schedule, s):
    rate, lag, count = schedule
    return jnp.clip((s - lag) // rate, 0, count - 1)


def rows_spec(schedule, shape):
    return pl.BlockSpec((shape[0] // schedule[2], shape[1]), lambda s: (chunk_index(schedule, s), 0))


WHOLE, HBM = object(), object()
MLP_WEIGHTS = ("w_gate", "w_up", "w_down")
QKV_WEIGHTS = ("w_q", "w_k", "w_v")
GRAD_OPERANDS = ("d_gates_all", "context_all", "act_all")


class Row:
    def __init__(self, layer):
        self.layer = layer


class Late:
    def __init__(self, layer=None):
        self.layer = layer

    def shape(self, array):
        return array.shape if self.layer is None else array.shape[1:]

    def copy(self, source, held, sem):
        return pltpu.make_async_copy(source if self.layer is None else source.at[self.layer], held, sem)


def step_kernel(owner, body, steps, ins, outs, scratch, collective_id, vmem=62):
    def spec(shape, where, is_in):
        if isinstance(where, pl.BlockSpec):
            return where
        if where is HBM or isinstance(where, Late):
            return pl.BlockSpec(memory_space=pl.ANY)
        if where is WHOLE or isinstance(where, Row):
            zeros = (0,) * len(shape)
            if is_in:
                return pl.BlockSpec(shape, lambda s: zeros, pipeline_mode=pl.Buffered(1))
            return pl.BlockSpec(memory_space=pltpu.VMEM)
        return rows_spec(where, shape)

    late = {name: where for name, (_, where) in ins.items() if isinstance(where, Late)}
    held = {name: pltpu.VMEM(where.shape(ins[name][0]), ins[name][0].dtype) for name, where in late.items()}
    flat, tree = jax.tree.flatten((scratch, held, {name: pltpu.SemaphoreType.DMA(()) for name in late}))

    def kernel(*refs):
        named = dict(zip(ins, refs))
        named.update(zip(outs, refs[len(ins) :]))
        own, held_refs, sems = jax.tree.unflatten(tree, refs[len(ins) + len(outs) :])
        copies = {name: where.copy(named[name], held_refs[name], sems[name]) for name, where in late.items()}
        for name, ref in own.items():
            named[name] = types.SimpleNamespace(**ref) if isinstance(ref, dict) else ref
        named.update(held_refs)
        for name, (_, where) in ins.items():
            if isinstance(where, Row):
                named[name] = named[name].at[where.layer : where.layer + 1]
        s = pl.program_id(0)

        @pl.when(s == 0)
        def _():
            for copy in copies.values():
                copy.start()

        def arrived(step, *names):
            @pl.when(s == step)
            def _():
                for name in names:
                    copies[name].wait()

        body(types.SimpleNamespace(arrived=arrived, **named), s)

    results = pl.pallas_call(
        kernel,
        grid=(steps,),
        in_specs=[spec(a.shape, w, True) for a, w in ins.values()],
        out_specs=[spec(shape, w, False) for shape, _, w in outs.values()],
        out_shape=[jax.ShapeDtypeStruct(shape, dtype) for shape, dtype, _ in outs.values()],
        scratch_shapes=flat,
        name=owner.__name__,
        compiler_params=pltpu.CompilerParams(
            collective_id=collective_id, has_side_effects=True, vmem_limit_bytes=vmem << 20
        ),
    )(*[a for a, _ in ins.values()])
    return types.SimpleNamespace(**dict(zip(outs, results)))


def at_chunk(s, schedule, work):
    rate, lag, count = schedule
    moved = s - lag
    here = (moved >= 0) & (moved < rate * count)
    if rate > 1:
        here = here & (lax.rem(moved, rate) == 0)

    @pl.when(here)
    def _():
        work(moved // rate if rate > 1 else moved)


def enter(devices):
    barrier = pltpu.get_barrier_semaphore()
    count = 0
    for device, exists in devices:
        if exists is True:
            pl.semaphore_signal(barrier, inc=1, device_id=device, device_id_type=MESH)
            count = count + 1
        else:

            @pl.when(exists)
            def _():
                pl.semaphore_signal(barrier, inc=1, device_id=device, device_id_type=MESH)

            count = count + jnp.where(exists, 1, 0)
    pl.semaphore_wait(barrier, count)


class LineSum:
    def __init__(self, refs, x=None):
        self.x, self.land = refs.x if x is None else x, refs.land
        self.send_sem, self.land_sem, self.out_sem = refs.send, refs.arrive, refs.out
        self.pieces = self.send_sem.shape[0]
        self.rows = self.x.shape[0] // self.pieces
        n = lax.axis_size("tensor")
        z = lax.axis_index("tensor")
        half = n // 2
        self.middle = (z == half - 1) | (z == half)
        self.has_outer = (z > 0) & (z < n - 1)
        self.inner = jnp.where(z < half, z + 1, z - 1)
        self.outer = jnp.clip(jnp.where(z < half, z - 1, z + 1), 0, n - 1)
        self.slot = jnp.where(self.middle, 1, 0)

    @staticmethod
    def scratch(rows, width, pieces, own=True):
        held = dict(x=pltpu.VMEM((rows, width), BF)) if own else {}
        return held | dict(
            land=pltpu.VMEM((2, rows, width), BF),
            send=pltpu.SemaphoreType.DMA((pieces,)),
            arrive=pltpu.SemaphoreType.DMA((2, pieces)),
            out=pltpu.SemaphoreType.DMA((pieces,)),
        )

    def neighbours(self):
        return [({"tensor": self.inner}, True), ({"tensor": self.outer}, self.has_outer)]

    def at(self, j, rows=None):
        rows = rows or self.rows
        return pl.ds(pl.multiple_of(j * rows, rows), rows)

    def inward(self, source, j, slot):
        return pltpu.make_async_remote_copy(
            source.at[self.at(j)], self.land.at[slot, self.at(j)], self.send_sem.at[j], self.land_sem.at[slot, j],
            device_id={"tensor": self.inner}, device_id_type=MESH)

    def outward(self, j):
        return pltpu.make_async_remote_copy(
            self.land.at[1, self.at(j)], self.land.at[1, self.at(j)], self.out_sem.at[j], self.land_sem.at[1, j],
            device_id={"tensor": self.outer}, device_id_type=MESH)

    def put(self, c, value):
        rows = value.shape[0]
        self.x[self.at(c, rows), :] = value.astype(BF)
        self.push(c, rows)

    def push(self, c, rows):
        @pl.when(jnp.logical_not(self.has_outer))
        def _():
            for i in range(rows // self.rows):
                self.inward(self.x, c * (rows // self.rows) + i, self.slot).start()

    def add(self, j, source, slot):
        self.land[slot, self.at(j), :] = (
            source[self.at(j), :].astype(F32) + self.land[slot, self.at(j), :].astype(F32)
        ).astype(BF)

    def relay(self, j):
        @pl.when(self.has_outer)
        def _():
            self.inward(self.x, j, 0).wait_recv()
            self.add(j, self.x, 0)
            self.inward(self.land.at[0], j, self.slot).start()

    def meet(self, j):
        @pl.when(self.middle)
        def _():
            self.inward(self.x, j, 1).wait_recv()

            @pl.when(self.has_outer)
            def _():
                self.add(j, self.land.at[0], 1)
                self.outward(j).start()

            @pl.when(jnp.logical_not(self.has_outer))
            def _():
                self.add(j, self.x, 1)

    def total(self, c, rows):
        @pl.when(jnp.logical_not(self.middle))
        def _():
            for i in range(rows // self.rows):
                j = c * (rows // self.rows) + i
                self.inward(self.x, j, 1).wait_recv()

                @pl.when(self.has_outer)
                def _():
                    self.outward(j).start()

        return self.land[1, self.at(c, rows), :].astype(F32)

    def finish(self):
        @pl.when(self.has_outer)
        def _():
            @pl.loop(0, self.pieces)
            def _(j):
                self.inward(self.land.at[0], j, self.slot).wait_send()
                self.outward(j).wait_send()

        @pl.when(jnp.logical_not(self.has_outer))
        def _():
            @pl.loop(0, self.pieces)
            def _(j):
                self.inward(self.x, j, self.slot).wait_send()


class KeyValueSend:
    def __init__(self, refs, reach, stretch):
        self.held, self.zeros, self.window = refs.kv.held, refs.kv.zeros, refs.window
        self.copy_sem, self.send_sem, self.land_sem = refs.kv.copy, refs.kv.send, refs.kv.land
        self.chunks = self.copy_sem.shape[0]
        self.rows = self.held.shape[0] // self.chunks
        self.reach, self.stretch = reach, stretch
        self.place = lax.axis_index("seq")
        self.count = lax.axis_size("seq")

    @staticmethod
    def scratch(rows, width, chunks, reach):
        held = max(reach, 1)
        return dict(
            held=pltpu.VMEM((rows, width), BF),
            zeros=pltpu.VMEM((rows // chunks, width), BF),
            copy=pltpu.SemaphoreType.DMA((chunks,)),
            send=pltpu.SemaphoreType.DMA((held, chunks)),
            land=pltpu.SemaphoreType.DMA((held, chunks)),
        )

    def neighbours(self):
        found = []
        for back in range(1, self.reach + 1):
            found.append(({"seq": jnp.minimum(self.place + back, self.count - 1)}, self.place + back < self.count))
            found.append(({"seq": jnp.maximum(self.place - back, 0)}, self.place >= back))
        return found

    def at(self, c):
        return pl.ds(pl.multiple_of(c * self.rows, self.rows), self.rows)

    def there(self, back, c):
        per = self.stretch // self.rows
        chunk = ((c // per) * (self.reach + 1) + self.reach - back) * per + lax.rem(c, per)
        return self.window.at[self.at(chunk)]

    def own(self, c):
        return pltpu.make_async_copy(self.held.at[self.at(c)], self.there(0, c), self.copy_sem.at[c])

    def blank(self, back, c):
        return pltpu.make_async_copy(self.zeros, self.there(back, c), self.land_sem.at[back - 1, c])

    def remote(self, back, c):
        return pltpu.make_async_remote_copy(
            self.held.at[self.at(c)], self.there(back, c), self.send_sem.at[back - 1, c],
            self.land_sem.at[back - 1, c],
            device_id={"seq": jnp.minimum(self.place + back, self.count - 1)}, device_id_type=MESH)

    def start(self):
        self.zeros[...] = jnp.zeros_like(self.zeros)

    def send(self, c):
        self.own(c).start()
        for back in range(1, self.reach + 1):

            @pl.when(self.place + back < self.count)
            def _():
                self.remote(back, c).start()

            @pl.when(self.place < back)
            def _():
                self.blank(back, c).start()

    def finish(self):
        @pl.loop(0, self.chunks)
        def _(c):
            self.own(c).wait()
            for back in range(1, self.reach + 1):

                @pl.when(self.place + back < self.count)
                def _():
                    self.remote(back, c).wait_send()

                @pl.when(self.place >= back)
                def _():
                    self.remote(back, c).wait_recv()

                @pl.when(self.place < back)
                def _():
                    self.blank(back, c).wait()


class KeyValueReturn:
    def __init__(self, refs, reach):
        self.prev, self.land = refs.d_prev, refs.kr.land
        self.send_sem, self.land_sem = refs.kr.send, refs.kr.arrive
        self.chunks = self.send_sem.shape[1]
        self.rows = self.land.shape[2] // self.chunks
        self.reach = reach
        self.place = lax.axis_index("seq")
        self.count = lax.axis_size("seq")

    @staticmethod
    def scratch(rows, width, chunks, reach):
        held = max(reach, 1)
        return dict(
            land=pltpu.VMEM((held, 2, rows, width), BF),
            send=pltpu.SemaphoreType.DMA((held, chunks)),
            arrive=pltpu.SemaphoreType.DMA((held, chunks)),
        )

    neighbours = KeyValueSend.neighbours
    at = KeyValueSend.at

    def copy(self, back, c):
        return pltpu.make_async_remote_copy(
            self.prev.at[self.reach - back, :, self.at(c)], self.land.at[back - 1, :, self.at(c)],
            self.send_sem.at[back - 1, c], self.land_sem.at[back - 1, c],
            device_id={"seq": jnp.maximum(self.place - back, 0)}, device_id_type=MESH)

    def start(self):
        for back in range(1, self.reach + 1):

            @pl.when(self.place >= back)
            def _():
                @pl.loop(0, self.chunks)
                def _(c):
                    self.copy(back, c).start()

    def add(self, own, c):
        for back in range(1, self.reach + 1):
            exists = self.place + back < self.count

            @pl.when(exists)
            def _():
                self.copy(back, c).wait_recv()

            own = own + jnp.where(exists, self.land[back - 1, :, self.at(c), :].astype(F32), 0.0)
        return own

    def finish(self):
        for back in range(1, self.reach + 1):

            @pl.when(self.place >= back)
            def _():
                @pl.loop(0, self.chunks)
                def _(c):
                    self.copy(back, c).wait_send()


def device_bit(axis):
    name, b = axis
    return lax.rem(lax.axis_index(name) // (1 << b), 2)


def device_partner(axis):
    name, b = axis
    return {name: lax.axis_index(name) + (1 - 2 * device_bit(axis)) * (1 << b)}


def bits_of(name):
    return lax.axis_size(name).bit_length() - 1


def block_axes():
    return [(name, b) for name in ("dp", "seq") for b in reversed(range(bits_of(name)))]


class Scatter:
    def __init__(self, refs, swapped):
        self.axes = block_axes()
        phases = len(self.axes)
        near = [k for k in range(phases) if self.axes[k][0] == "seq"][::-1]
        far = [k for k in range(phases) if self.axes[k][0] == "dp"]
        self.order = near + (far if swapped else far[::-1])
        self.buffer, self.lands = refs.held, refs.lands
        self.send_sem, self.land_sem = refs.send, refs.arrive

    @staticmethod
    def scratch(rows, width):
        phases = len(block_axes())
        return dict(
            held=pltpu.VMEM((2,) * phases + (rows, width), BF),
            lands=[pltpu.VMEM((2,) * (phases - k - 1) + (rows, width), BF) for k in range(phases)],
            send=pltpu.SemaphoreType.DMA((phases,)),
            arrive=pltpu.SemaphoreType.DMA((phases,)),
        )

    def neighbours(self):
        return [(device_partner(axis), True) for axis in self.axes]

    def put(self, block, columns, value):
        phases = len(self.axes)
        place = tuple(lax.rem(block // (1 << (phases - 1 - k)), 2) for k in range(phases))
        self.buffer[place + (slice(None), columns)] = value.astype(BF)

    def view(self, k, mine):
        index = [slice(None)] * len(self.axes)
        for earlier in self.order[:k]:
            index[earlier] = device_bit(self.axes[earlier])
        bit = device_bit(self.axes[self.order[k]])
        index[self.order[k]] = bit if mine else 1 - bit
        return tuple(index)

    def copy(self, k):
        return pltpu.make_async_remote_copy(
            self.buffer.at[self.view(k, False)], self.lands[k], self.send_sem.at[k], self.land_sem.at[k],
            device_id=device_partner(self.axes[self.order[k]]), device_id_type=MESH)

    def send(self, k):
        self.copy(k).start()

    def fold(self, k, store=None):
        self.copy(k).wait_recv()
        index = self.view(k, True)
        free = [i for i, v in enumerate(index) if isinstance(v, slice)]
        for j in range(1 << len(free)):
            place = [(j >> (len(free) - 1 - i)) & 1 for i in range(len(free))]
            here = list(index)
            for i, axis in enumerate(free):
                here[axis] = place[i]
            here = tuple(here)
            total = self.buffer[here].astype(F32) + self.lands[k][tuple(place)].astype(F32)
            if store is None:
                self.buffer[here] = total.astype(BF)
            else:
                store(total)

    def finish(self):
        for k in range(len(self.axes)):
            self.copy(k).wait_send()


class Butterfly:
    def __init__(self, refs):
        self.axes = [(name, b) for name in ("seq", "dp", "tensor") for b in range(bits_of(name))]
        self.held, self.land = refs.held, refs.land
        self.send_sem, self.land_sem = refs.send, refs.arrive

    @staticmethod
    def scratch(shape):
        phases = bits_of("seq") + bits_of("dp") + bits_of("tensor")
        return dict(
            held=pltpu.VMEM((phases + 1,) + shape, F32),
            land=pltpu.VMEM((phases,) + shape, F32),
            send=pltpu.SemaphoreType.DMA((phases,)),
            arrive=pltpu.SemaphoreType.DMA((phases,)),
        )

    def neighbours(self):
        return [(device_partner(axis), True) for axis in self.axes]

    def copy(self, k):
        return pltpu.make_async_remote_copy(
            self.held.at[k], self.land.at[k], self.send_sem.at[k], self.land_sem.at[k],
            device_id=device_partner(self.axes[k]), device_id_type=MESH)

    def put(self, value):
        self.held[0] = value
        self.copy(0).start()

    def fold(self, k):
        self.copy(k).wait_recv()
        self.held[k + 1] = self.held[k] + self.land[k]
        if k + 1 < len(self.axes):
            self.copy(k + 1).start()

    def total(self):
        return self.held[len(self.axes)]

    def finish(self):
        for k in range(len(self.axes)):
            self.copy(k).wait_send()


def norm_parts(value):
    inverse = lax.rsqrt(jnp.mean(value * value, -1, keepdims=True) + EPS)
    return value * inverse, inverse


def norm_back(grad, gain, hat, inverse):
    scaled = grad * gain
    inner = jnp.mean(scaled * hat, -1, keepdims=True)
    return inverse * (scaled - hat * inner)


def row_sums(value):
    return jnp.sum(value, 0, keepdims=True)


def heads_of(value):
    return [value[:, h * HEAD : (h + 1) * HEAD] for h in range(value.shape[1] // HEAD)]


def rope(value, cosine, signed_sine):
    return value * cosine + pltpu.roll(value, HEAD // 2, 1) * signed_sine


def rope_back(grad, cosine, signed_sine):
    return grad * cosine - pltpu.roll(grad, HEAD // 2, 1) * signed_sine


def attend(r, c, stretch):
    rows, span = r.queries_in.shape[0], r.window_in.shape[0] // (r.low.shape[1] // stretch)
    offset = span - stretch
    per = stretch // rows
    length = min(WINDOW + rows, span)
    q_start = offset + lax.rem(c, per) * rows
    start = jnp.clip(q_start + rows - length, 0, span - length)
    here = pl.ds(pl.multiple_of((c // per) * span + start, rows), length)
    group = r.queries_in.shape[1] * 2 // r.window_in.shape[1]
    low = r.low[:, pl.ds(pl.multiple_of(c * rows, rows), rows)].astype(F32)
    low = jnp.broadcast_to(low, (HEAD, rows)).T[:, :1]
    key_index = (start + lax.broadcasted_iota(jnp.int32, (rows, length), 1)).astype(F32)
    q_index = (q_start + lax.broadcasted_iota(jnp.int32, (rows, 1), 0)).astype(F32)
    mask = (key_index >= low) & (key_index <= q_index)
    mask = jnp.concatenate([mask] * group, 0)
    queries = heads_of(r.queries_in[...])
    kv_heads = len(queries) // group
    outs = []
    for g in range(kv_heads):
        keys = r.window_in[here, g * HEAD : (g + 1) * HEAD]
        values = r.window_in[here, (kv_heads + g) * HEAD : (kv_heads + g + 1) * HEAD]
        s = dot(jnp.concatenate(queries[g * group : (g + 1) * group], 0), keys, NT) * (SCALE * LOG2E)
        p = jnp.where(mask, jnp.exp2(s), 0.0)
        part = p[:, :HEAD]
        for k in range(1, length // HEAD):
            part = part + p[:, k * HEAD : (k + 1) * HEAD]
        total = jnp.sum(part, 1, keepdims=True)
        o = (dot(p.astype(BF), values) / total).astype(BF)
        log_total = jnp.broadcast_to(jnp.log2(total), (group * rows, HEAD))
        for h in range(group):
            outs.append(o[h * rows : (h + 1) * rows])
            r.lse[g, h : h + 1, :] = log_total[h * rows : (h + 1) * rows].T[0:1, :]
    context = jnp.concatenate(outs, 1)
    r.context[...] = context
    return context


def attend_ins(a, low, when):
    return dict(
        queries_in=(a.queries, when),
        window_in=(a.window, Late()),
        low=(low, WHOLE),
    )


def attend_outs(a, when):
    kv_heads = a.window.shape[1] // (2 * HEAD)
    rows, width = a.queries.shape
    shape = (kv_heads, width // (kv_heads * HEAD), rows)
    return dict(
        context=((rows, width), BF, when),
        lse=(shape, F32, pl.BlockSpec(shape[:2] + (rows // when[2],), lambda s: (0, 0, chunk_index(when, s)))),
    )


def project(r, hidden, kv, c):
    hat, _ = norm_parts(hidden)
    low = (hat * r.attn_gain[...].astype(F32)).astype(BF)
    r.attn_low[...] = low
    q_raw = dot(low, r.w_q[...])
    k_raw = dot(low, r.w_k[...])
    values = dot(low, r.w_v[...])
    r.raw[...] = jnp.concatenate([q_raw, k_raw], 1)
    cosine, sine = r.tables[:, :HEAD], r.tables[:, HEAD:]

    def turned(raw, gain):
        return jnp.concatenate(
            [rope(norm_parts(u)[0] * gain, cosine, sine).astype(BF) for u in heads_of(raw)], 1)

    r.queries[...] = turned(q_raw, r.q_gain[...].astype(F32))
    kv.held[kv.at(c), :] = jnp.concatenate([turned(k_raw, r.k_gain[...].astype(F32)), values.astype(BF)], 1)
    kv.send(c)


def project_outs(rows, width, w, stretch, reach, when):
    q_width, k_width = w.w_q.shape[2], w.w_k.shape[2]
    return dict(
        attn_low=((rows, width), BF, when),
        raw=((rows, q_width + k_width), F32, when),
        queries=((rows, q_width), BF, when),
        window=((rows // stretch * (reach + 1) * stretch, k_width + w.w_v.shape[2]), BF, HBM),
    )


def project_ins(w, layer, tables, when):
    def weight(array):
        if tables is not None:
            return array, Late(layer)
        shape = array.shape[1:]
        return array, pl.BlockSpec((None,) + shape, lambda s: (layer, 0, 0), pipeline_mode=pl.Buffered(1))

    return dict(
        attn_gain=(w.attn_gain, Row(layer)),
        w_q=weight(w.w_q),
        w_k=weight(w.w_k),
        w_v=weight(w.w_v),
        q_gain=(w.q_gain, Row(layer)),
        k_gain=(w.k_gain, Row(layer)),
    ) | ({} if tables is None else dict(tables=(tables, when)))


def mlp_gates(r, low):
    gate = dot(low, r.w_gate[...])
    up = dot(low, r.w_up[...])
    sigma = jax.nn.sigmoid(gate)
    return gate, up, sigma


def mlp_back(r, g_low, gate, up, sigma):
    d_act = dot(g_low, r.w_down[...], NT)
    d_gate = (d_act * up * sigma * (1.0 + gate * (1.0 - sigma))).astype(BF)
    d_up = (d_act * gate * sigma).astype(BF)
    return jnp.concatenate([d_gate, d_up], 1), dot(d_gate, r.w_gate[...], NT) + dot(d_up, r.w_up[...], NT)


def first_projection(hidden, segments, positions, w, stretch, reach, chunks, collective_id):
    rows, width = hidden.shape
    when = (1, 0, chunks)
    kv_width = w.w_k.shape[2] + w.w_v.shape[2]

    held = max(reach, 1)
    seqs = rows // stretch

    def body(r, s):
        kv = KeyValueSend(r, reach, stretch)

        def documents(back):
            return pltpu.make_async_remote_copy(
                r.segments, r.docs.at[back - 1], r.doc_send.at[back - 1], r.doc_land.at[back - 1],
                device_id={"seq": jnp.minimum(kv.place + back, kv.count - 1)}, device_id_type=MESH)

        @pl.when(s == 0)
        def _():
            r.docs[...] = jnp.full_like(r.docs, -1)
            enter(kv.neighbours())
            kv.start()
            for back in range(1, reach + 1):

                @pl.when(kv.place + back < kv.count)
                def _():
                    documents(back).start()

        angle = jnp.broadcast_to(r.positions[...].astype(F32), (HEAD, rows // chunks)).T * r.frequency[...]
        lane = lax.broadcasted_iota(jnp.int32, angle.shape, 1)
        sine = jnp.sin(angle)
        r.tables[...] = jnp.concatenate([jnp.cos(angle), jnp.where(lane < HEAD // 2, -sine, sine)], 1)
        project(r, r.hidden[...].astype(F32), kv, s)

        @pl.when(s == chunks - 1)
        def _():
            kv.finish()
            for back in range(1, reach + 1):

                @pl.when(kv.place + back < kv.count)
                def _():
                    documents(back).wait_send()

                @pl.when(kv.place >= back)
                def _():
                    documents(back).wait_recv()

            for q in range(seqs):
                here = slice(q * stretch, (q + 1) * stretch)
                own = r.segments[:, here]
                docs = [r.docs[back - 1, :, here] for back in range(1, reach + 1)]

                def first_of(document):
                    counts = [jnp.sum((d < document).astype(jnp.int32), 1, keepdims=True) for d in docs + [own]]
                    return functools.reduce(jnp.add, counts)

                low = jnp.broadcast_to(first_of(0), own.shape)
                for document in range(1, 4):
                    low = jnp.where(own >= document, first_of(document), low)
                index = lax.broadcasted_iota(jnp.int32, own.shape, 1)
                r.low[:, here] = jnp.maximum(low, reach * stretch + index - (WINDOW - 1))

    frequency = (THETA ** (-np.arange(0, HEAD, 2) / HEAD)).astype(np.float32)
    return step_kernel(
        first_projection, body, chunks,
        dict(
            hidden=(hidden, when),
            segments=(segments.reshape(1, rows), WHOLE),
            positions=(
                positions.reshape(1, rows), pl.BlockSpec((1, rows // chunks), lambda s: (0, chunk_index(when, s)))),
            frequency=(jnp.asarray(np.concatenate([frequency, frequency])[None]), WHOLE),
        )
        | project_ins(w, 0, None, when),
        project_outs(rows, width, w, stretch, reach, when)
        | dict(
            tables=((rows, 2 * HEAD), F32, when),
            low=((1, rows), jnp.int32, WHOLE),
        ),
        dict(
            kv=KeyValueSend.scratch(rows, kv_width, chunks, reach),
            docs=pltpu.VMEM((held, 1, rows), jnp.int32),
            doc_send=pltpu.SemaphoreType.DMA((held,)),
            doc_land=pltpu.SemaphoreType.DMA((held,)),
        ),
        collective_id)


def between_forward(a, low, w, layer, tables, stretch, reach, chunks, collective_id):
    hidden = a.hidden
    rows, width = hidden.shape
    kv_width = w.w_k.shape[2] + w.w_v.shape[2]
    ff = w.w_gate.shape[2]
    pieces = chunks * FINE
    first, second, third = (FINE, 0, chunks), (FINE, 8, chunks), (FINE, 17, chunks)
    steps = FINE * (chunks - 1) + third[1] + 1
    chunk = rows // chunks

    def body(r, s):
        kv = KeyValueSend(r, reach, stretch)
        attn, mlp = LineSum(r.attn), LineSum(r.mlp)

        @pl.when(s == 0)
        def _():
            enter(attn.neighbours() + kv.neighbours())
            kv.start()

        def send_attn(c):
            attn.put(c, dot(attend(r, c, stretch), r.w_o[...]))

        def feed_forward(c):
            middle = r.hidden[...].astype(F32) + attn.total(c, chunk)
            r.hidden_mid[...] = middle
            r.mid_held[attn.at(c, chunk), :] = middle
            hat, _ = norm_parts(middle)
            low = (hat * r.mlp_gain[...].astype(F32)).astype(BF)
            r.mlp_low[...] = low
            gate, up, sigma = mlp_gates(r, low)
            r.gates[...] = jnp.concatenate([gate, up], 1)
            act = (gate * sigma * up).astype(BF)
            r.act[...] = act
            mlp.put(c, dot(act, r.w_down[...]))

        def next_layer(c):
            hidden_next = r.mid_held[mlp.at(c, chunk), :] + mlp.total(c, chunk)
            r.hidden_next[...] = hidden_next
            project(r, hidden_next, kv, c)

        r.arrived(0, "window_in", "w_o")
        at_chunk(s, first, send_attn)
        at_chunk(s, (1, 2, pieces), attn.relay)
        at_chunk(s, (1, 4, pieces), attn.meet)
        r.arrived(second[1], *MLP_WEIGHTS)
        at_chunk(s, second, feed_forward)
        at_chunk(s, (1, 12, pieces), mlp.relay)
        at_chunk(s, (1, 14, pieces), mlp.meet)
        r.arrived(third[1], *QKV_WEIGHTS)
        at_chunk(s, third, next_layer)

        @pl.when(s == steps - 1)
        def _():
            attn.finish()
            mlp.finish()
            kv.finish()

    return step_kernel(
        between_forward, body, steps,
        attend_ins(a, low, first)
        | dict(
            w_o=(w.w_o, Late(layer)),
            hidden=(hidden, second),
            mlp_gain=(w.mlp_gain, Row(layer)),
            w_gate=(w.w_gate, Late(layer)),
            w_up=(w.w_up, Late(layer)),
            w_down=(w.w_down, Late(layer)),
        )
        | project_ins(w, layer + 1, tables, third),
        attend_outs(a, first)
        | dict(
            hidden_mid=((rows, width), F32, second),
            mlp_low=((rows, width), BF, second),
            gates=((rows, 2 * ff), F32, second),
            act=((rows, ff), BF, second),
            hidden_next=((rows, width), F32, third),
        )
        | project_outs(rows, width, w, stretch, reach, third),
        dict(
            attn=LineSum.scratch(rows, width, pieces),
            mlp=LineSum.scratch(rows, width, pieces),
            kv=KeyValueSend.scratch(rows, kv_width, chunks, reach),
            mid_held=pltpu.VMEM((rows, width), F32),
        ),
        collective_id)


def turn_around(a, low, cotangent, w, layer, stretch, chunks, collective_id):
    hidden = a.hidden
    rows, width = hidden.shape
    ff = w.w_gate.shape[2]
    pieces = chunks * FINE
    first, second, third = (FINE, 0, chunks), (FINE, 9, chunks), (FINE, 17, chunks)
    steps = FINE * (chunks - 1) + third[1] + 1
    chunk = rows // chunks

    def body(r, s):
        attn, back = LineSum(r.attn), LineSum(r.back)

        @pl.when(s == 0)
        def _():
            enter(attn.neighbours())
            r.gain_grad[...] = jnp.zeros_like(r.gain_grad)

        def send_attn(c):
            attn.put(c, dot(attend(r, c, stretch), r.w_o[...]))

        def feed_forward(c):
            middle = r.hidden[...] + attn.total(c, chunk)
            r.hidden_mid[...] = middle
            r.mid_held[attn.at(c, chunk), :] = middle
            hat, _ = norm_parts(middle)
            low = (hat * r.mlp_gain[...].astype(F32)).astype(BF)
            r.mlp_low[...] = low
            gate, up, sigma = mlp_gates(r, low)
            d_gates, part = mlp_back(r, r.cotangent[...], gate, up, sigma)
            back.put(c, part)
            r.d_gates[...] = d_gates
            act = (gate * sigma * up).astype(BF)
            r.act[...] = act
            part = dot(act, r.w_down[...]).astype(BF)

            @pl.when(c < chunks // 2)
            def _():
                r.lower_part[...] = part

            @pl.when(c >= chunks // 2)
            def _():
                r.upper_part[...] = part

        def middle_grad(c):
            hat, inverse = norm_parts(r.mid_held[back.at(c, chunk), :])
            d_in = back.total(c, chunk)
            r.gain_grad[0:1, :] += row_sums(d_in * hat)
            g_mid = r.cotangent_late[...].astype(F32) + norm_back(d_in, r.mlp_gain[...].astype(F32), hat, inverse)
            r.g_mid[...] = g_mid
            mid_low = g_mid.astype(BF)
            r.mid_low[...] = mid_low
            r.d_context[...] = dot(mid_low, r.w_o[...], NT).astype(BF)

        r.arrived(0, "window_in", "w_o")
        at_chunk(s, first, send_attn)
        at_chunk(s, (1, 2, pieces), attn.relay)
        at_chunk(s, (1, 4, pieces), attn.meet)
        r.arrived(second[1], *MLP_WEIGHTS)
        at_chunk(s, second, feed_forward)
        at_chunk(s, (1, 12, pieces), back.relay)
        at_chunk(s, (1, 14, pieces), back.meet)
        at_chunk(s, third, middle_grad)

        @pl.when(s == steps - 1)
        def _():
            attn.finish()
            back.finish()

    return step_kernel(
        turn_around, body, steps,
        attend_ins(a, low, first)
        | dict(
            w_o=(w.w_o, Late(layer)),
            hidden=(hidden, second),
            cotangent=(cotangent, second),
            cotangent_late=(cotangent, third),
            mlp_gain=(w.mlp_gain, Row(layer)),
            w_gate=(w.w_gate, Late(layer)),
            w_up=(w.w_up, Late(layer)),
            w_down=(w.w_down, Late(layer)),
        ),
        attend_outs(a, first)
        | dict(
            mlp_low=((rows, width), BF, second),
            act=((rows, ff), BF, second),
            hidden_mid=((rows, width), F32, second),
            lower_part=((rows // 2, width), BF, (FINE, second[1], chunks // 2)),
            upper_part=((rows // 2, width), BF, (FINE, second[1] + FINE * (chunks // 2), chunks // 2)),
            d_gates=((rows, 2 * ff), BF, second),
            g_mid=((rows, width), F32, third),
            mid_low=((rows, width), BF, third),
            d_context=(a.queries.shape, BF, third),
            gain_grad=((8, width), F32, WHOLE),
        ),
        dict(
            attn=LineSum.scratch(rows, width, pieces),
            back=LineSum.scratch(rows, width, pieces),
            mid_held=pltpu.VMEM((rows, width), F32),
        ),
        collective_id)


def attention_backward(a, d_context, low, part, quarter, stretch, pieces, collective_id):
    rows = a.queries.shape[0]
    kv_heads = a.window.shape[1] // (2 * HEAD)
    width = a.queries.shape[1] // kv_heads
    group = width // HEAD
    qb = min(2 * CHUNK, stretch)
    count = stretch // qb
    seqs = rows // stretch
    span = a.window.shape[0] // seqs
    reach = span // stretch - 1
    held = max(reach, 1)
    offset = reach * stretch
    length = min(WINDOW + qb, span)
    steps = seqs * kv_heads * count

    def places(s):
        return s // (kv_heads * count), lax.rem(s // count, kv_heads), lax.rem(s, count)

    def block(shape, index):
        return pl.BlockSpec(shape, lambda s: index(*places(s)))

    def body(r, s):
        seq, g, i = places(s)
        line = LineSum(r.line, r.part)
        q_start = i * qb + offset
        start = jnp.clip(q_start + qb - length, 0, span - length)
        here = pl.ds(pl.multiple_of(start, HEAD), length)

        @pl.when(s == 0)
        def _():
            enter(line.neighbours())
            line.push(0, line.x.shape[0])

        @pl.when(i == 0)
        def _():
            r.d_keys[...] = jnp.zeros_like(r.d_keys)
            r.d_values[...] = jnp.zeros_like(r.d_values)

        for j in range(pieces):

            @pl.when(s == min(2 + j // 2, steps - 1))
            def _():
                line.relay(j)

        for j in range(pieces):

            @pl.when(s == min(4 + j // 2, steps - 1))
            def _():
                line.meet(j)

        def stack(ref):
            return jnp.concatenate([ref[:, h * HEAD : (h + 1) * HEAD] for h in range(group)], 0)

        queries = stack(r.queries)
        d_out = stack(r.d_context)
        lse = jnp.concatenate([r.lse[h : h + 1, :] for h in range(group)], 1)
        product = d_out.astype(F32) * stack(r.context).astype(F32)
        delta = jnp.sum(product.T, 0, keepdims=True)
        keys = r.keys[here, :]
        values = r.values[here, :]
        key_index = start + lax.broadcasted_iota(jnp.int32, (length, qb), 0)
        q_index = q_start + lax.broadcasted_iota(jnp.int32, (1, qb), 1)
        mask = (key_index >= r.low[...]) & (key_index <= q_index)
        mask = jnp.concatenate([mask] * group, 1)
        scores = dot(keys, queries, NT) * (SCALE * LOG2E) - lse
        p = jnp.where(mask, jnp.exp2(scores), 0.0)
        p = p.astype(BF)
        ds = p * (dot(values, d_out, NT) - delta).astype(BF)
        r.d_values[here, :] += dot(p, d_out)
        r.d_keys[here, :] += dot(ds, queries)
        dq = (dot(keys, ds, TN) * SCALE).T
        for h in range(group):
            r.d_q[:, h * HEAD : (h + 1) * HEAD] = dq[h * qb : (h + 1) * qb]

        @pl.when(i == count - 1)
        def _():
            r.d_own[0] = r.d_keys[offset:, :] * SCALE
            r.d_own[1] = r.d_values[offset:, :]
            for j in range(reach):
                r.d_prev[j, 0] = (r.d_keys[j * stretch : (j + 1) * stretch, :] * SCALE).astype(BF)
                r.d_prev[j, 1] = r.d_values[j * stretch : (j + 1) * stretch, :].astype(BF)

        @pl.when(s == steps - 1)
        def _():
            r.total[...] = line.total(0, line.x.shape[0]).astype(BF)
            line.finish()

    by_rows = block((qb, width), lambda seq, g, i: (seq * count + i, g))
    part_rows = part.shape[0] // 2
    return step_kernel(
        attention_backward, body, steps,
        dict(
            low=(low, block((1, qb), lambda seq, g, i: (0, seq * count + i))),
            lse=(a.lse, block((None, group, qb), lambda seq, g, i: (g, 0, seq * count + i))),
            queries=(a.queries, by_rows),
            d_context=(d_context, by_rows),
            context=(a.context, by_rows),
            keys=(a.window, block((span, HEAD), lambda seq, g, i: (seq, g))),
            values=(a.window, block((span, HEAD), lambda seq, g, i: (seq, kv_heads + g))),
            part=(part, pl.BlockSpec(
                (part_rows, part.shape[1]), lambda s: (quarter, 0), pipeline_mode=pl.Buffered(1))),
        ),
        dict(
            d_q=(a.queries.shape, F32, by_rows),
            d_own=((2, rows, kv_heads * HEAD), F32, block((2, stretch, HEAD), lambda seq, g, i: (0, seq, g))),
            d_prev=(
                (held, 2, rows, kv_heads * HEAD), BF,
                block((held, 2, stretch, HEAD), lambda seq, g, i: (0, 0, seq, g))),
            total=((part_rows, part.shape[1]), BF, WHOLE),
        ),
        dict(
            line=LineSum.scratch(part_rows, part.shape[1], pieces, False),
            d_keys=pltpu.VMEM((span, HEAD), F32),
            d_values=pltpu.VMEM((span, HEAD), F32),
        ),
        collective_id)


def attention_grads(r, back, line, c):
    cosine, sine = r.tables[:, :HEAD], r.tables[:, HEAD:]
    both = back.add(r.d_own[...], c)

    def raw_back(grads, raws, gain):
        lows, gains = [], 0.0
        for grad, raw in zip(heads_of(grads), heads_of(raws)):
            grad = rope_back(grad, cosine, sine)
            hat, inverse = norm_parts(raw)
            gains = gains + row_sums(grad * hat)
            lows.append(norm_back(grad, gain, hat, inverse).astype(BF))
        return jnp.concatenate(lows, 1), gains

    q_width = r.d_q.shape[1]
    d_q, q_gain = raw_back(r.d_q[...], r.raw[:, :q_width], r.q_gain[...].astype(F32))
    d_k, k_gain = raw_back(both[0], r.raw[:, q_width:], r.k_gain[...].astype(F32))
    d_v = both[1].astype(BF)
    r.head_gain[0:1, 0:HEAD] += q_gain
    r.head_gain[0:1, HEAD : 2 * HEAD] += k_gain
    r.d_held[line.at(c, d_q.shape[0]), :] = jnp.concatenate([d_q, d_k, d_v], 1)
    part = dot(d_q, r.w_q[...], NT) + dot(d_k, r.w_k[...], NT) + dot(d_v, r.w_v[...], NT)
    line.put(c, part)
    return part


class WeightGrads:
    def __init__(self, r, plan):
        self.r = r
        self.plan = plan
        self.slabs = plan.slabs[2]
        self.late = Scatter(r.sc_q, False), Scatter(r.sc_kv, True)
        self.early = Scatter(r.sc_a, False), Scatter(r.sc_b, True)
        self.blocks = 1 << len(block_axes())

    @staticmethod
    def scratch(rows, width, q_width, k_width, ff):
        per = width // (1 << len(block_axes()))
        return dict(
            sc_a=Scatter.scratch(per, ff + q_width),
            sc_b=Scatter.scratch(per, 2 * ff),
            sc_q=Scatter.scratch(per, q_width),
            sc_kv=Scatter.scratch(per, 2 * k_width),
            d_held=pltpu.VMEM((rows, q_width + 2 * k_width), BF),
        )

    def neighbours(self):
        return self.late[0].neighbours()

    def put(self, scatter, slab, columns, value):
        per = self.blocks // self.slabs
        rows = value.shape[0] // per
        for j in range(per):
            scatter.put(slab * per + j, columns, value[j * rows : (j + 1) * rows])

    def mlp_slab(self, slab):
        r = self.r
        ff = r.act_all.shape[1]
        q_width = r.context_all.shape[1]
        both = dot(r.mlp_low_slab[...], r.d_gates_all[...], TN)
        self.put(self.early[0], slab, slice(0, ff), both[:, :ff])
        self.put(self.early[0], slab, slice(ff, ff + q_width), dot(r.mid_low_slab[...], r.context_all[...], TN))
        self.put(self.early[1], slab, slice(0, ff), both[:, ff:])
        self.put(self.early[1], slab, slice(ff, 2 * ff), dot(r.g_low_slab[...], r.act_all[...], TN))

    def qkv_slab(self, slab):
        r = self.r
        slab_width = r.attn_low_all.shape[1] // self.slabs
        q_width = r.d_q.shape[1]
        columns = pl.ds(pl.multiple_of(slab * slab_width, slab_width), slab_width)
        value = dot(r.attn_low_all[:, columns], r.d_held[...], TN)
        self.put(self.late[0], slab, slice(None), value[:, :q_width])
        self.put(self.late[1], slab, slice(None), value[:, q_width:])

    def each(self, scatters, work):
        for scatter in scatters:
            work(scatter)

    def store(self):
        r = self.r
        last = len(block_axes()) - 1
        ff = r.act_all.shape[1]
        k_width = r.grad_k.shape[1]

        def store_a(total):
            r.grad_gate[...] = total[:, :ff]
            r.grad_o[...] = total[:, ff:]

        def store_b(total):
            r.grad_up[...] = total[:, :ff]
            r.grad_down[...] = total[:, ff:]

        def store_q(total):
            r.grad_q[...] = total

        def store_kv(total):
            r.grad_k[...] = total[:, :k_width]
            r.grad_v[...] = total[:, k_width:]

        self.early[0].fold(last, store_a)
        self.early[1].fold(last, store_b)
        self.late[0].fold(last, store_q)
        self.late[1].fold(last, store_kv)

    def late_slabs(self, s):
        _, lag, count = self.plan.late_slabs
        self.r.arrived(lag, "attn_low_all")
        at_chunk(s, self.plan.late_slabs, self.qkv_slab)

        @pl.when(s == lag + count - 1)
        def _():
            self.each(self.late, lambda scatter: scatter.send(0))

    def run(self, s):
        rate, lag, count = self.plan.slabs
        self.r.arrived(lag, *GRAD_OPERANDS)
        at_chunk(s, self.plan.slabs, self.mlp_slab)

        @pl.when(s == lag + rate * (count - 1))
        def _():
            self.each(self.early, lambda scatter: scatter.send(0))

        for k in range(len(block_axes()) - 1):

            def move(scatter):
                scatter.fold(k)
                scatter.send(k + 1)

            @pl.when(s == self.plan.early(k))
            def _():
                self.each(self.early, move)

            @pl.when(s == self.plan.late(k))
            def _():
                self.each(self.late, move)

    def finish(self):
        self.each(self.early + self.late, lambda scatter: scatter.finish())


def slab_count(chunks):
    return min(4, max(1, chunks // 2))


def grads_ins(a, rows, width, when):
    slab = pl.BlockSpec((rows, width // when[2]), lambda s: (0, chunk_index(when, s)))
    return dict(
        mlp_low_slab=(a.mlp_low, slab),
        mid_low_slab=(a.mid_low, slab),
        g_low_slab=(a.g_low, slab),
        attn_low_all=(a.attn_low, Late()),
        d_gates_all=(a.d_gates, Late()),
        context_all=(a.context, Late()),
        act_all=(a.act, Late()),
    )


def grads_outs(width, q_width, k_width, ff):
    per = width // (1 << len(block_axes()))
    return dict(
        grad_q=((per, q_width), F32, WHOLE),
        grad_k=((per, k_width), F32, WHOLE),
        grad_v=((per, k_width), F32, WHOLE),
        grad_o=((per, q_width), F32, WHOLE),
        grad_gate=((per, ff), F32, WHOLE),
        grad_up=((per, ff), F32, WHOLE),
        grad_down=((per, ff), F32, WHOLE),
    )


def attention_grads_ins(a, w, layer, tables, when):
    rows, k_width = a.raw.shape[0], w.w_k.shape[2]
    own = pl.BlockSpec((2, rows // when[2], k_width), lambda s: (0, chunk_index(when, s), 0))
    return dict(
        d_q=(a.d_q, when),
        d_own=(a.d_own, own),
        d_prev=(a.d_prev, HBM),
        raw=(a.raw, when),
        tables=(tables, when),
        w_q=(w.w_q, Late(layer)),
        w_k=(w.w_k, Late(layer)),
        w_v=(w.w_v, Late(layer)),
        q_gain=(w.q_gain, Row(layer)),
        k_gain=(w.k_gain, Row(layer)),
        attn_gain=(w.attn_gain, Row(layer)),
    )


def between_backward(a, below, g_mid, w, layer, tables, reach, chunks, collective_id):
    rows, width = g_mid.shape
    q_width, k_width, ff = w.w_q.shape[2], w.w_k.shape[2], w.w_gate.shape[2]
    pieces = chunks * PIECES
    first, second, third = (PIECES, 0, chunks), (PIECES, 5, chunks), (PIECES, 11, chunks)
    steps = PIECES * (chunks - 1) + third[1] + 1
    chunk = rows // chunks
    after = PIECES * (chunks - 1) + 1
    slabs = slab_count(chunks)
    plan = types.SimpleNamespace(
        slabs=(2, 2, slabs),
        early=lambda k: min(4 + 2 * slabs + 4 * k, steps - 2),
        late_slabs=(1, after, slabs),
        late=lambda k: min(after + slabs + 2 * k, steps - 2),
    )

    def body(r, s):
        back = KeyValueReturn(r, reach)
        attn, mlp = LineSum(r.attn), LineSum(r.mlp)
        grads = WeightGrads(r, plan)

        @pl.when(s == 0)
        def _():
            enter(attn.neighbours() + back.neighbours() + grads.neighbours())
            back.start()
            r.gain_grad[...] = jnp.zeros_like(r.gain_grad)
            r.head_gain[...] = jnp.zeros_like(r.head_gain)

        def send_attn(c):
            attention_grads(r, back, attn, c)

        def feed_forward(c):
            hat, inverse = norm_parts(r.hidden[...])
            d_in = attn.total(c, chunk)
            r.gain_grad[0:1, :] += row_sums(d_in * hat)
            g = r.g_above[...] + norm_back(d_in, r.attn_gain[...].astype(F32), hat, inverse)
            r.g_held[lax.rem(c, 4)] = g
            g_low = g.astype(BF)
            r.g_low[...] = g_low
            gate, up = r.gates[:, :ff], r.gates[:, ff:]
            d_gates, part = mlp_back(r, g_low, gate, up, jax.nn.sigmoid(gate))
            r.d_gates[...] = d_gates
            mlp.put(c, part)

        def middle_grad(c):
            hat, inverse = norm_parts(r.hidden_mid[...])
            d_in = mlp.total(c, chunk)
            r.gain_grad[1:2, :] += row_sums(d_in * hat)
            g_mid = r.g_held[lax.rem(c, 4)] + norm_back(d_in, r.mlp_gain[...].astype(F32), hat, inverse)
            r.g_mid[...] = g_mid
            mid_low = g_mid.astype(BF)
            r.mid_low[...] = mid_low
            r.d_context[...] = dot(mid_low, r.w_o[...], NT).astype(BF)

        r.arrived(first[1], *QKV_WEIGHTS)
        at_chunk(s, first, send_attn)
        grads.late_slabs(s)
        at_chunk(s, (1, 2, pieces), attn.relay)
        at_chunk(s, (1, 3, pieces), attn.meet)
        r.arrived(second[1], *MLP_WEIGHTS)
        at_chunk(s, second, feed_forward)
        at_chunk(s, (1, 7, pieces), mlp.relay)
        at_chunk(s, (1, 8, pieces), mlp.meet)
        r.arrived(third[1], "w_o")
        at_chunk(s, third, middle_grad)
        grads.run(s)

        @pl.when(s == steps - 1)
        def _():
            grads.store()
            attn.finish()
            mlp.finish()
            back.finish()
            grads.finish()

    return step_kernel(
        between_backward, body, steps,
        attention_grads_ins(a, w, layer, tables, first)
        | grads_ins(a, rows, width, plan.slabs)
        | dict(
            hidden=(a.hidden, second),
            g_above=(g_mid, second),
            gates=(below.gates, second),
            hidden_mid=(below.hidden_mid, third),
            mlp_gain=(w.mlp_gain, Row(layer - 1)),
            w_gate=(w.w_gate, Late(layer - 1)),
            w_up=(w.w_up, Late(layer - 1)),
            w_down=(w.w_down, Late(layer - 1)),
            w_o=(w.w_o, Late(layer - 1)),
        ),
        dict(
            g_low=((rows, width), BF, second),
            d_gates=((rows, 2 * ff), BF, second),
            g_mid=((rows, width), F32, third),
            mid_low=((rows, width), BF, third),
            d_context=((rows, q_width), BF, third),
            gain_grad=((8, width), F32, WHOLE),
            head_gain=((8, 2 * HEAD), F32, WHOLE),
        )
        | grads_outs(width, q_width, k_width, ff),
        dict(
            attn=LineSum.scratch(rows, width, pieces),
            mlp=LineSum.scratch(rows, width, pieces),
            kr=KeyValueReturn.scratch(rows, k_width, chunks, reach),
            **WeightGrads.scratch(rows, width, q_width, k_width, ff),
            g_held=pltpu.VMEM((4, rows // chunks, width), F32),
        ),
        collective_id)


def last_backward(a, top, quarters, above, w, tables, reach, chunks, collective_id):
    g_mid = above.g_mid
    rows, width = g_mid.shape
    q_width, k_width, ff = w.w_q.shape[2], w.w_k.shape[2], w.w_gate.shape[2]
    layer = 0
    pieces = chunks * PIECES
    pairs = max(1, chunks // 2)
    half = rows // 2
    half_pieces = pieces // 2
    out_chunk = min(rows // chunks, half // 2)
    out_count = rows // out_chunk
    first, second = (4, 0, pairs), (PIECES, 13, chunks)
    third = (PIECES * chunks // out_count, 13, out_count)
    steps = max(PIECES * (chunks - 1) + second[1], third[0] * (out_count - 1) + third[1]) + 1
    chunk = rows // chunks
    after = 4 * (pairs - 1)
    slabs = slab_count(chunks)
    plan = types.SimpleNamespace(
        slabs=(2, 0, slabs),
        early=lambda k: min(2 * slabs + 1 + 7 * k, steps - 2),
        late_slabs=(1, after + 3, slabs),
        late=lambda k: min(after + 5 + slabs + 5 * k, steps - 2),
    )

    def body(r, s):
        back = KeyValueReturn(r, reach)
        attn, upper = LineSum(r.attn), LineSum(r.upper, r.upper_part)
        grads = WeightGrads(r, plan)
        sums = Butterfly(r.sums)

        @pl.when(s == 0)
        def _():
            enter(attn.neighbours() + back.neighbours() + sums.neighbours())
            back.start()
            upper.push(0, half)
            r.head_gain[...] = jnp.zeros_like(r.head_gain)
            r.gain_held[...] = jnp.zeros_like(r.gain_held)

        def send_attn(c):
            part = attention_grads(r, back, attn, c)
            hat, _ = norm_parts(r.hidden[...].astype(F32))
            r.gain_held[...] += row_sums(part * hat)

        def give_output(c):
            per = out_count // 4
            for q in range(2):

                @pl.when((c >= q * per) & (c < (q + 1) * per))
                def _():
                    here = pl.ds(pl.multiple_of(jnp.clip(c - q * per, 0, per - 1) * out_chunk, out_chunk), out_chunk)
                    total = (r.quarter_0, r.quarter_1)[q][here, :].astype(F32)
                    r.output[...] = (r.hidden_mid[...] + total).astype(BF)

            @pl.when(c >= 2 * per)
            def _():
                r.output[...] = (r.hidden_mid[...] + upper.total(c - 2 * per, out_chunk)).astype(BF)

        def give_input(c):
            hat, inverse = norm_parts(r.hidden_late[...].astype(F32))
            r.input_grad[...] = r.g_above[...] + norm_back(attn.total(c, chunk), r.attn_gain[...].astype(F32), hat, inverse)

        r.arrived(first[1], *QKV_WEIGHTS)
        at_chunk(s, first, send_attn)
        grads.late_slabs(s)
        at_chunk(s, (1, 0, half_pieces), upper.relay)
        at_chunk(s, (1, 8, pieces), attn.relay)
        at_chunk(s, (1, 2, half_pieces), upper.meet)
        at_chunk(s, (1, 10, pieces), attn.meet)
        at_chunk(s, third, give_output)
        at_chunk(s, second, give_input)
        grads.run(s)

        @pl.when(s == after + 1)
        def _():
            row = lax.broadcasted_iota(jnp.int32, (8, width), 0)
            once = jnp.where(lax.axis_index("tensor") == 0, 1.0, 0.0)
            heads = [r.head_gain[0:1, :], r.above_head_gain[0:1, :], jnp.zeros((1, width - 4 * HEAD), F32)]
            packet = jnp.zeros((8, width), F32)
            for place, part in enumerate([
                r.gain_held[...], r.above_gain[0:1, :] * once, r.above_gain[1:2, :] * once, r.top_gain[0:1, :] * once,
                jnp.concatenate(heads, 1),
            ]):
                packet = jnp.where(row == place, part, packet)
            sums.put(packet)

        for k in range(len(sums.axes)):

            @pl.when(s == max(steps - len(sums.axes) - 4 + k, after + 2))
            def _():
                sums.fold(k)

        @pl.when(s == steps - 1)
        def _():
            grads.store()
            r.gains[...] = sums.total()
            attn.finish()
            upper.finish()
            back.finish()
            grads.finish()
            sums.finish()

    return step_kernel(
        last_backward, body, steps,
        attention_grads_ins(a, w, layer, tables, first)
        | grads_ins(a, rows, width, plan.slabs)
        | dict(
            hidden=(a.hidden, first),
            hidden_late=(a.hidden, second),
            g_above=(g_mid, second),
            above_gain=(above.gain_grad, WHOLE),
            above_head_gain=(above.head_gain, WHOLE),
            top_gain=(top.gain_grad, WHOLE),
            upper_part=(top.upper_part, WHOLE),
            quarter_0=(quarters[0], WHOLE),
            quarter_1=(quarters[1], WHOLE),
            hidden_mid=(top.hidden_mid, third),
        ),
        dict(
            input_grad=((rows, width), F32, second),
            output=((rows, width), BF, third),
            gains=((8, width), F32, WHOLE),
        )
        | grads_outs(width, q_width, k_width, ff),
        dict(
            attn=LineSum.scratch(rows, width, pieces),
            upper=LineSum.scratch(half, width, half_pieces, False),
            kr=KeyValueReturn.scratch(rows, k_width, pairs, reach),
            **WeightGrads.scratch(rows, width, q_width, k_width, ff),
            sums=Butterfly.scratch((8, width)),
            head_gain=pltpu.VMEM((8, 2 * HEAD), F32),
            gain_held=pltpu.VMEM((1, width), F32),
        ),
        collective_id)


def collect_kernel(count, output_in, input_in, gains, *refs):
    ins, (output, input_grad, attn, mlp, q_gain, k_gain), outs = refs[: 2 * count], refs[2 * count : 2 * count + 6], refs[2 * count + 6 :]
    output[...] = output_in[...]
    input_grad[...] = input_in[...]
    s = pl.program_id(0)

    @pl.when(s == 0)
    def _():
        attn[...] = gains[0:2, :]
        mlp[...] = gains[2:4, :]
        for layer in range(2):
            at = 2 * layer * HEAD
            q_gain[layer : layer + 1, :] = gains[4:5, at : at + HEAD]
            k_gain[layer : layer + 1, :] = gains[4:5, at + HEAD : at + 2 * HEAD]

    for g in range(count):
        for layer in range(2):
            value = ins[2 * g + layer]
            if outs[g].shape[1] == value.shape[0]:
                outs[g][layer] = value[...]
            else:

                @pl.when(s == 0)
                def _():
                    outs[g][layer] = value[...].T


def collect(end, above):
    rows, width = end.output.shape
    straight = [(k.grad_q, k.grad_k, k.grad_v, k.grad_gate, k.grad_up) for k in (end, above)]
    turned = [(k.grad_o, k.grad_down) for k in (end, above)]
    per = straight[0][0].shape[0]
    steps = max(1, min(2, per // 8))
    whole = pl.BlockSpec(memory_space=pltpu.VMEM)

    def blocks(array):
        return pl.BlockSpec((array.shape[0] // steps, array.shape[1]), lambda s: (s, 0))

    ins = [end.output, end.input_grad, end.gains]
    in_specs = [blocks(end.output), blocks(end.input_grad), whole]
    outs = [
        ((rows, width), BF, blocks(end.output)), ((rows, width), F32, blocks(end.input_grad)),
        ((2, width), F32, whole), ((2, width), F32, whole), ((2, HEAD), F32, whole), ((2, HEAD), F32, whole),
    ]
    for pair in zip(*straight):
        ins += pair
        in_specs += [blocks(a) for a in pair]
        shape = pair[0].shape
        outs.append(((2,) + shape, F32, pl.BlockSpec((2, per // steps, shape[1]), lambda s: (0, s, 0))))
    for pair in zip(*turned):
        ins += pair
        in_specs += [whole, whole]
        outs.append(((2,) + pair[0].shape[::-1], F32, whole))
    return pl.pallas_call(
        functools.partial(collect_kernel, 7),
        grid=(steps,),
        in_specs=in_specs,
        out_specs=[o[2] for o in outs],
        out_shape=[jax.ShapeDtypeStruct(o[0], o[1]) for o in outs],
        name=collect.__name__,
        compiler_params=pltpu.CompilerParams(vmem_limit_bytes=62 << 20),
    )(*ins)


def per_device(
    tokens, cotangent, segments, positions, attn_gain, w_query, key_projection, value_projection, query_gain, key_gain,
    w_output, mlp_gain, w_gate, w_up, w_down,
):
    seqs_here, stretch, width = tokens.shape
    rows = seqs_here * stretch
    reach = min(lax.axis_size("seq") - 1, (WINDOW + stretch - 2) // stretch)
    chunks = rows // min(CHUNK, stretch)

    w = types.SimpleNamespace(
        attn_gain=attn_gain, mlp_gain=mlp_gain, q_gain=query_gain, k_gain=key_gain,
        w_q=w_query, w_k=key_projection, w_v=value_projection, w_o=w_output, w_gate=w_gate, w_up=w_up, w_down=w_down,
    )
    tokens = tokens.reshape(rows, width)
    cotangent = cotangent.reshape(rows, width)

    a0 = first_projection(tokens, segments, positions, w, stretch, reach, rows // min(2 * CHUNK, stretch), 1)
    tables, low = a0.tables, a0.low
    a0.hidden = tokens
    mid = between_forward(a0, low, w, 0, tables, stretch, reach, chunks, 2)
    a0.context, a0.lse = mid.context, mid.lse
    a1 = types.SimpleNamespace(
        attn_low=mid.attn_low, raw=mid.raw, queries=mid.queries, window=mid.window,
        hidden=mid.hidden_next)
    turn = turn_around(a1, low, cotangent, w, 1, stretch, chunks, 3)
    a1.context, a1.lse = turn.context, turn.lse
    a1.mlp_low, a1.act, a1.d_gates = turn.mlp_low, turn.act, turn.d_gates
    a1.mid_low, a1.g_low = turn.mid_low, cotangent
    pieces = chunks * FINE // 4
    back = attention_backward(a1, turn.d_context, low, turn.lower_part, 0, stretch, pieces, 6)
    a1.d_q, a1.d_own, a1.d_prev = back.d_q, back.d_own, back.d_prev
    quarters = [back.total]
    down = between_backward(a1, mid, turn.g_mid, w, 1, tables, reach, chunks, 4)
    a0.mlp_low, a0.act, a0.d_gates = mid.mlp_low, mid.act, down.d_gates
    a0.mid_low, a0.g_low = down.mid_low, down.g_low
    back = attention_backward(a0, down.d_context, low, turn.lower_part, 1, stretch, pieces, 7)
    a0.d_q, a0.d_own, a0.d_prev = back.d_q, back.d_own, back.d_prev
    quarters.append(back.total)
    end = last_backward(a0, turn, quarters, down, w, tables, reach, chunks, 5)
    output, input_grad, attn, mlp, q_gain, k_gain, d_q, d_k, d_v, d_gate, d_up, d_o, d_down = collect(end, down)
    shape = (seqs_here, stretch, width)
    return (
        output.reshape(shape), input_grad.reshape(shape), attn, d_q, d_k, d_v, q_gain, k_gain, d_o, mlp, d_gate, d_up,
        d_down,
    )


def solution(mesh):
    placed = (
        P("dp", "seq", None), P("dp", "seq", None), P("dp", "seq"), P("dp", "seq"), P(), P(None, None, "tensor"),
        P(None, None, "tensor"), P(None, None, "tensor"), P(), P(), P(None, "tensor", None), P(),
        P(None, None, "tensor"), P(None, None, "tensor"), P(None, "tensor", None),
    )
    by_rows = P(None, ("dp", "seq"), "tensor")
    by_columns = P(None, "tensor", ("dp", "seq"))
    return jax.shard_map(
        per_device,
        mesh=mesh,
        in_specs=placed,
        out_specs=(
            P("dp", "seq", None), P("dp", "seq", None), P(), by_rows, by_rows, by_rows, P(), P(), by_columns, P(),
            by_rows, by_rows, by_columns,
        ),
        check_vma=False,
    )
```
